32 devices in a mesh: rep: 4 (over y, x), shard: 8 (over z, core).
Axes of the slice: x: 2, y: 2, z: 4, core: 2. Of those that a mesh axis runs over, the one named last changes fastest.
Arguments:
- tokens: bfloat16 [32, 256, 1024], P(('rep', 'shard')), may hold values from -6 to 6
- states: bfloat16 [32, 384, 1024], P(('rep', 'shard')), may hold values from -6 to 6
- cotangent: bfloat16 [32, 256, 1024], P(('rep', 'shard')), may hold values from -6 to 6
- dec_len: int32 [32], P(('rep', 'shard')), may hold values from 64 to 256, as said below
- enc_len: int32 [32], P(('rep', 'shard')), may hold values from 96 to 384, as said below
- self_weights: float32 [4, 1024, 1024], P(None, 'shard'), may hold values from -0.5625 to 0.5625
- cross_weights: float32 [4, 1024, 1024], P(None, 'shard'), may hold values from -0.5625 to 0.5625
- fc_in: float32 [1024, 4096], P('shard'), may hold values from -0.1875 to 0.1875
- fc_out: float32 [4096, 1024], P('shard'), may hold values from -0.09375 to 0.09375
- norm_params: float32 [2, 3, 1024], replicated, may hold values from -1.5 to 1.5, as said below
- self_moment: float32 [4, 1024, 1024], P(None, 'shard'), may hold values from -217.2232 to 217.2232
- cross_moment: float32 [4, 1024, 1024], P(None, 'shard'), may hold values from -217.2232 to 217.2232
- fc_in_moment: float32 [1024, 4096], P('shard'), may hold values from -162.9174 to 162.9174
- fc_out_moment: float32 [4096, 1024], P('shard'), may hold values from -325.8348 to 325.8348
- norm_moment: float32 [2, 3, 1024], P(None, None, 'shard'), may hold values from -543.058 to 543.058
Outputs:
- block_out: bfloat16 [32, 256, 1024], P(('rep', 'shard'))
- tokens_grad: bfloat16 [32, 256, 1024], P(('rep', 'shard'))
- states_grad: bfloat16 [32, 384, 1024], P(('rep', 'shard'))
- self_grad: float32 [4, 1024, 1024], P(None, 'shard')
- cross_grad: float32 [4, 1024, 1024], P(None, 'shard')
- fc_in_grad: float32 [1024, 4096], P('shard')
- fc_out_grad: float32 [4096, 1024], P('shard')
- norm_grad: float32 [2, 3, 1024], P(None, None, 'shard')
- self_moment_new: float32 [4, 1024, 1024], P(None, 'shard')
- cross_moment_new: float32 [4, 1024, 1024], P(None, 'shard')
- fc_in_moment_new: float32 [1024, 4096], P('shard')
- fc_out_moment_new: float32 [4096, 1024], P('shard')
- norm_moment_new: float32 [2, 3, 1024], P(None, None, 'shard')
- self_new: float32 [4, 1024, 1024], P(None, 'shard')
- cross_new: float32 [4, 1024, 1024], P(None, 'shard')
- fc_in_new: float32 [1024, 4096], P('shard')
- fc_out_new: float32 [4096, 1024], P('shard')
- norm_new: float32 [2, 3, 1024], P(None, None, 'shard')
- self_low: bfloat16 [4, 1024, 1024], P(None, 'shard')
- cross_low: bfloat16 [4, 1024, 1024], P(None, 'shard')
- fc_in_low: bfloat16 [1024, 4096], P('shard')
- fc_out_low: bfloat16 [4096, 1024], P('shard')
The draws below stay inside these ranges and needn't reach their ends.
Inputs may be any that keep to these rules, and one draw needn't show every extreme that they name: `dec_len`: at least a quarter of the slots are used; some sequence of every draw uses all 256. `enc_len`: at least a quarter of the slots are used; some sequence of every draw uses all 384. `norm_params`: gains between 0.7 and 1.4.
All inputs are finite; a program needn't handle non-finite values.
Results may differ from the reference program's by a relative error of at most 0.024.
Values may be sent and summed in bfloat16 or wider, within the bound.
No kernel may reach another device: no remote copies, remote signals or barrier semaphores. Data moves between devices by JAX's collectives and lax.ppermute only.
A program may use at most 256 MiB of HBM per device.

```python
import math
import jax
import jax.numpy as jnp
from jax import lax

D = 1024
HEADS = 16
HEAD_DIM = 64
FF = 4096
SLOTS = 256
ENC_SLOTS = 384
NS_STEPS = 3
SEQS = 32


def draw_lengths(key, longest):
    value_key, chosen_key = jax.random.split(key)
    seq_count = SEQS
    values = jax.random.randint(value_key, (seq_count,), longest // 4, longest + 1)
    chosen = jax.random.randint(chosen_key, (), 0, seq_count)
    return jnp.where(jnp.arange(seq_count) == chosen, longest, values).astype(jnp.int32)


def draw_dec_len(key, part):
    key = jax.random.fold_in(key, 11)
    return draw_lengths(key, SLOTS)


def draw_enc_len(key, part):
    key = jax.random.fold_in(key, 12)
    return draw_lengths(key, ENC_SLOTS)


def attention_stack(key):
    normal_part = jnp.clip(jax.random.normal(key, (4, D, D), jnp.float32), -6.0, 6.0)
    factor = jnp.array([1.0, 1.0, 1.0, 3.0], jnp.float32)
    return normal_part * D ** (-0.5) * factor[:, None, None]


def draw_self_weights(key, part):
    key = jax.random.fold_in(key, 21)
    return attention_stack(key)


def draw_cross_weights(key, part):
    key = jax.random.fold_in(key, 22)
    return attention_stack(key)


def draw_norm_params(key, part):
    key = jax.random.fold_in(key, 31)
    gain_key, bias_key = jax.random.split(key)
    gain_rows = jnp.exp(jax.random.uniform(gain_key, (3, D), jnp.float32, jnp.log(0.7), jnp.log(1.4)))
    bias_rows = jnp.clip(0.3 * jax.random.normal(bias_key, (3, D), jnp.float32), -1.5, 1.5)
    return jnp.stack([gain_rows, bias_rows])


def steps_of(stream_key, shape, cuts, low, largest):
    def one(position, blocks):
        steps = jax.random.uniform(jax.random.fold_in(jax.random.fold_in(stream_key, 6), position), (blocks,), jnp.float32, low / len(cuts), largest / len(cuts))
        return jnp.repeat(jnp.exp(steps), shape[position] // blocks).reshape((-1,) + (1,) * (len(shape) - position - 1))

    factor_of = one(*cuts[0])
    for cut in cuts[1:]:
        factor_of = factor_of * one(*cut)
    return factor_of


def gaussian(own_key, shape, scale, most, cuts=(), held_as=jnp.bfloat16):
    loudness = steps_of(own_key, shape, cuts, -0.22, 0.18) if cuts else 1.0
    drawn = jax.random.normal(own_key, shape, jnp.float32) * scale * loudness
    return jnp.minimum(jnp.maximum(drawn, -most), most).astype(held_as)


def setup_inputs(seed: int = 0) -> dict:
    splits = jax.random.split(jax.random.key(seed), 16)
    tokens = gaussian(splits[0], (SEQS, SLOTS, D), 1.0, 6.0, ((0, 32),))
    states = gaussian(splits[1], (SEQS, ENC_SLOTS, D), 1.0, 6.0, ((0, 32),))
    cotangent = gaussian(splits[2], (SEQS, SLOTS, D), 1.0, 6.0, ((0, 32),))
    dec_len = draw_dec_len(jax.random.fold_in(splits[15], 71), 0)
    enc_len = draw_enc_len(jax.random.fold_in(splits[15], 71), 0)
    self_weights = draw_self_weights(jax.random.fold_in(splits[15], 71), 0)
    cross_weights = draw_cross_weights(jax.random.fold_in(splits[15], 71), 0)
    fc_in = gaussian(splits[7], (D, FF), D ** -0.5, 0.1875, ((0, 8),), jnp.float32)
    fc_out = gaussian(splits[8], (FF, D), FF ** -0.5, 0.09375, ((0, 8),), jnp.float32)
    norm_params = draw_norm_params(jax.random.fold_in(splits[15], 71), 0)
    self_moment = gaussian(splits[10], (4, D, D), (0.4 * (SEQS * SLOTS) ** 0.5), 217.2232, ((1, 8),), jnp.float32)
    cross_moment = gaussian(splits[11], (4, D, D), (0.4 * (SEQS * SLOTS) ** 0.5), 217.2232, ((1, 8),), jnp.float32)
    fc_in_moment = gaussian(splits[12], (D, FF), (0.3 * (SEQS * SLOTS) ** 0.5), 162.9174, ((0, 8),), jnp.float32)
    fc_out_moment = gaussian(splits[13], (FF, D), (0.6 * (SEQS * SLOTS) ** 0.5), 325.8348, ((0, 8),), jnp.float32)
    norm_moment = gaussian(splits[14], (2, 3, D), ((SEQS * SLOTS) ** 0.5), 543.058, ((2, 8),), jnp.float32)
    return dict(tokens=tokens, states=states, cotangent=cotangent, dec_len=dec_len, enc_len=enc_len, self_weights=self_weights, cross_weights=cross_weights, fc_in=fc_in, fc_out=fc_out, norm_params=norm_params, self_moment=self_moment, cross_moment=cross_moment, fc_in_moment=fc_in_moment, fc_out_moment=fc_out_moment, norm_moment=norm_moment)


@jax.custom_vjp
def bfloat_copy(v):
    return lax.optimization_barrier(v.astype(jnp.bfloat16)).astype(jnp.float32)

@jax.custom_vjp
def low_back(v):
    return v

def low_keep(v):
    return (bfloat_copy(v), None)

def low_pass(kept, grad):
    return (grad,)

def back_keep(v):
    return (v, None)

def back_low(kept, grad):
    return (bfloat_copy(grad),)
bfloat_copy.defvjp(low_keep, low_pass)
low_back.defvjp(back_keep, back_low)
NORM_EPSILON = 1e-05
MOMENTUM_DECAY = 0.9
MATRIX_RATE = 0.6
VECTOR_RATE = 0.05
SCHULZ_FIRST = 3.4445
SCHULZ_SECOND = -4.775
SCHULZ_THIRD = 2.0315

def rounded_both(values):
    return bfloat_copy(low_back(values))

def product(left, right):
    return jnp.dot(left, right, precision=lax.Precision.HIGHEST)

def normalize(values, gain, bias):
    centered = values - lax.optimization_barrier(jnp.mean(values, axis=-1, keepdims=True))
    variance = lax.optimization_barrier(jnp.mean(centered * centered, axis=-1, keepdims=True))
    return centered * lax.rsqrt(variance + NORM_EPSILON) * gain + bias

def attend(query_rows, incoming_keys, incoming_values, valid):
    row_count = query_rows.shape[0]
    key_count = incoming_keys.shape[0]
    queries_by_head = query_rows.reshape(row_count, HEADS, HEAD_DIM)
    keys_by_head = incoming_keys.reshape(key_count, HEADS, HEAD_DIM)
    values_by_head = incoming_values.reshape(key_count, HEADS, HEAD_DIM)
    logit_scores = jnp.einsum('pwj,rwj->wpr', queries_by_head, keys_by_head, precision=lax.Precision.HIGHEST)
    logit_scores = low_back(logit_scores * HEAD_DIM ** (-0.5))
    logit_scores = jnp.where(valid[None], logit_scores, -jnp.inf)
    row_max = lax.optimization_barrier(jnp.max(logit_scores, axis=-1, keepdims=True))
    exponent = jnp.exp(logit_scores - row_max)
    attention_weights = exponent / lax.optimization_barrier(jnp.sum(exponent, axis=-1, keepdims=True))
    attended_values = jnp.einsum('onw,wov->nov', bfloat_copy(attention_weights), values_by_head, precision=lax.Precision.HIGHEST)
    return rounded_both(attended_values.reshape(row_count, HEADS * HEAD_DIM))

def sequence(weights, source, encoded, dec_length, enc_length):
    self_w, cross_w, first_fc, second_fc, norms = weights
    place = jnp.arange(SLOTS)
    enc_place = jnp.arange(ENC_SLOTS)
    self_valid = (place[None, :] <= place[:, None]) & (place[None, :] < dec_length)
    cross_valid = jnp.broadcast_to(enc_place[None, :] < enc_length, (SLOTS, ENC_SLOTS))
    first = bfloat_copy(normalize(source, norms[0, 0], norms[1, 0]))
    query_rows = rounded_both(product(first, self_w[0]))
    incoming_keys = rounded_both(product(first, self_w[1]))
    incoming_values = rounded_both(product(first, self_w[2]))
    attended_values = attend(query_rows, incoming_keys, incoming_values, self_valid)
    after_self = source + low_back(product(attended_values, self_w[3]))
    second = bfloat_copy(normalize(after_self, norms[0, 1], norms[1, 1]))
    cross_query = rounded_both(product(second, cross_w[0]))
    cross_keys = rounded_both(product(encoded, cross_w[1]))
    cross_values = rounded_both(product(encoded, cross_w[2]))
    cross_mixed = attend(cross_query, cross_keys, cross_values, cross_valid)
    after_cross = after_self + low_back(product(cross_mixed, cross_w[3]))
    third = bfloat_copy(normalize(after_cross, norms[0, 2], norms[1, 2]))
    hidden = bfloat_copy(jax.nn.gelu(low_back(product(third, first_fc))))
    return after_cross + low_back(product(hidden, second_fc))

def orthogonalize(matrix):
    is_tall = matrix.shape[0] > matrix.shape[1]
    current = matrix.T if is_tall else matrix
    current = bfloat_copy(current / (jnp.sqrt(jnp.sum(current * current)) + 1e-07))
    for sweep_index in range(NS_STEPS):
        gram_matrix = bfloat_copy(product(current, current.T))
        polynomial = bfloat_copy(SCHULZ_SECOND * gram_matrix + SCHULZ_THIRD * product(gram_matrix, gram_matrix))
        current = bfloat_copy(SCHULZ_FIRST * current + product(polynomial, current))
    return current.T if is_tall else current

def stretch(shape):
    return math.sqrt(max(shape[0], shape[1]) / min(shape[0], shape[1]))

def muon_step(weight, moment, grad):
    fresh = MOMENTUM_DECAY * moment + grad
    return (fresh, weight - MATRIX_RATE * stretch(weight.shape) * orthogonalize(bfloat_copy(fresh)))

def muon_stack(weight, moment, grad):
    fresh = MOMENTUM_DECAY * moment + grad
    updated_list = []
    for matrix_index in range(weight.shape[0]):
        single = weight[matrix_index]
        updated_list.append(single - MATRIX_RATE * stretch(single.shape) * orthogonalize(bfloat_copy(fresh[matrix_index])))
    return (fresh, jnp.stack(updated_list))

def reference(tokens, states, cotangent, dec_len, enc_len, self_weights, cross_weights, fc_in, fc_out, norm_params, self_moment, cross_moment, fc_in_moment, fc_out_moment, norm_moment):

    def forward(self_w, cross_w, first_fc, second_fc, norms, sources, encodings):
        weights = (bfloat_copy(self_w), bfloat_copy(cross_w), bfloat_copy(first_fc), bfloat_copy(second_fc), norms)

        def single(sequence_item):
            return sequence(weights, sequence_item[0], sequence_item[1], sequence_item[2], sequence_item[3])
        return lax.map(jax.checkpoint(single), (sources, encodings, dec_len, enc_len))
    outputs, pullback = jax.vjp(forward, self_weights, cross_weights, fc_in, fc_out, norm_params, tokens.astype(jnp.float32), states.astype(jnp.float32))
    self_grad, cross_grad, fc_in_grad, fc_out_grad, norm_grad, tokens_grad, states_grad = pullback(cotangent.astype(jnp.float32))
    self_fresh, self_new = muon_stack(self_weights, self_moment, self_grad)
    cross_fresh, cross_new = muon_stack(cross_weights, cross_moment, cross_grad)
    in_fresh, in_new = muon_step(fc_in, fc_in_moment, fc_in_grad)
    out_fresh, out_new = muon_step(fc_out, fc_out_moment, fc_out_grad)
    norm_fresh = MOMENTUM_DECAY * norm_moment + norm_grad
    norm_new = norm_params - VECTOR_RATE * norm_fresh / math.sqrt(SEQS * SLOTS)
    return (outputs.astype(jnp.bfloat16), tokens_grad.astype(jnp.bfloat16), states_grad.astype(jnp.bfloat16), self_grad, cross_grad, fc_in_grad, fc_out_grad, norm_grad, self_fresh, cross_fresh, in_fresh, out_fresh, norm_fresh, self_new, cross_new, in_new, out_new, norm_new, self_new.astype(jnp.bfloat16), cross_new.astype(jnp.bfloat16), in_new.astype(jnp.bfloat16), out_new.astype(jnp.bfloat16))
```

```python
import math

import jax
import jax.numpy as jnp
from jax import lax
from jax.experimental import pallas as pl
from jax.experimental.pallas import tpu as pltpu
from jax.sharding import PartitionSpec as P

HEADS = 16
HEAD_DIM = 64
NS_STEPS = 3


NORM_EPSILON = 1e-05
MOMENTUM_DECAY = 0.9
MATRIX_RATE = 0.6
VECTOR_RATE = 0.05
SCHULZ_FIRST = 3.4445
SCHULZ_SECOND = -4.775
SCHULZ_THIRD = 2.0315


def matmul(left, right):
    return jnp.dot(left, right, preferred_element_type=jnp.float32)


def matmul_left_t(left, right):
    return lax.dot_general(
        left, right, (((0,), (0,)), ((), ())), preferred_element_type=jnp.float32
    )


def matmul_right_t(left, right):
    return lax.dot_general(
        left, right, (((1,), (1,)), ((), ())), preferred_element_type=jnp.float32
    )


def normalize_parts(values, gain, bias):
    centered = values - jnp.mean(values, axis=-1, keepdims=True)
    inverse = lax.rsqrt(jnp.mean(centered * centered, axis=-1, keepdims=True) + NORM_EPSILON)
    unit_part = centered * inverse
    return (unit_part * gain + bias, unit_part, inverse)


def normalize_back(grad_out, unit_part, inverse, gain):
    grad_unit = grad_out * gain
    grad_in = inverse * (
        grad_unit
        - jnp.mean(grad_unit, axis=-1, keepdims=True)
        - unit_part * jnp.mean(grad_unit * unit_part, axis=-1, keepdims=True)
    )
    return (grad_in, jnp.sum(grad_out * unit_part, axis=0), jnp.sum(grad_out, axis=0))


PAIR = 2 * HEAD_DIM
SMALL = pl.CostEstimate(flops=1024, bytes_accessed=1024, transcendentals=0)


def attention_parts(count_ref, causal, query_part, keys, is_first):
    lane = lax.broadcasted_iota(jnp.int32, (1, PAIR), 1)
    own = (lane < HEAD_DIM) == is_first
    scores = matmul_right_t(jnp.where(own, query_part, 0), keys) * HEAD_DIM ** (-0.5)
    key_place = lax.broadcasted_iota(jnp.int32, scores.shape, 1)
    valid = key_place < count_ref[0]
    if causal:
        valid = valid & (key_place <= lax.broadcasted_iota(jnp.int32, scores.shape, 0))
    scores = jnp.where(valid, scores, -jnp.inf)
    exponent = jnp.exp(scores - jnp.max(scores, axis=-1, keepdims=True))
    return exponent / jnp.sum(exponent, axis=-1, keepdims=True), own


def head_pairs(width, body):
    def step(index, carry):
        body(pl.ds(pl.multiple_of(index * PAIR, PAIR), PAIR))
        return carry

    lax.fori_loop(0, width // PAIR, step, 0)


def attention_call(kernel, out_shapes, count, arrays, waited):
    rows, width = arrays[0].shape
    keys = arrays[1].shape[0]
    vmem = pl.BlockSpec(memory_space=pltpu.VMEM)
    return pl.pallas_call(
        kernel,
        out_shape=tuple(out_shapes),
        in_specs=[pl.BlockSpec(memory_space=pltpu.SMEM)]
        + [vmem] * len(arrays)
        + [pl.BlockSpec(memory_space=pl.ANY)] * len(waited),
        out_specs=tuple([vmem] * len(out_shapes)),
        compiler_params=pltpu.CompilerParams(vmem_limit_bytes=56 * 2**20),
        cost_estimate=SMALL,
    )(count, *arrays, *waited)


def attend_forward(query_rows, incoming_keys, incoming_values, count, causal, *waited):
    def kernel(count_ref, query_ref, key_ref, value_ref, *refs):
        mixed_ref = refs[-1]

        def one_pair(columns):
            query_part, keys = query_ref[:, columns], key_ref[:, columns]
            values = value_ref[:, columns]
            mixed = None
            for is_first in (True, False):
                weights, own = attention_parts(count_ref, causal, query_part, keys, is_first)
                here = matmul(weights.astype(jnp.bfloat16), values)
                mixed = here if mixed is None else jnp.where(own, here, mixed)
            mixed_ref[:, columns] = mixed.astype(jnp.bfloat16)

        head_pairs(query_ref.shape[1], one_pair)

    return attention_call(
        kernel,
        [low(*query_rows.shape)],
        count,
        [query_rows, incoming_keys, incoming_values],
        waited,
    )[0]


def attend_backward(
    query_rows, incoming_keys, incoming_values, count, causal, grad_mixed, *waited
):
    def kernel(count_ref, query_ref, key_ref, value_ref, grad_ref, *refs):
        grad_query, grad_keys, grad_values = refs[-3:]
        scale = HEAD_DIM ** (-0.5)

        def one_pair(columns):
            query_part, keys = query_ref[:, columns], key_ref[:, columns]
            values, grads = value_ref[:, columns], grad_ref[:, columns]
            found = None
            for is_first in (True, False):
                weights, own = attention_parts(count_ref, causal, query_part, keys, is_first)
                grad_prob = matmul_right_t(jnp.where(own, grads, 0), values)
                shift = jnp.sum(grad_prob * weights, axis=-1, keepdims=True)
                score_grad = (weights * (grad_prob - shift)).astype(jnp.bfloat16)
                here = (
                    matmul(score_grad, keys) * scale,
                    matmul_left_t(score_grad, query_part) * scale,
                    matmul_left_t(weights.astype(jnp.bfloat16), grads),
                )
                if found is None:
                    found = here
                else:
                    found = [jnp.where(own, new, old) for new, old in zip(here, found)]
            for ref, value in zip((grad_query, grad_keys, grad_values), found):
                ref[:, columns] = value.astype(jnp.bfloat16)

        head_pairs(query_ref.shape[1], one_pair)

    return attention_call(
        kernel,
        [low(*query_rows.shape), low(*incoming_keys.shape), low(*incoming_keys.shape)],
        count,
        [query_rows, incoming_keys, incoming_values, grad_mixed],
        waited,
    )


TILE = 256


def in_tiles(size, body):
    def step(index, carry):
        body(pl.ds(pl.multiple_of(index * TILE, TILE), TILE))
        return carry

    lax.fori_loop(0, size // TILE, step, 0)


def wide_view(ref, rows):
    return ref[rows, :].astype(jnp.float32)


def first_and_opposite(rows, total):
    return slice(0, rows), slice(total // 2, total // 2 + rows)


def square_schulz(mine, sibling, rows, *waited):
    size = mine.shape[1]
    half = mine.shape[0]

    def kernel(mine_ref, sibling_ref, *refs):
        result, current, gram, poly, total = refs[len(waited) :]
        current[:half], current[half:] = mine_ref[...], sibling_ref[...]
        total[...] = jnp.zeros_like(total)

        def add_squares(rows):
            part = wide_view(current, rows)
            total[...] += jnp.sum(part * part, axis=0, keepdims=True)

        in_tiles(size, add_squares)
        scale = 1.0 / (jnp.sqrt(jnp.sum(total[...])) + 1e-07)

        def scaled(rows):
            current[rows, :] = (wide_view(current, rows) * scale).astype(jnp.bfloat16)

        in_tiles(size, scaled)
        for sweep_index in range(NS_STEPS):

            def gram_rows(rows):
                gram[rows, :] = matmul_right_t(current[rows, :], current[...]).astype(
                    jnp.bfloat16
                )

            def poly_rows(rows):
                poly[rows, :] = (
                    SCHULZ_SECOND * wide_view(gram, rows)
                    + SCHULZ_THIRD * matmul(gram[rows, :], gram[...])
                ).astype(jnp.bfloat16)

            def next_rows(rows):
                gram[rows, :] = (
                    SCHULZ_FIRST * wide_view(current, rows) + matmul(poly[rows, :], current[...])
                ).astype(jnp.bfloat16)

            in_tiles(size, gram_rows)
            if sweep_index == NS_STEPS - 1:
                for block, here in enumerate(first_and_opposite(rows, half)):
                    poly_rows(here)
                    result[block] = (
                        SCHULZ_FIRST * wide_view(current, here)
                        + matmul(poly[here, :], current[...])
                    ).astype(jnp.bfloat16)
            else:
                in_tiles(size, poly_rows)
                in_tiles(size, next_rows)
                current[...] = gram[...]

    vmem = pl.BlockSpec(memory_space=pltpu.VMEM)
    return pl.pallas_call(
        kernel,
        out_shape=low(2, rows, size),
        in_specs=[vmem] * 2 + [pl.BlockSpec(memory_space=pl.ANY)] * len(waited),
        out_specs=vmem,
        scratch_shapes=[pltpu.VMEM((size, size), jnp.bfloat16)] * 3
        + [pltpu.VMEM((1, size), jnp.float32)],
        compiler_params=pltpu.CompilerParams(vmem_limit_bytes=56 * 2**20),
        cost_estimate=SMALL,
    )(mine, sibling, *waited)


def gram_parts(place, mine, sibling, reps, *waited):
    size = mine.shape[1]
    half = mine.shape[0]
    part = size // (2 * reps)

    def kernel(place_ref, mine_ref, sibling_ref, *refs):
        to_x, to_y, kept, later, both, gram = refs[len(waited) :]
        both[:half], both[half:] = mine_ref[...], sibling_ref[...]
        is_lower = place_ref[3] == 1

        def row_products(rows):
            gram[rows, :] = matmul_right_t(both[rows, :], both[...]).astype(jnp.bfloat16)

        def column_products(columns):
            gram[columns, :] = matmul_left_t(both[:, columns], both[...]).astype(jnp.bfloat16)

        @pl.when(is_lower)
        def _():
            in_tiles(size, row_products)

        @pl.when(jnp.logical_not(is_lower))
        def _():
            in_tiles(size, column_products)

        def piece(step, index):
            first_row = (place_ref[0] ^ step) * (2 * part) + index * part
            return gram[pl.ds(pl.multiple_of(first_row, part), part), :]

        to_x[0, 0], to_x[0, 1] = piece(1, 0), piece(3, 0)
        to_y[0, 0], to_y[0, 1] = piece(2, 1), piece(3, 1)
        kept[0, 0], kept[0, 1] = piece(0, 0), piece(0, 1)
        later[0, 0], later[0, 1] = piece(2, 0), piece(1, 1)

    vmem = pl.BlockSpec(memory_space=pltpu.VMEM)
    return pl.pallas_call(
        kernel,
        out_shape=tuple([low(1, 2, part, size)] * 4),
        in_specs=[pl.BlockSpec(memory_space=pltpu.SMEM)]
        + [vmem] * 2
        + [pl.BlockSpec(memory_space=pl.ANY)] * len(waited),
        out_specs=tuple([vmem] * 4),
        scratch_shapes=[pltpu.VMEM((size, size), jnp.bfloat16)] * 2,
        compiler_params=pltpu.CompilerParams(vmem_limit_bytes=56 * 2**20),
        cost_estimate=SMALL,
    )(place, mine, sibling, *waited)


def gram_schulz(place, quarters, mine, sibling, rows, *waited):
    size = mine.shape[1]
    half_rows = mine.shape[0]
    part = quarters[0].shape[0]

    def kernel(place_ref, q_ref, x_ref, y_ref, a_ref, b_ref, mine_ref, sibling_ref, *refs):
        result, gram, product, current, poly, half, unit = refs[len(waited) :]
        my_rep = place_ref[0]

        def put(step, offset, ref):
            first_row = (my_rep ^ step) * part + offset
            size_here = ref.shape[0]
            gram[pl.ds(pl.multiple_of(first_row, size_here), size_here), :] = ref[...]

        put(0, 0, q_ref)
        put(1, 0, x_ref)
        put(2, 0, y_ref)
        put(3, 0, a_ref)
        put(3, part // 2, b_ref)

        def trace_of(index, total):
            rows = pl.ds(pl.multiple_of(index * TILE, TILE), TILE)
            here = wide_view(gram, rows)
            row_number = lax.broadcasted_iota(jnp.int32, here.shape, 0) + index * TILE
            column_number = lax.broadcasted_iota(jnp.int32, here.shape, 1)
            return total + jnp.sum(jnp.where(row_number == column_number, here, 0.0))

        trace = lax.fori_loop(0, size // TILE, trace_of, jnp.float32(0.0))
        scale = (1.0 / (jnp.sqrt(jnp.full((8, 128), trace)) + 1e-07))[0:1, 0:1]
        unit[:half_rows] = (mine_ref[...].astype(jnp.float32) * scale).astype(jnp.bfloat16)
        unit[half_rows:] = (sibling_ref[...].astype(jnp.float32) * scale).astype(jnp.bfloat16)

        def scaled(rows):
            current[rows, :] = (wide_view(gram, rows) * (scale * scale)).astype(jnp.bfloat16)

        in_tiles(size, scaled)
        factor = 1.0
        for sweep_index in range(NS_STEPS):

            def poly_rows(rows):
                poly[rows, :] = (
                    SCHULZ_SECOND * wide_view(current, rows)
                    + SCHULZ_THIRD * matmul(current[rows, :], current[...])
                ).astype(jnp.bfloat16)

            def product_rows(rows):
                half[rows, :] = (
                    SCHULZ_FIRST * wide_view(product, rows)
                    + factor * wide_view(poly, rows)
                    + matmul(poly[rows, :], product[...])
                ).astype(jnp.bfloat16)

            def half_rows_of(rows):
                half[rows, :] = (
                    SCHULZ_FIRST * wide_view(current, rows) + matmul(poly[rows, :], current[...])
                ).astype(jnp.bfloat16)

            def current_rows(rows):
                current[rows, :] = (
                    SCHULZ_FIRST * wide_view(half, rows) + matmul(half[rows, :], poly[...])
                ).astype(jnp.bfloat16)

            in_tiles(size, poly_rows)
            if sweep_index == 0:
                product[...] = poly[...]
            else:
                in_tiles(size, product_rows)
                product[...] = half[...]
            factor = factor * SCHULZ_FIRST
            if sweep_index < NS_STEPS - 1:
                in_tiles(size, half_rows_of)
                in_tiles(size, current_rows)

        is_lower = place_ref[3] == 1
        for block, here in enumerate(first_and_opposite(rows, half_rows)):
            plain = factor * wide_view(unit, here)

            @pl.when(is_lower)
            def _():
                turned = matmul(product[here, :], unit[...])
                result[block] = (plain + turned).astype(jnp.bfloat16)

            @pl.when(jnp.logical_not(is_lower))
            def _():
                turned = matmul(unit[here, :], product[...])
                result[block] = (plain + turned).astype(jnp.bfloat16)

    vmem = pl.BlockSpec(memory_space=pltpu.VMEM)
    return pl.pallas_call(
        kernel,
        out_shape=low(2, rows, size),
        in_specs=[pl.BlockSpec(memory_space=pltpu.SMEM)]
        + [vmem] * 7
        + [pl.BlockSpec(memory_space=pl.ANY)] * len(waited),
        out_specs=vmem,
        scratch_shapes=[pltpu.VMEM((size, size), jnp.bfloat16)] * 6,
        compiler_params=pltpu.CompilerParams(vmem_limit_bytes=56 * 2**20),
        cost_estimate=SMALL,
    )(place, *quarters, mine, sibling, *waited)


def low(*shape):
    return jax.ShapeDtypeStruct(shape, jnp.bfloat16)


def fresh_blocks(place, own, arrived, moments, *waited):
    kinds, rows, width = own.shape
    chips = len(arrived) + 1

    def kernel(place_ref, own_ref, *refs):
        arrived_refs = refs[: chips - 1]
        moment_ref = refs[chips - 1]
        grad_ref, *out = refs[chips + len(waited) : -1]
        fresh_ref = refs[-1]
        for kind in range(kinds):
            grad_ref[kind] = add_low(own_ref[kind], *[ref[kind] for ref in arrived_refs])
            fresh_ref[kind] = (
                MOMENTUM_DECAY * moment_ref[kind] + grad_ref[kind].astype(jnp.float32)
            ).astype(jnp.bfloat16)
        for turn in range(chips):
            chip = lax.rem(place_ref[1] + chips - turn, chips)
            out[turn][...] = fresh_ref[jnp.where(chip < chips // 2, 0, 1)]

    vmem = pl.BlockSpec(memory_space=pltpu.VMEM)
    return pl.pallas_call(
        kernel,
        out_shape=tuple([low(kinds, rows, width)] + [low(rows, width)] * chips),
        in_specs=[pl.BlockSpec(memory_space=pltpu.SMEM)]
        + [vmem] * (chips + 1)
        + [pl.BlockSpec(memory_space=pl.ANY)] * len(waited),
        out_specs=tuple([vmem] * (chips + 1)),
        scratch_shapes=[pltpu.VMEM((kinds, rows, width), jnp.bfloat16)],
        compiler_params=pltpu.CompilerParams(vmem_limit_bytes=56 * 2**20),
        cost_estimate=SMALL,
    )(place, own, *arrived, moments, *waited)


def first_seen(arrays):
    kept, index = [], []
    for array in arrays:
        found = [place for place, other in enumerate(kept) if other is array]
        if not found:
            kept.append(array)
        index.append(found[0] if found else len(kept) - 1)
    return kept, index


def weight_rows(place, kinds, received=None, waited=()):
    count = len(kinds)
    steps = len(kinds[0][0])
    rows, width = kinds[0][0][0].shape[1] // 2, kinds[0][1][0].shape[1]
    half = rows // 2
    is_own = received is not None
    aligned = all(kind[2] % 128 == 0 for kind in kinds)
    lefts, left_index = first_seen([left for kind in kinds for left in kind[0]])
    rights, right_index = first_seen([right for kind in kinds for right in kind[1]])
    core_rows = [
        kinds[left_index.index(index) // steps][2] for index in range(len(lefts))
    ]
    if not aligned:
        def chosen(left, size):
            cut = left.reshape(left.shape[0], -1, 2, size)
            first_core = (place[2] == 0) if is_own else (place[2] == 1)
            return jnp.where(first_core, cut[:, :, 0], cut[:, :, 1]).reshape(left.shape[0], rows)

        lefts = [chosen(left, size) for left, size in zip(lefts, core_rows)]
    arrays = lefts + rights + (list(received) if is_own else [])

    def kernel(place_ref, *refs):
        left_refs = refs[: len(lefts)]
        right_refs = refs[len(lefts) : len(lefts) + len(rights)]
        received_refs = refs[len(lefts) + len(rights) : len(arrays)]
        rest = refs[len(arrays) + len(waited) :]
        core = place_ref[2] if is_own else 1 - place_ref[2]

        def columns(index):
            ref, size = left_refs[index], core_rows[index]
            if not aligned:
                return ref[...]
            parts = [
                ref[:, pl.ds(pl.multiple_of((2 * chip + core) * size, 128), size)]
                for chip in range(rows // size)
            ]
            return jnp.concatenate(parts, axis=1)

        for kind in range(count):
            for block in range(steps):
                spot = kind * steps + block
                total = matmul_left_t(
                    columns(left_index[spot]), right_refs[right_index[spot]][...]
                )
                step = (place_ref[0] ^ block) if kinds[kind][3] else block
                if is_own:
                    total = total + received_refs[kind][step].astype(jnp.float32)
                    rest[4][kind, step] = total.astype(jnp.bfloat16)
                else:
                    rest[kind][step] = total.astype(jnp.bfloat16)
            if is_own:
                to_x, to_y, kept, later, sums = rest
                to_x[kind, 0], to_x[kind, 1] = sums[kind, 1, :half], sums[kind, 3, :half]
                to_y[kind, 0], to_y[kind, 1] = sums[kind, 2, half:], sums[kind, 3, half:]
                kept[kind, 0], kept[kind, 1] = sums[kind, 0, :half], sums[kind, 0, half:]
                later[kind, 0], later[kind, 1] = sums[kind, 2, :half], sums[kind, 1, half:]

    if is_own:
        out_shapes = [low(count, 2, half, width)] * 4
    else:
        out_shapes = [low(steps, rows, width)] * count
    vmem = pl.BlockSpec(memory_space=pltpu.VMEM)
    flops = sum(2 * rows * width * left.shape[0] for kind in kinds for left in kind[0])
    return pl.pallas_call(
        kernel,
        out_shape=tuple(out_shapes),
        in_specs=[pl.BlockSpec(memory_space=pltpu.SMEM)]
        + [vmem] * len(arrays)
        + [pl.BlockSpec(memory_space=pl.ANY)] * len(waited),
        out_specs=tuple([vmem] * len(out_shapes)),
        scratch_shapes=(
            [pltpu.VMEM((count, steps, rows, width), jnp.bfloat16)] if is_own else []
        ),
        compiler_params=pltpu.CompilerParams(vmem_limit_bytes=56 * 2**20),
        cost_estimate=SMALL,
    )(place, *arrays, *waited)


def later_sums(later, by_x, by_y, waited):
    def kernel(later_ref, x_ref, y_ref, *refs):
        to_y, to_x = refs[-2:]
        for kind in range(later_ref.shape[0]):
            to_y[kind] = add_low(later_ref[kind, 0], x_ref[kind, 1])
            to_x[kind] = add_low(later_ref[kind, 1], y_ref[kind, 1])

    vmem = pl.BlockSpec(memory_space=pltpu.VMEM)
    shape = low(later.shape[0], *later.shape[2:])
    return pl.pallas_call(
        kernel,
        out_shape=(shape, shape),
        in_specs=[vmem] * 3 + [pl.BlockSpec(memory_space=pl.ANY)] * len(waited),
        out_specs=(vmem, vmem),
        compiler_params=pltpu.CompilerParams(vmem_limit_bytes=56 * 2**20),
        cost_estimate=SMALL,
    )(later, by_x, by_y, *waited)


def held_until(value, *waited):
    def kernel(*refs):
        del refs

    anywhere = pl.BlockSpec(memory_space=pl.ANY)
    return pl.pallas_call(
        kernel,
        out_shape=jax.ShapeDtypeStruct(value.shape, value.dtype),
        in_specs=[anywhere] * (1 + len(waited)),
        out_specs=anywhere,
        input_output_aliases={0: 0},
        compiler_params=pltpu.CompilerParams(
            vmem_limit_bytes=56 * 2**20, has_side_effects=True
        ),
        cost_estimate=SMALL,
    )(value, *waited)


def sorted_blocks(place, kept, by_x, by_y, last_x, last_y, chips, waited):
    kinds, _, half, width = kept.shape
    rows = 2 * half // chips

    def kernel(place_ref, kept_ref, x_ref, y_ref, last_x_ref, last_y_ref, *refs):
        out, whole = refs[len(waited) : -1], refs[-1]
        for kind in range(kinds):
            whole[: chips // 2] = add_low(
                kept_ref[kind, 0], x_ref[kind, 0], last_y_ref[kind]
            ).reshape(chips // 2, rows, width)
            whole[chips // 2 :] = add_low(
                kept_ref[kind, 1], y_ref[kind, 0], last_x_ref[kind]
            ).reshape(chips // 2, rows, width)
            for turn in range(chips):
                out[turn][kind] = whole[lax.rem(place_ref[1] + turn, chips)]

    vmem = pl.BlockSpec(memory_space=pltpu.VMEM)
    return pl.pallas_call(
        kernel,
        out_shape=tuple([low(kinds, rows, width)] * chips),
        in_specs=[pl.BlockSpec(memory_space=pltpu.SMEM)]
        + [vmem] * 5
        + [pl.BlockSpec(memory_space=pl.ANY)] * len(waited),
        out_specs=tuple([vmem] * chips),
        scratch_shapes=[pltpu.VMEM((chips, rows, width), jnp.bfloat16)],
        compiler_params=pltpu.CompilerParams(vmem_limit_bytes=56 * 2**20),
        cost_estimate=SMALL,
    )(place, kept, by_x, by_y, last_x, last_y, *waited)


def held_until(value, *waited):
    def kernel(*refs):
        del refs

    anywhere = pl.BlockSpec(memory_space=pl.ANY)
    return pl.pallas_call(
        kernel,
        out_shape=jax.ShapeDtypeStruct(value.shape, value.dtype),
        in_specs=[anywhere] * (1 + len(waited)),
        out_specs=anywhere,
        input_output_aliases={0: 0},
        compiler_params=pltpu.CompilerParams(
            vmem_limit_bytes=56 * 2**20, has_side_effects=True
        ),
        cost_estimate=SMALL,
    )(value, *waited)


def stretch(shape):
    return math.sqrt(max(shape[0], shape[1]) / min(shape[0], shape[1]))


def add_low(*terms):
    total = terms[0].astype(jnp.float32)
    for term in terms[1:]:
        total = total + term.astype(jnp.float32)
    return total.astype(jnp.bfloat16)


def phase_blocks(arrived, by_x, by_y, waited):
    given = [*(arrived or []), *([by_x, by_y] if by_x is not None else [])]
    width = given[0].shape[-1]
    if arrived:
        rows, turns = arrived[0].shape[0], len(arrived)
        total = rows * turns
        half = total // 2
    else:
        total, half = 0, by_x.shape[0] // 3
    send = total + (half if by_x is not None else 0)
    came = by_x.shape[0] if by_x is not None else 0
    out_shapes = [low(send, width)] * 2 + [low(2 * came + total, width)]

    def kernel(*refs):
        inputs = list(refs[: len(given)])
        to_x, to_y, to_core = refs[len(given) + len(waited) :]
        if arrived:
            for turn in range(turns):
                here = slice(turn * rows, (turn + 1) * rows)
                block = inputs.pop(0)[...]
                to_x[here] = to_y[here] = block
                first_row = 2 * came + turn * rows
                to_core[first_row : first_row + rows] = block
        if by_x is not None:
            x_ref, y_ref = inputs.pop(0), inputs.pop(0)
            to_x[total:] = y_ref[:half]
            to_y[total:] = x_ref[half : 2 * half]
            to_core[:came], to_core[came : 2 * came] = x_ref[...], y_ref[...]

    vmem = pl.BlockSpec(memory_space=pltpu.VMEM)
    return pl.pallas_call(
        kernel,
        out_shape=tuple(out_shapes),
        in_specs=[vmem] * len(given) + [pl.BlockSpec(memory_space=pl.ANY)] * len(waited),
        out_specs=tuple([vmem] * len(out_shapes)),
        compiler_params=pltpu.CompilerParams(vmem_limit_bytes=56 * 2**20),
        cost_estimate=SMALL,
    )(*given, *waited)


def block_shares(shares):
    flat = [part[0] if isinstance(part, tuple) else part for share in shares for part in share]
    starts = [part[1] for share in shares for part in share[1:]]
    return flat, starts


def start_blocks(place_ref, flat_refs, starts, out, sem_of, kind, chips, by_rep):
    reps, rows = flat_refs[0].shape[1:3]
    turns = chips - 1
    half = turns * rows // 2
    my_rep, my_chip, my_core = place_ref[0], place_ref[1], place_ref[2]
    cuts = []
    for turn in range(turns):
        low_end, high_end = turn * rows, (turn + 1) * rows
        middle = min(max(half, low_end), high_end)
        if middle > low_end:
            cuts.append((0, low_end, turn, 0, middle - low_end))
        if high_end > middle:
            cuts.append((1, middle - half, turn, middle - low_end, high_end - middle))
    copies = [[] for step in range(reps)]

    def start(step, source, target):
        copy = pltpu.make_async_copy(source, target, sem_of(step, len(copies[step])))
        copy.start()
        copies[step].append(copy)

    for step in range(reps):
        from_rep = my_rep ^ step
        to_rep = from_rep if by_rep else step
        for side in range(2):
            core = my_core if side == 0 else 1 - my_core
            own, *moved = flat_refs[6 * side : 6 * side + 6]
            first_rows = starts[5 * side : 5 * side + 5]
            start(step, own.at[kind, from_rep], out.at[to_rep, my_chip, core])
            if step < reps - 1:
                for turn in range(turns):
                    start(
                        step,
                        moved[step].at[pl.ds(first_rows[step] + turn * rows, rows)],
                        out.at[to_rep, lax.rem(my_chip + 1 + turn, chips), core],
                    )
            else:
                for part, source_row, turn, target_row, count in cuts:
                    start(
                        step,
                        moved[3 + part].at[pl.ds(first_rows[3 + part] + source_row, count)],
                        out.at[
                            to_rep,
                            lax.rem(my_chip + 1 + turn, chips),
                            core,
                            pl.ds(target_row, count),
                        ],
                    )
    return copies


def placed_blocks(place, shares, kind, chips, waited):
    reps, rows, width = shares[0][0].shape[1:]
    flat, starts = block_shares(shares)

    def kernel(place_ref, *refs):
        results = refs[len(flat) + len(waited) : -3]
        out, sems, out_sems = refs[-3:]
        copies = start_blocks(
            place_ref,
            refs[: len(flat)],
            starts,
            out,
            lambda step, index: sems.at[step, index],
            kind,
            chips,
            True,
        )
        for step in range(reps):
            for copy in copies[step]:
                copy.wait()
        writes = [
            pltpu.make_async_copy(out.at[step], results[step], out_sems.at[step])
            for step in range(reps)
        ]
        for write in writes:
            write.start()
        for write in writes:
            write.wait()

    shape = (reps, chips, 2, rows, width)
    anywhere = pl.BlockSpec(memory_space=pl.ANY)
    full = pl.pallas_call(
        kernel,
        out_shape=tuple([low(*shape[1:])] * reps),
        in_specs=[pl.BlockSpec(memory_space=pltpu.SMEM)] + [anywhere] * (len(flat) + len(waited)),
        out_specs=tuple([anywhere] * reps),
        scratch_shapes=[
            pltpu.VMEM(shape, jnp.bfloat16),
            pltpu.SemaphoreType.DMA((reps, 2 * chips + 2)),
            pltpu.SemaphoreType.DMA((reps,)),
        ],
        compiler_params=pltpu.CompilerParams(vmem_limit_bytes=56 * 2**20),
        cost_estimate=SMALL,
    )(place, *flat, *waited)
    return [matrix.reshape(-1, width) for matrix in full]


GELU_SCALE = math.sqrt(2.0 / math.pi)
GELU_CUBE = 0.044715


def feed_forward(place, in_shares, out_shares, chips, third_low, residual, grad_branch):
    reps, rows, width = in_shares[0][0].shape[1:]
    in_flat, in_starts = block_shares(in_shares)
    out_flat, out_starts = block_shares(out_shares)
    tokens = third_low.shape[0]

    def kernel(place_ref, third_ref, residual_ref, branch_ref, *refs):
        in_refs = refs[: len(in_flat)]
        out_refs = refs[len(in_flat) : len(in_flat) + len(out_flat)]
        block_out, grad_third, *parts = refs[len(in_flat) + len(out_flat) : -3]
        hidden, grad_pre = parts[:reps], parts[reps:]
        in_full, out_full, sems = refs[-3:]
        in_copies = start_blocks(
            place_ref, in_refs, in_starts, in_full,
            lambda step, index: sems.at[0, step, index], 2, chips, False,
        )
        out_copies = start_blocks(
            place_ref, out_refs, out_starts, out_full,
            lambda step, index: sems.at[1, step, index], 3, chips, False,
        )
        for step in range(reps):
            for copy in in_copies[step]:
                copy.wait()
            in_weights = in_full[step].reshape(-1, width)
            pre = matmul(third_ref[...], in_weights)
            for copy in out_copies[step]:
                copy.wait()
            out_weights = out_full[step].reshape(-1, width)
            grad_hidden = matmul_right_t(branch_ref[...], out_weights)
            square = pre * pre
            bent = jnp.tanh(GELU_SCALE * pre * (1.0 + GELU_CUBE * square))
            units = (0.5 * pre * (1.0 + bent)).astype(jnp.bfloat16)
            slope = 0.5 * (1.0 + bent) + 0.5 * pre * (1.0 - bent * bent) * GELU_SCALE * (
                1.0 + 3.0 * GELU_CUBE * square
            )
            grads = (grad_hidden * slope).astype(jnp.bfloat16)
            hidden[step][...] = units
            grad_pre[step][...] = grads
            to_third = matmul_right_t(grads, in_weights)
            to_out = matmul(units, out_weights)
            if step == 0:
                grad_third[...] = to_third
                block_out[...] = residual_ref[...] + to_out
            else:
                grad_third[...] += to_third
                block_out[...] += to_out

    vmem = pl.BlockSpec(memory_space=pltpu.VMEM)
    whole = jax.ShapeDtypeStruct((tokens, width), jnp.float32)
    shape = (reps, chips, 2, rows, width)
    results = pl.pallas_call(
        kernel,
        out_shape=(whole, whole, *[low(tokens, width)] * (2 * reps)),
        in_specs=[pl.BlockSpec(memory_space=pltpu.SMEM)]
        + [vmem] * 3
        + [pl.BlockSpec(memory_space=pl.ANY)] * (len(in_flat) + len(out_flat)),
        out_specs=(vmem,) * (2 + 2 * reps),
        scratch_shapes=[
            pltpu.VMEM(shape, jnp.bfloat16),
            pltpu.VMEM(shape, jnp.bfloat16),
            pltpu.SemaphoreType.DMA((2, reps, 2 * chips + 2)),
        ],
        compiler_params=pltpu.CompilerParams(vmem_limit_bytes=56 * 2**20),
        cost_estimate=SMALL,
    )(place, third_low, residual, grad_branch, *in_flat, *out_flat)
    block_out, grad_third, *parts = results
    return block_out, grad_third, parts[:reps], parts[reps:]


def prepared(place, matrices, moments, shards, sub, waited):
    reps, rows, width = matrices[0].shape

    def kernel(place_ref, *refs):
        stacks, hidden_in, hidden_out = refs[0:2], refs[2], refs[3]
        old_stacks, old_in, old_out = refs[4:6], refs[6], refs[7]
        whole, *outs = refs[8 + len(waited) :]
        quarters, wide_old, square_old, sems = outs[:3], outs[3], outs[4], outs[5]
        my_rep = place_ref[0]
        copies = []

        def start(source, target):
            copy = pltpu.make_async_copy(source, target, sems.at[len(copies)])
            copy.start()
            copies.append(copy)

        for kind in range(2):
            start(old_stacks[kind].at[my_rep], square_old.at[kind])
        start(old_out.at[pl.ds(pl.multiple_of(my_rep * sub, sub), sub)], wide_old.at[1])
        for shard in range(shards):
            first = pl.multiple_of((shard * reps + my_rep) * sub, sub)
            start(
                old_in.at[:, pl.ds(first, sub)],
                wide_old.at[0, :, pl.ds(shard * sub, sub)],
            )
        for kind in range(2):
            whole[kind] = stacks[kind][...].astype(jnp.bfloat16)
        for step in range(reps):
            for shard in range(shards):
                first = (shard * reps + step) * sub
                whole[2, step, :, shard * sub : (shard + 1) * sub] = hidden_in[
                    :, first : first + sub
                ].astype(jnp.bfloat16)
            whole[3, step] = hidden_out[step * sub : (step + 1) * sub].astype(jnp.bfloat16)
        for kind in range(1, 4):
            quarters[kind - 1][...] = whole[kind, my_rep]
        for copy in copies:
            copy.wait()

    vmem = pl.BlockSpec(memory_space=pltpu.VMEM)
    anywhere = pl.BlockSpec(memory_space=pl.ANY)
    old = jax.ShapeDtypeStruct((2, rows, width), jnp.float32)
    whole, *parts, wide_old, square_old = pl.pallas_call(
        kernel,
        out_shape=(low(4, reps, rows, width), *[low(rows, width)] * 3, old, old),
        in_specs=[pl.BlockSpec(memory_space=pltpu.SMEM)]
        + [vmem] * 4
        + [anywhere] * (4 + len(waited)),
        out_specs=(vmem,) * 6,
        scratch_shapes=[pltpu.SemaphoreType.DMA((shards + 3,))],
        compiler_params=pltpu.CompilerParams(vmem_limit_bytes=56 * 2**20),
        cost_estimate=SMALL,
    )(place, *matrices, *moments, *waited)
    return whole, parts, wide_old, square_old


def on_device(
    tokens,
    states,
    cotangent,
    dec_len,
    enc_len,
    self_weights,
    cross_weights,
    fc_in,
    fc_out,
    norm_params,
    self_moment,
    cross_moment,
    fc_in_moment,
    fc_out_moment,
    norm_moment,
):
    reps = lax.axis_size("rep")
    shards = lax.axis_size("shard")
    chips = shards // 2
    my_rep = lax.axis_index("rep")
    my_place = lax.axis_index("shard")
    my_chip = my_place // 2
    my_core = lax.rem(my_place, 2)
    even = my_core == 0
    width = self_weights.shape[2]
    rows = self_weights.shape[1]
    hidden_width = fc_in.shape[1]
    sub = hidden_width // (shards * reps)

    def swap(values):
        return lax.ppermute(values, "shard", [(index, index ^ 1) for index in range(shards)])

    def from_chip(values, turn):
        pairs = [
            (2 * ((chip + turn) % chips) + core, 2 * chip + core)
            for chip in range(chips)
            for core in range(2)
        ]
        return lax.ppermute(values, "shard", pairs)

    def from_rep(values, step):
        return lax.ppermute(values, "rep", [(index ^ step, index) for index in range(reps)])

    low_bit = (my_rep & 1) == 1
    high_bit = (my_rep & 2) == 2

    def by_rep(steps):
        turned = [jnp.where(low_bit, steps[step ^ 1], steps[step]) for step in range(reps)]
        return [jnp.where(high_bit, turned[step ^ 2], turned[step]) for step in range(reps)]

    is_lower = my_chip < chips // 2
    place_now = jnp.stack([my_rep, my_chip, my_core, is_lower]).astype(jnp.int32)

    def gather_kinds(quarter, prepare):
        arrived, by_x, by_y, came = [], [], [], []
        arrived.append([from_chip(quarter, turn) for turn in range(1, chips)])
        shards, quarters, *others = prepare(arrived[0][0])
        count = shards.shape[0]
        other_shards = swap(shards)
        for phase in range(count + 1):
            waited = [came[-1]] if phase > 1 else [shards, *quarters] if phase == 0 else []
            to_x, to_y, to_core = phase_blocks(
                arrived[phase] if phase < count else None,
                by_x[-1] if phase > 0 else None,
                by_y[-1] if phase > 0 else None,
                [*waited, other_shards] if phase == 1 else waited,
            )
            if phase + 1 < count:
                quarter = held_until(quarters[phase], to_core)
                arrived.append([from_chip(quarter, turn) for turn in range(1, chips)])
            by_x.append(from_rep(to_x, 1))
            by_y.append(from_rep(to_y, 2))
            came.append(swap(to_core))
        came.append((swap(by_x[-1]), swap(by_y[-1])))
        total = (chips - 1) * rows
        shares = []
        for kind in range(count):
            size = total if kind == 0 else total + total // 2
            next_size = total // 2 if kind == count - 1 else total + total // 2
            behind = next_size - total // 2
            before = 0 if kind == 0 else 2 * (total if kind == 1 else total + total // 2)
            mine = [
                shards,
                (jnp.concatenate(arrived[kind]), 0),
                (by_x[kind], 0),
                (by_y[kind], 0),
                (by_x[kind + 1], behind),
                (by_y[kind + 1], behind),
            ]
            last = came[kind + 2]
            siblings = [
                other_shards,
                (came[kind], before),
                (came[kind + 1], 0),
                (came[kind + 1], size),
                (last[0], behind) if kind == count - 1 else (last, behind),
                (last[1], behind) if kind == count - 1 else (last, next_size + behind),
            ]
            shares.append((mine, siblings))
        return shares, others

    def of_rep(values):
        return lax.dynamic_index_in_dim(values, my_rep, 0, keepdims=False)

    def in_quarters(matrix):
        return matrix.reshape(rows, shards, reps, sub).transpose(2, 0, 1, 3).reshape(
            reps, rows, shards * sub
        )

    def in_shard(pieces):
        cut = jnp.stack(pieces).reshape(reps, rows, shards, sub)
        return cut.transpose(1, 2, 0, 3).reshape(rows, hidden_width)

    def prepare(first):
        matrices = [self_weights, cross_weights, fc_in, fc_out]
        moments = [self_moment, cross_moment, fc_in_moment, fc_out_moment]
        if sub % 128 == 0:
            return prepared(place_now, matrices, moments, shards, sub, [first])
        whole = jnp.stack(
            [
                self_weights.astype(jnp.bfloat16),
                cross_weights.astype(jnp.bfloat16),
                in_quarters(fc_in.astype(jnp.bfloat16)),
                fc_out.reshape(reps, sub, width).astype(jnp.bfloat16),
            ]
        )
        wide_old = [of_rep(in_quarters(fc_in_moment)), of_rep(moments[3].reshape(reps, sub, width))]
        square_old = [of_rep(self_moment), of_rep(cross_moment)]
        quarters = [of_rep(whole[kind]) for kind in range(1, 4)]
        return whole, quarters, jnp.stack(wide_old), jnp.stack(square_old)

    shares, (wide_moments, square_moments) = gather_kinds(
        of_rep(self_weights).astype(jnp.bfloat16), prepare
    )
    self_full = placed_blocks(place_now, shares[0], 0, chips, [])
    cross_full = placed_blocks(place_now, shares[1], 1, chips, [])

    def first_sums(kinds, others, *waited):
        received = [swap(other) for other in others]
        to_x, to_y, kept, later = weight_rows(place_now, kinds, received, waited)
        return kept, later, from_rep(to_x, 1), from_rep(to_y, 2)

    def second_sums(stage, *waited):
        kept, later, by_x, by_y = stage
        to_y, to_x = later_sums(later, by_x, by_y, waited)
        return (kept, by_x, by_y, from_rep(to_x, 1), from_rep(to_y, 2)), to_x

    def third_sums(stage, *waited):
        blocks = sorted_blocks(place_now, *stage, chips, waited)
        arrived = [from_chip(blocks[chips - turn], turn) for turn in range(1, chips)]
        return blocks[0], arrived

    def share_pair(pair, *waited):
        by_x, by_y = from_rep(pair, 1), from_rep(pair, 2)
        across = jnp.stack([from_rep(by_y[0], 1), from_rep(by_x[1], 2)])
        return [pair, by_x, by_y, across]

    def to_replicas(steps):
        return by_rep([step[0] for step in steps]), by_rep([step[1] for step in steps])

    source = tokens[0].astype(jnp.float32)
    encoded = states[0]
    gain_rows = norm_params[0]
    bias_rows = norm_params[1]
    first, first_unit, first_inv = normalize_parts(source, gain_rows[0], bias_rows[0])
    first_low = first.astype(jnp.bfloat16)
    query_rows = matmul(first_low, self_full[0]).astype(jnp.bfloat16)
    incoming_keys = matmul(first_low, self_full[1]).astype(jnp.bfloat16)
    incoming_values = matmul(first_low, self_full[2]).astype(jnp.bfloat16)
    attended_values = attend_forward(query_rows, incoming_keys, incoming_values, dec_len, True)
    after_self = source + matmul(attended_values, self_full[3])
    second, second_unit, second_inv = normalize_parts(after_self, gain_rows[1], bias_rows[1])
    second_low = second.astype(jnp.bfloat16)
    cross_query = matmul(second_low, cross_full[0]).astype(jnp.bfloat16)
    cross_keys = matmul(encoded, cross_full[1]).astype(jnp.bfloat16)
    cross_values = matmul(encoded, cross_full[2]).astype(jnp.bfloat16)
    cross_mixed = attend_forward(cross_query, cross_keys, cross_values, enc_len, False)
    after_cross = after_self + matmul(cross_mixed, cross_full[3])
    third, third_unit, third_inv = normalize_parts(after_cross, gain_rows[2], bias_rows[2])
    third_low = third.astype(jnp.bfloat16)
    grad_out = cotangent[0].astype(jnp.float32)
    grad_branch = cotangent[0]
    block_out, grad_third, hidden, grad_pre = feed_forward(
        place_now, shares[2], shares[3], chips, third_low, after_cross, grad_branch
    )
    wide_kinds = [
        ([third_low] * reps, grad_pre, rows, False),
        (hidden, [grad_branch] * reps, sub, False),
    ]
    wide_other = weight_rows(place_now, wide_kinds)
    wide_stage = first_sums(wide_kinds, wide_other)
    grad_norm, third_gain, third_bias = normalize_back(
        grad_third, third_unit, third_inv, gain_rows[2]
    )
    grad_cross = grad_out + grad_norm
    cross_branch = grad_cross.astype(jnp.bfloat16)
    grad_mixed = matmul_right_t(cross_branch, cross_full[3]).astype(jnp.bfloat16)
    grad_cq, grad_ck, grad_cv = attend_backward(
        cross_query, cross_keys, cross_values, enc_len, False, grad_mixed, wide_stage[0]
    )
    cross_kind = (
        [second_low, encoded, encoded, cross_mixed],
        [grad_cq, grad_ck, grad_cv, cross_branch],
        rows,
        True,
    )
    cross_other = weight_rows(place_now, [cross_kind])[0]
    grad_second = matmul_right_t(grad_cq, cross_full[0])
    grad_norm, second_gain, second_bias = normalize_back(
        grad_second, second_unit, second_inv, gain_rows[1]
    )
    grad_self = grad_cross + grad_norm
    self_branch = grad_self.astype(jnp.bfloat16)
    grad_mixed = matmul_right_t(self_branch, self_full[3]).astype(jnp.bfloat16)
    wide_stage, wide_token = second_sums(wide_stage, grad_mixed)
    cross_stage = first_sums([cross_kind], [cross_other], wide_token)
    grad_sq, grad_sk, grad_sv = attend_backward(
        query_rows, incoming_keys, incoming_values, dec_len, True, grad_mixed, cross_stage[0]
    )
    self_kind = (
        [first_low, first_low, first_low, attended_values],
        [grad_sq, grad_sk, grad_sv, self_branch],
        rows,
        True,
    )
    self_other = weight_rows(place_now, [self_kind])[0]
    wide_stage = third_sums(wide_stage, self_other)
    cross_stage, cross_token = second_sums(cross_stage, wide_stage[0])
    self_stage = first_sums([self_kind], [self_other], cross_token)
    grad_sq = held_until(grad_sq, self_stage[0])
    grad_states = matmul_right_t(grad_ck, cross_full[1]) + matmul_right_t(grad_cv, cross_full[2])
    grad_first = (
        matmul_right_t(grad_sq, self_full[0])
        + matmul_right_t(grad_sk, self_full[1])
        + matmul_right_t(grad_sv, self_full[2])
    )
    grad_norm, first_gain, first_bias = normalize_back(
        grad_first, first_unit, first_inv, gain_rows[0]
    )
    grad_tokens = grad_self + grad_norm
    def owned(grads_fresh):
        mine, *sent = grads_fresh[1:]
        arrived = [from_chip(sent[turn - 1], turn) for turn in range(1, chips)]
        mine = jnp.concatenate([mine, *arrived])
        return mine, swap(mine)

    def to_both(result):
        other = from_chip(result[1], chips // 2)
        return jnp.stack(
            [jnp.where(is_lower, result[0], other), jnp.where(is_lower, other, result[0])]
        )

    self_stage, self_token = second_sums(self_stage)
    wide_fresh = fresh_blocks(place_now, *wide_stage, wide_moments)
    wide_grads = wide_fresh[0]
    wide_own = owned(wide_fresh)
    cross_stage = third_sums(cross_stage, wide_grads)
    self_stage = third_sums(self_stage)
    to_x, to_y, kept, later = gram_parts(place_now, *wide_own, reps, self_token)
    gram_stage, gram_token = second_sums((kept, later, from_rep(to_x, 1), from_rep(to_y, 2)))
    kept, by_x, by_y, last_x, last_y = gram_stage
    quarter = jnp.concatenate(
        [add_low(kept[0, 0], by_x[0, 0], last_y[0]), add_low(kept[0, 1], by_y[0, 0], last_x[0])]
    )
    quarter_x, quarter_y = from_rep(quarter, 1), from_rep(quarter, 2)
    part = quarter.shape[0] // 2
    quarters = [
        quarter,
        quarter_x,
        quarter_y,
        from_rep(quarter_y[:part], 1),
        from_rep(quarter_x[part:], 2),
    ]
    square_fresh = fresh_blocks(
        place_now,
        jnp.concatenate([self_stage[0], cross_stage[0]]),
        [jnp.concatenate(pair) for pair in zip(self_stage[1], cross_stage[1])],
        square_moments,
    )
    square_grads = square_fresh[0]
    square_own = owned(square_fresh)
    wide_grads_shared = share_pair(wide_grads)
    square_grads_shared = share_pair(square_grads)
    wide_rows = gram_schulz(
        place_now, quarters, *wide_own, rows, wide_grads_shared[1], self_stage[0]
    )
    wide_orth_shared = share_pair(to_both(wide_rows))
    square_rows = square_schulz(
        *square_own, rows, wide_rows, square_grads_shared[1], wide_grads_shared[3]
    )
    square_orth = held_until(
        to_both(square_rows), wide_orth_shared[3], square_grads_shared[3]
    )
    square_orth_shared = share_pair(square_orth)
    norm_local = jnp.stack(
        [
            jnp.stack([first_gain, second_gain, third_gain]),
            jnp.stack([first_bias, second_bias, third_bias]),
        ]
    )
    norm_local = held_until(norm_local, quarters[-1])
    norm_total = norm_local + swap(norm_local)
    norm_total = norm_total + from_rep(norm_total, 1)
    norm_total = norm_total + from_rep(norm_total, 2)
    norm_total = sum([from_chip(norm_total, turn) for turn in range(1, chips)], norm_total)
    width_part = norm_moment.shape[2]
    norm_grad = lax.dynamic_slice_in_dim(norm_total, my_place * width_part, width_part, 2)

    in_shared, out_shared = to_replicas(wide_grads_shared)
    self_shared, cross_shared = to_replicas(square_grads_shared)
    in_orth_shared, out_orth_shared = to_replicas(wide_orth_shared)
    self_orth_shared, cross_orth_shared = to_replicas(square_orth_shared)

    def stacked(pieces):
        return jnp.stack(pieces).astype(jnp.float32)

    def lengthwise(pieces):
        return jnp.concatenate(pieces).astype(jnp.float32)

    self_grad = stacked(self_shared)
    cross_grad = stacked(cross_shared)
    fc_in_grad = in_shard(in_shared).astype(jnp.float32)
    fc_out_grad = lengthwise(out_shared)
    self_orth = stacked(self_orth_shared)
    cross_orth = stacked(cross_orth_shared)
    in_orth = in_shard(in_orth_shared).astype(jnp.float32)
    out_orth = lengthwise(out_orth_shared)

    self_fresh = MOMENTUM_DECAY * self_moment + self_grad
    cross_fresh = MOMENTUM_DECAY * cross_moment + cross_grad
    in_fresh = MOMENTUM_DECAY * fc_in_moment + fc_in_grad
    out_fresh = MOMENTUM_DECAY * fc_out_moment + fc_out_grad
    norm_fresh = MOMENTUM_DECAY * norm_moment + norm_grad
    self_new = self_weights - MATRIX_RATE * stretch((width, width)) * self_orth
    cross_new = cross_weights - MATRIX_RATE * stretch((width, width)) * cross_orth
    in_new = fc_in - MATRIX_RATE * stretch((width, hidden_width)) * in_orth
    out_new = fc_out - MATRIX_RATE * stretch((hidden_width, width)) * out_orth
    own_params = lax.dynamic_slice_in_dim(norm_params, my_place * width_part, width_part, 2)
    total_tokens = reps * shards * tokens.shape[0] * tokens.shape[1]
    norm_new = own_params - VECTOR_RATE * norm_fresh / math.sqrt(total_tokens)
    return (
        block_out[None].astype(jnp.bfloat16),
        grad_tokens[None].astype(jnp.bfloat16),
        grad_states[None].astype(jnp.bfloat16),
        self_grad,
        cross_grad,
        fc_in_grad,
        fc_out_grad,
        norm_grad,
        self_fresh,
        cross_fresh,
        in_fresh,
        out_fresh,
        norm_fresh,
        self_new,
        cross_new,
        in_new,
        out_new,
        norm_new,
        self_new.astype(jnp.bfloat16),
        cross_new.astype(jnp.bfloat16),
        in_new.astype(jnp.bfloat16),
        out_new.astype(jnp.bfloat16),
    )


def solution(mesh):
    placed = (
        P(("rep", "shard"), None, None),
        P(("rep", "shard"), None, None),
        P(("rep", "shard"), None, None),
        P(("rep", "shard")),
        P(("rep", "shard")),
        P(None, "shard", None),
        P(None, "shard", None),
        P("shard", None),
        P("shard", None),
        P(),
        P(None, "shard", None),
        P(None, "shard", None),
        P("shard", None),
        P("shard", None),
        P(None, None, "shard"),
    )
    return jax.shard_map(
        on_device,
        mesh=mesh,
        in_specs=placed,
        out_specs=(
            P(("rep", "shard"), None, None),
            P(("rep", "shard"), None, None),
            P(("rep", "shard"), None, None),
            P(None, "shard", None),
            P(None, "shard", None),
            P("shard", None),
            P("shard", None),
            P(None, None, "shard"),
            P(None, "shard", None),
            P(None, "shard", None),
            P("shard", None),
            P("shard", None),
            P(None, None, "shard"),
            P(None, "shard", None),
            P(None, "shard", None),
            P("shard", None),
            P("shard", None),
            P(None, None, "shard"),
            P(None, "shard", None),
            P(None, "shard", None),
            P("shard", None),
            P("shard", None),
        ),
        check_vma=False,
    )
```

```python
import math

import jax
import jax.numpy as jnp
from jax import lax
from jax.experimental import pallas as pl
from jax.experimental.pallas import tpu as pltpu
from jax.sharding import PartitionSpec as P

HEADS = 16
HEAD_DIM = 64
NS_STEPS = 3


NORM_EPSILON = 1e-05
MOMENTUM_DECAY = 0.9
MATRIX_RATE = 0.6
VECTOR_RATE = 0.05
SCHULZ_FIRST = 3.4445
SCHULZ_SECOND = -4.775
SCHULZ_THIRD = 2.0315


def matmul(left, right):
    return jnp.dot(left, right, preferred_element_type=jnp.float32)


def matmul_left_t(left, right):
    return lax.dot_general(
        left, right, (((0,), (0,)), ((), ())), preferred_element_type=jnp.float32
    )


def matmul_right_t(left, right):
    return lax.dot_general(
        left, right, (((1,), (1,)), ((), ())), preferred_element_type=jnp.float32
    )


def normalize_parts(values, gain, bias):
    centered = values - jnp.mean(values, axis=-1, keepdims=True)
    inverse = lax.rsqrt(jnp.mean(centered * centered, axis=-1, keepdims=True) + NORM_EPSILON)
    unit_part = centered * inverse
    return (unit_part * gain + bias, unit_part, inverse)


def normalize_back(grad_out, unit_part, inverse, gain):
    grad_unit = grad_out * gain
    grad_in = inverse * (
        grad_unit
        - jnp.mean(grad_unit, axis=-1, keepdims=True)
        - unit_part * jnp.mean(grad_unit * unit_part, axis=-1, keepdims=True)
    )
    return (grad_in, jnp.sum(grad_out * unit_part, axis=0), jnp.sum(grad_out, axis=0))


PAIR = 2 * HEAD_DIM
SMALL = pl.CostEstimate(flops=1024, bytes_accessed=1024, transcendentals=0)


def attention_parts(count_ref, causal, query_part, keys, is_first):
    lane = lax.broadcasted_iota(jnp.int32, (1, PAIR), 1)
    own = (lane < HEAD_DIM) == is_first
    scores = matmul_right_t(jnp.where(own, query_part, 0), keys) * HEAD_DIM ** (-0.5)
    key_place = lax.broadcasted_iota(jnp.int32, scores.shape, 1)
    valid = key_place < count_ref[0]
    if causal:
        valid = valid & (key_place <= lax.broadcasted_iota(jnp.int32, scores.shape, 0))
    scores = jnp.where(valid, scores, -jnp.inf)
    exponent = jnp.exp(scores - jnp.max(scores, axis=-1, keepdims=True))
    return exponent / jnp.sum(exponent, axis=-1, keepdims=True), own


def head_pairs(width, body):
    def step(index, carry):
        body(pl.ds(pl.multiple_of(index * PAIR, PAIR), PAIR))
        return carry

    lax.fori_loop(0, width // PAIR, step, 0)


def attention_call(kernel, out_shapes, count, arrays, waited):
    rows, width = arrays[0].shape
    keys = arrays[1].shape[0]
    vmem = pl.BlockSpec(memory_space=pltpu.VMEM)
    return pl.pallas_call(
        kernel,
        out_shape=tuple(out_shapes),
        in_specs=[pl.BlockSpec(memory_space=pltpu.SMEM)]
        + [vmem] * len(arrays)
        + [pl.BlockSpec(memory_space=pl.ANY)] * len(waited),
        out_specs=tuple([vmem] * len(out_shapes)),
        compiler_params=pltpu.CompilerParams(vmem_limit_bytes=56 * 2**20),
        cost_estimate=SMALL,
    )(count, *arrays, *waited)


def attend_forward(query_rows, incoming_keys, incoming_values, count, causal, *waited):
    def kernel(count_ref, query_ref, key_ref, value_ref, *refs):
        mixed_ref = refs[-1]

        def one_pair(columns):
            query_part, keys = query_ref[:, columns], key_ref[:, columns]
            values = value_ref[:, columns]
            mixed = None
            for is_first in (True, False):
                weights, own = attention_parts(count_ref, causal, query_part, keys, is_first)
                here = matmul(weights.astype(jnp.bfloat16), values)
                mixed = here if mixed is None else jnp.where(own, here, mixed)
            mixed_ref[:, columns] = mixed.astype(jnp.bfloat16)

        head_pairs(query_ref.shape[1], one_pair)

    return attention_call(
        kernel,
        [low(*query_rows.shape)],
        count,
        [query_rows, incoming_keys, incoming_values],
        waited,
    )[0]


def attend_backward(
    query_rows, incoming_keys, incoming_values, count, causal, grad_mixed, *waited
):
    def kernel(count_ref, query_ref, key_ref, value_ref, grad_ref, *refs):
        grad_query, grad_keys, grad_values = refs[-3:]
        scale = HEAD_DIM ** (-0.5)

        def one_pair(columns):
            query_part, keys = query_ref[:, columns], key_ref[:, columns]
            values, grads = value_ref[:, columns], grad_ref[:, columns]
            found = None
            for is_first in (True, False):
                weights, own = attention_parts(count_ref, causal, query_part, keys, is_first)
                grad_prob = matmul_right_t(jnp.where(own, grads, 0), values)
                shift = jnp.sum(grad_prob * weights, axis=-1, keepdims=True)
                score_grad = (weights * (grad_prob - shift)).astype(jnp.bfloat16)
                here = (
                    matmul(score_grad, keys) * scale,
                    matmul_left_t(score_grad, query_part) * scale,
                    matmul_left_t(weights.astype(jnp.bfloat16), grads),
                )
                if found is None:
                    found = here
                else:
                    found = [jnp.where(own, new, old) for new, old in zip(here, found)]
            for ref, value in zip((grad_query, grad_keys, grad_values), found):
                ref[:, columns] = value.astype(jnp.bfloat16)

        head_pairs(query_ref.shape[1], one_pair)

    return attention_call(
        kernel,
        [low(*query_rows.shape), low(*incoming_keys.shape), low(*incoming_keys.shape)],
        count,
        [query_rows, incoming_keys, incoming_values, grad_mixed],
        waited,
    )


TILE = 256


def in_tiles(size, body):
    def step(index, carry):
        body(pl.ds(pl.multiple_of(index * TILE, TILE), TILE))
        return carry

    lax.fori_loop(0, size // TILE, step, 0)


def wide_view(ref, rows):
    return ref[rows, :].astype(jnp.float32)


def first_and_opposite(rows, total):
    return slice(0, rows), slice(total // 2, total // 2 + rows)


def square_schulz(mine, sibling, rows, *waited):
    size = mine.shape[1]
    half = mine.shape[0]

    def kernel(mine_ref, sibling_ref, *refs):
        result, current, gram, poly, total = refs[len(waited) :]
        current[:half], current[half:] = mine_ref[...], sibling_ref[...]
        total[...] = jnp.zeros_like(total)

        def add_squares(rows):
            part = wide_view(current, rows)
            total[...] += jnp.sum(part * part, axis=0, keepdims=True)

        in_tiles(size, add_squares)
        scale = 1.0 / (jnp.sqrt(jnp.sum(total[...])) + 1e-07)

        def scaled(rows):
            current[rows, :] = (wide_view(current, rows) * scale).astype(jnp.bfloat16)

        in_tiles(size, scaled)
        for sweep_index in range(NS_STEPS):

            def gram_rows(rows):
                gram[rows, :] = matmul_right_t(current[rows, :], current[...]).astype(
                    jnp.bfloat16
                )

            def poly_rows(rows):
                poly[rows, :] = (
                    SCHULZ_SECOND * wide_view(gram, rows)
                    + SCHULZ_THIRD * matmul(gram[rows, :], gram[...])
                ).astype(jnp.bfloat16)

            def next_rows(rows):
                gram[rows, :] = (
                    SCHULZ_FIRST * wide_view(current, rows) + matmul(poly[rows, :], current[...])
                ).astype(jnp.bfloat16)

            in_tiles(size, gram_rows)
            if sweep_index == NS_STEPS - 1:
                for block, here in enumerate(first_and_opposite(rows, half)):
                    poly_rows(here)
                    result[block] = (
                        SCHULZ_FIRST * wide_view(current, here)
                        + matmul(poly[here, :], current[...])
                    ).astype(jnp.bfloat16)
            else:
                in_tiles(size, poly_rows)
                in_tiles(size, next_rows)
                current[...] = gram[...]

    vmem = pl.BlockSpec(memory_space=pltpu.VMEM)
    return pl.pallas_call(
        kernel,
        out_shape=low(2, rows, size),
        in_specs=[vmem] * 2 + [pl.BlockSpec(memory_space=pl.ANY)] * len(waited),
        out_specs=vmem,
        scratch_shapes=[pltpu.VMEM((size, size), jnp.bfloat16)] * 3
        + [pltpu.VMEM((1, size), jnp.float32)],
        compiler_params=pltpu.CompilerParams(vmem_limit_bytes=56 * 2**20),
        cost_estimate=SMALL,
    )(mine, sibling, *waited)


def gram_parts(place, mine, sibling, reps, *waited):
    size = mine.shape[1]
    half = mine.shape[0]
    part = size // (2 * reps)

    def kernel(place_ref, mine_ref, sibling_ref, *refs):
        to_x, to_y, kept, later, both, gram = refs[len(waited) :]
        both[:half], both[half:] = mine_ref[...], sibling_ref[...]
        is_lower = place_ref[3] == 1

        def row_products(rows):
            gram[rows, :] = matmul_right_t(both[rows, :], both[...]).astype(jnp.bfloat16)

        def column_products(columns):
            gram[columns, :] = matmul_left_t(both[:, columns], both[...]).astype(jnp.bfloat16)

        @pl.when(is_lower)
        def _():
            in_tiles(size, row_products)

        @pl.when(jnp.logical_not(is_lower))
        def _():
            in_tiles(size, column_products)

        def piece(step, index):
            first_row = (place_ref[0] ^ step) * (2 * part) + index * part
            return gram[pl.ds(pl.multiple_of(first_row, part), part), :]

        to_x[0, 0], to_x[0, 1] = piece(1, 0), piece(3, 0)
        to_y[0, 0], to_y[0, 1] = piece(2, 1), piece(3, 1)
        kept[0, 0], kept[0, 1] = piece(0, 0), piece(0, 1)
        later[0, 0], later[0, 1] = piece(2, 0), piece(1, 1)

    vmem = pl.BlockSpec(memory_space=pltpu.VMEM)
    return pl.pallas_call(
        kernel,
        out_shape=tuple([low(1, 2, part, size)] * 4),
        in_specs=[pl.BlockSpec(memory_space=pltpu.SMEM)]
        + [vmem] * 2
        + [pl.BlockSpec(memory_space=pl.ANY)] * len(waited),
        out_specs=tuple([vmem] * 4),
        scratch_shapes=[pltpu.VMEM((size, size), jnp.bfloat16)] * 2,
        compiler_params=pltpu.CompilerParams(vmem_limit_bytes=56 * 2**20),
        cost_estimate=SMALL,
    )(place, mine, sibling, *waited)


def gram_schulz(place, quarters, mine, sibling, rows, *waited):
    size = mine.shape[1]
    half_rows = mine.shape[0]
    part = quarters[0].shape[0]

    def kernel(place_ref, q_ref, x_ref, y_ref, a_ref, b_ref, mine_ref, sibling_ref, *refs):
        result, gram, product, current, poly, half, unit = refs[len(waited) :]
        my_rep = place_ref[0]

        def put(step, offset, ref):
            first_row = (my_rep ^ step) * part + offset
            size_here = ref.shape[0]
            gram[pl.ds(pl.multiple_of(first_row, size_here), size_here), :] = ref[...]

        put(0, 0, q_ref)
        put(1, 0, x_ref)
        put(2, 0, y_ref)
        put(3, 0, a_ref)
        put(3, part // 2, b_ref)

        def trace_of(index, total):
            rows = pl.ds(pl.multiple_of(index * TILE, TILE), TILE)
            here = wide_view(gram, rows)
            row_number = lax.broadcasted_iota(jnp.int32, here.shape, 0) + index * TILE
            column_number = lax.broadcasted_iota(jnp.int32, here.shape, 1)
            return total + jnp.sum(jnp.where(row_number == column_number, here, 0.0))

        trace = lax.fori_loop(0, size // TILE, trace_of, jnp.float32(0.0))
        scale = (1.0 / (jnp.sqrt(jnp.full((8, 128), trace)) + 1e-07))[0:1, 0:1]
        unit[:half_rows] = (mine_ref[...].astype(jnp.float32) * scale).astype(jnp.bfloat16)
        unit[half_rows:] = (sibling_ref[...].astype(jnp.float32) * scale).astype(jnp.bfloat16)

        def scaled(rows):
            current[rows, :] = (wide_view(gram, rows) * (scale * scale)).astype(jnp.bfloat16)

        in_tiles(size, scaled)
        factor = 1.0
        for sweep_index in range(NS_STEPS):

            def poly_rows(rows):
                poly[rows, :] = (
                    SCHULZ_SECOND * wide_view(current, rows)
                    + SCHULZ_THIRD * matmul(current[rows, :], current[...])
                ).astype(jnp.bfloat16)

            def product_rows(rows):
                half[rows, :] = (
                    SCHULZ_FIRST * wide_view(product, rows)
                    + factor * wide_view(poly, rows)
                    + matmul(poly[rows, :], product[...])
                ).astype(jnp.bfloat16)

            def half_rows_of(rows):
                half[rows, :] = (
                    SCHULZ_FIRST * wide_view(current, rows) + matmul(poly[rows, :], current[...])
                ).astype(jnp.bfloat16)

            def current_rows(rows):
                current[rows, :] = (
                    SCHULZ_FIRST * wide_view(half, rows) + matmul(half[rows, :], poly[...])
                ).astype(jnp.bfloat16)

            in_tiles(size, poly_rows)
            if sweep_index == 0:
                product[...] = poly[...]
            else:
                in_tiles(size, product_rows)
                product[...] = half[...]
            factor = factor * SCHULZ_FIRST
            if sweep_index < NS_STEPS - 1:
                in_tiles(size, half_rows_of)
                in_tiles(size, current_rows)

        is_lower = place_ref[3] == 1
        for block, here in enumerate(first_and_opposite(rows, half_rows)):
            plain = factor * wide_view(unit, here)

            @pl.when(is_lower)
            def _():
                turned = matmul(product[here, :], unit[...])
                result[block] = (plain + turned).astype(jnp.bfloat16)

            @pl.when(jnp.logical_not(is_lower))
            def _():
                turned = matmul(unit[here, :], product[...])
                result[block] = (plain + turned).astype(jnp.bfloat16)

    vmem = pl.BlockSpec(memory_space=pltpu.VMEM)
    return pl.pallas_call(
        kernel,
        out_shape=low(2, rows, size),
        in_specs=[pl.BlockSpec(memory_space=pltpu.SMEM)]
        + [vmem] * 7
        + [pl.BlockSpec(memory_space=pl.ANY)] * len(waited),
        out_specs=vmem,
        scratch_shapes=[pltpu.VMEM((size, size), jnp.bfloat16)] * 6,
        compiler_params=pltpu.CompilerParams(vmem_limit_bytes=56 * 2**20),
        cost_estimate=SMALL,
    )(place, *quarters, mine, sibling, *waited)


def low(*shape):
    return jax.ShapeDtypeStruct(shape, jnp.bfloat16)


def fresh_blocks(place, own, arrived, moments, *waited):
    kinds, rows, width = own.shape
    chips = len(arrived) + 1

    def kernel(place_ref, own_ref, *refs):
        arrived_refs = refs[: chips - 1]
        moment_ref = refs[chips - 1]
        grad_ref, *out = refs[chips + len(waited) : -1]
        fresh_ref = refs[-1]
        for kind in range(kinds):
            grad_ref[kind] = add_low(own_ref[kind], *[ref[kind] for ref in arrived_refs])
            fresh_ref[kind] = (
                MOMENTUM_DECAY * moment_ref[kind] + grad_ref[kind].astype(jnp.float32)
            ).astype(jnp.bfloat16)
        for turn in range(chips):
            chip = lax.rem(place_ref[1] + chips - turn, chips)
            out[turn][...] = fresh_ref[jnp.where(chip < chips // 2, 0, 1)]

    vmem = pl.BlockSpec(memory_space=pltpu.VMEM)
    return pl.pallas_call(
        kernel,
        out_shape=tuple([low(kinds, rows, width)] + [low(rows, width)] * chips),
        in_specs=[pl.BlockSpec(memory_space=pltpu.SMEM)]
        + [vmem] * (chips + 1)
        + [pl.BlockSpec(memory_space=pl.ANY)] * len(waited),
        out_specs=tuple([vmem] * (chips + 1)),
        scratch_shapes=[pltpu.VMEM((kinds, rows, width), jnp.bfloat16)],
        compiler_params=pltpu.CompilerParams(vmem_limit_bytes=56 * 2**20),
        cost_estimate=SMALL,
    )(place, own, *arrived, moments, *waited)


def first_seen(arrays):
    kept, index = [], []
    for array in arrays:
        found = [place for place, other in enumerate(kept) if other is array]
        if not found:
            kept.append(array)
        index.append(found[0] if found else len(kept) - 1)
    return kept, index


def weight_rows(place, kinds, received=None, waited=()):
    count = len(kinds)
    steps = len(kinds[0][0])
    rows, width = kinds[0][0][0].shape[1] // 2, kinds[0][1][0].shape[1]
    half = rows // 2
    is_own = received is not None
    aligned = all(kind[2] % 128 == 0 for kind in kinds)
    lefts, left_index = first_seen([left for kind in kinds for left in kind[0]])
    rights, right_index = first_seen([right for kind in kinds for right in kind[1]])
    core_rows = [
        kinds[left_index.index(index) // steps][2] for index in range(len(lefts))
    ]
    if not aligned:
        def chosen(left, size):
            cut = left.reshape(left.shape[0], -1, 2, size)
            first_core = (place[2] == 0) if is_own else (place[2] == 1)
            return jnp.where(first_core, cut[:, :, 0], cut[:, :, 1]).reshape(left.shape[0], rows)

        lefts = [chosen(left, size) for left, size in zip(lefts, core_rows)]
    arrays = lefts + rights + (list(received) if is_own else [])

    def kernel(place_ref, *refs):
        left_refs = refs[: len(lefts)]
        right_refs = refs[len(lefts) : len(lefts) + len(rights)]
        received_refs = refs[len(lefts) + len(rights) : len(arrays)]
        rest = refs[len(arrays) + len(waited) :]
        core = place_ref[2] if is_own else 1 - place_ref[2]

        def columns(index):
            ref, size = left_refs[index], core_rows[index]
            if not aligned:
                return ref[...]
            parts = [
                ref[:, pl.ds(pl.multiple_of((2 * chip + core) * size, 128), size)]
                for chip in range(rows // size)
            ]
            return jnp.concatenate(parts, axis=1)

        for kind in range(count):
            for block in range(steps):
                spot = kind * steps + block
                total = matmul_left_t(
                    columns(left_index[spot]), right_refs[right_index[spot]][...]
                )
                step = (place_ref[0] ^ block) if kinds[kind][3] else block
                if is_own:
                    total = total + received_refs[kind][step].astype(jnp.float32)
                    rest[4][kind, step] = total.astype(jnp.bfloat16)
                else:
                    rest[kind][step] = total.astype(jnp.bfloat16)
            if is_own:
                to_x, to_y, kept, later, sums = rest
                to_x[kind, 0], to_x[kind, 1] = sums[kind, 1, :half], sums[kind, 3, :half]
                to_y[kind, 0], to_y[kind, 1] = sums[kind, 2, half:], sums[kind, 3, half:]
                kept[kind, 0], kept[kind, 1] = sums[kind, 0, :half], sums[kind, 0, half:]
                later[kind, 0], later[kind, 1] = sums[kind, 2, :half], sums[kind, 1, half:]

    if is_own:
        out_shapes = [low(count, 2, half, width)] * 4
    else:
        out_shapes = [low(steps, rows, width)] * count
    vmem = pl.BlockSpec(memory_space=pltpu.VMEM)
    flops = sum(2 * rows * width * left.shape[0] for kind in kinds for left in kind[0])
    return pl.pallas_call(
        kernel,
        out_shape=tuple(out_shapes),
        in_specs=[pl.BlockSpec(memory_space=pltpu.SMEM)]
        + [vmem] * len(arrays)
        + [pl.BlockSpec(memory_space=pl.ANY)] * len(waited),
        out_specs=tuple([vmem] * len(out_shapes)),
        scratch_shapes=(
            [pltpu.VMEM((count, steps, rows, width), jnp.bfloat16)] if is_own else []
        ),
        compiler_params=pltpu.CompilerParams(vmem_limit_bytes=56 * 2**20),
        cost_estimate=SMALL,
    )(place, *arrays, *waited)


def later_sums(later, by_x, by_y, waited):
    def kernel(later_ref, x_ref, y_ref, *refs):
        to_y, to_x = refs[-2:]
        for kind in range(later_ref.shape[0]):
            to_y[kind] = add_low(later_ref[kind, 0], x_ref[kind, 1])
            to_x[kind] = add_low(later_ref[kind, 1], y_ref[kind, 1])

    vmem = pl.BlockSpec(memory_space=pltpu.VMEM)
    shape = low(later.shape[0], *later.shape[2:])
    return pl.pallas_call(
        kernel,
        out_shape=(shape, shape),
        in_specs=[vmem] * 3 + [pl.BlockSpec(memory_space=pl.ANY)] * len(waited),
        out_specs=(vmem, vmem),
        compiler_params=pltpu.CompilerParams(vmem_limit_bytes=56 * 2**20),
        cost_estimate=SMALL,
    )(later, by_x, by_y, *waited)


def held_until(value, *waited):
    def kernel(*refs):
        del refs

    anywhere = pl.BlockSpec(memory_space=pl.ANY)
    return pl.pallas_call(
        kernel,
        out_shape=jax.ShapeDtypeStruct(value.shape, value.dtype),
        in_specs=[anywhere] * (1 + len(waited)),
        out_specs=anywhere,
        input_output_aliases={0: 0},
        compiler_params=pltpu.CompilerParams(
            vmem_limit_bytes=56 * 2**20, has_side_effects=True
        ),
        cost_estimate=SMALL,
    )(value, *waited)


def sorted_blocks(place, kept, by_x, by_y, last_x, last_y, chips, waited):
    kinds, _, half, width = kept.shape
    rows = 2 * half // chips

    def kernel(place_ref, kept_ref, x_ref, y_ref, last_x_ref, last_y_ref, *refs):
        out, whole = refs[len(waited) : -1], refs[-1]
        for kind in range(kinds):
            whole[: chips // 2] = add_low(
                kept_ref[kind, 0], x_ref[kind, 0], last_y_ref[kind]
            ).reshape(chips // 2, rows, width)
            whole[chips // 2 :] = add_low(
                kept_ref[kind, 1], y_ref[kind, 0], last_x_ref[kind]
            ).reshape(chips // 2, rows, width)
            for turn in range(chips):
                out[turn][kind] = whole[lax.rem(place_ref[1] + turn, chips)]

    vmem = pl.BlockSpec(memory_space=pltpu.VMEM)
    return pl.pallas_call(
        kernel,
        out_shape=tuple([low(kinds, rows, width)] * chips),
        in_specs=[pl.BlockSpec(memory_space=pltpu.SMEM)]
        + [vmem] * 5
        + [pl.BlockSpec(memory_space=pl.ANY)] * len(waited),
        out_specs=tuple([vmem] * chips),
        scratch_shapes=[pltpu.VMEM((chips, rows, width), jnp.bfloat16)],
        compiler_params=pltpu.CompilerParams(vmem_limit_bytes=56 * 2**20),
        cost_estimate=SMALL,
    )(place, kept, by_x, by_y, last_x, last_y, *waited)


def held_until(value, *waited):
    def kernel(*refs):
        del refs

    anywhere = pl.BlockSpec(memory_space=pl.ANY)
    return pl.pallas_call(
        kernel,
        out_shape=jax.ShapeDtypeStruct(value.shape, value.dtype),
        in_specs=[anywhere] * (1 + len(waited)),
        out_specs=anywhere,
        input_output_aliases={0: 0},
        compiler_params=pltpu.CompilerParams(
            vmem_limit_bytes=56 * 2**20, has_side_effects=True
        ),
        cost_estimate=SMALL,
    )(value, *waited)


def stretch(shape):
    return math.sqrt(max(shape[0], shape[1]) / min(shape[0], shape[1]))


def add_low(*terms):
    total = terms[0].astype(jnp.float32)
    for term in terms[1:]:
        total = total + term.astype(jnp.float32)
    return total.astype(jnp.bfloat16)


def phase_blocks(arrived, by_x, by_y, waited):
    given = [*(arrived or []), *([by_x, by_y] if by_x is not None else [])]
    width = given[0].shape[-1]
    if arrived:
        rows, turns = arrived[0].shape[0], len(arrived)
        total = rows * turns
        half = total // 2
    else:
        total, half = 0, by_x.shape[0] // 3
    send = total + (half if by_x is not None else 0)
    came = by_x.shape[0] if by_x is not None else 0
    out_shapes = [low(send, width)] * 2 + [low(2 * came + total, width)]

    def kernel(*refs):
        inputs = list(refs[: len(given)])
        to_x, to_y, to_core = refs[len(given) + len(waited) :]
        if arrived:
            for turn in range(turns):
                here = slice(turn * rows, (turn + 1) * rows)
                block = inputs.pop(0)[...]
                to_x[here] = to_y[here] = block
                first_row = 2 * came + turn * rows
                to_core[first_row : first_row + rows] = block
        if by_x is not None:
            x_ref, y_ref = inputs.pop(0), inputs.pop(0)
            to_x[total:] = y_ref[:half]
            to_y[total:] = x_ref[half : 2 * half]
            to_core[:came], to_core[came : 2 * came] = x_ref[...], y_ref[...]

    vmem = pl.BlockSpec(memory_space=pltpu.VMEM)
    return pl.pallas_call(
        kernel,
        out_shape=tuple(out_shapes),
        in_specs=[vmem] * len(given) + [pl.BlockSpec(memory_space=pl.ANY)] * len(waited),
        out_specs=tuple([vmem] * len(out_shapes)),
        compiler_params=pltpu.CompilerParams(vmem_limit_bytes=56 * 2**20),
        cost_estimate=SMALL,
    )(*given, *waited)


def block_shares(shares):
    flat = [part[0] if isinstance(part, tuple) else part for share in shares for part in share]
    starts = [part[1] for share in shares for part in share[1:]]
    return flat, starts


def start_blocks(place_ref, flat_refs, starts, out, sem_of, kind, chips, by_rep):
    reps, rows = flat_refs[0].shape[1:3]
    turns = chips - 1
    half = turns * rows // 2
    my_rep, my_chip, my_core = place_ref[0], place_ref[1], place_ref[2]
    cuts = []
    for turn in range(turns):
        low_end, high_end = turn * rows, (turn + 1) * rows
        middle = min(max(half, low_end), high_end)
        if middle > low_end:
            cuts.append((0, low_end, turn, 0, middle - low_end))
        if high_end > middle:
            cuts.append((1, middle - half, turn, middle - low_end, high_end - middle))
    copies = [[] for step in range(reps)]

    def start(step, source, target):
        copy = pltpu.make_async_copy(source, target, sem_of(step, len(copies[step])))
        copy.start()
        copies[step].append(copy)

    for step in range(reps):
        from_rep = my_rep ^ step
        to_rep = from_rep if by_rep else step
        for side in range(2):
            core = my_core if side == 0 else 1 - my_core
            own, *moved = flat_refs[6 * side : 6 * side + 6]
            first_rows = starts[5 * side : 5 * side + 5]
            start(step, own.at[kind, from_rep], out.at[to_rep, my_chip, core])
            if step < reps - 1:
                for turn in range(turns):
                    start(
                        step,
                        moved[step].at[pl.ds(first_rows[step] + turn * rows, rows)],
                        out.at[to_rep, lax.rem(my_chip + 1 + turn, chips), core],
                    )
            else:
                for part, source_row, turn, target_row, count in cuts:
                    start(
                        step,
                        moved[3 + part].at[pl.ds(first_rows[3 + part] + source_row, count)],
                        out.at[
                            to_rep,
                            lax.rem(my_chip + 1 + turn, chips),
                            core,
                            pl.ds(target_row, count),
                        ],
                    )
    return copies


def placed_blocks(place, shares, kind, chips, waited):
    reps, rows, width = shares[0][0].shape[1:]
    flat, starts = block_shares(shares)

    def kernel(place_ref, *refs):
        results = refs[len(flat) + len(waited) : -3]
        out, sems, out_sems = refs[-3:]
        copies = start_blocks(
            place_ref,
            refs[: len(flat)],
            starts,
            out,
            lambda step, index: sems.at[step, index],
            kind,
            chips,
            True,
        )
        for step in range(reps):
            for copy in copies[step]:
                copy.wait()
        writes = [
            pltpu.make_async_copy(out.at[step], results[step], out_sems.at[step])
            for step in range(reps)
        ]
        for write in writes:
            write.start()
        for write in writes:
            write.wait()

    shape = (reps, chips, 2, rows, width)
    anywhere = pl.BlockSpec(memory_space=pl.ANY)
    full = pl.pallas_call(
        kernel,
        out_shape=tuple([low(*shape[1:])] * reps),
        in_specs=[pl.BlockSpec(memory_space=pltpu.SMEM)] + [anywhere] * (len(flat) + len(waited)),
        out_specs=tuple([anywhere] * reps),
        scratch_shapes=[
            pltpu.VMEM(shape, jnp.bfloat16),
            pltpu.SemaphoreType.DMA((reps, 2 * chips + 2)),
            pltpu.SemaphoreType.DMA((reps,)),
        ],
        compiler_params=pltpu.CompilerParams(vmem_limit_bytes=56 * 2**20),
        cost_estimate=SMALL,
    )(place, *flat, *waited)
    return [matrix.reshape(-1, width) for matrix in full]


GELU_SCALE = math.sqrt(2.0 / math.pi)
GELU_CUBE = 0.044715


def feed_forward(place, in_shares, out_shares, chips, third_low, residual, grad_branch):
    reps, rows, width = in_shares[0][0].shape[1:]
    in_flat, in_starts = block_shares(in_shares)
    out_flat, out_starts = block_shares(out_shares)
    tokens = third_low.shape[0]

    def kernel(place_ref, third_ref, residual_ref, branch_ref, *refs):
        in_refs = refs[: len(in_flat)]
        out_refs = refs[len(in_flat) : len(in_flat) + len(out_flat)]
        block_out, grad_third, *parts = refs[len(in_flat) + len(out_flat) : -3]
        hidden, grad_pre = parts[:reps], parts[reps:]
        in_full, out_full, sems = refs[-3:]
        in_copies = start_blocks(
            place_ref, in_refs, in_starts, in_full,
            lambda step, index: sems.at[0, step, index], 2, chips, False,
        )
        out_copies = start_blocks(
            place_ref, out_refs, out_starts, out_full,
            lambda step, index: sems.at[1, step, index], 3, chips, False,
        )
        for step in range(reps):
            for copy in in_copies[step]:
                copy.wait()
            in_weights = in_full[step].reshape(-1, width)
            pre = matmul(third_ref[...], in_weights)
            for copy in out_copies[step]:
                copy.wait()
            out_weights = out_full[step].reshape(-1, width)
            grad_hidden = matmul_right_t(branch_ref[...], out_weights)
            square = pre * pre
            bent = jnp.tanh(GELU_SCALE * pre * (1.0 + GELU_CUBE * square))
            units = (0.5 * pre * (1.0 + bent)).astype(jnp.bfloat16)
            slope = 0.5 * (1.0 + bent) + 0.5 * pre * (1.0 - bent * bent) * GELU_SCALE * (
                1.0 + 3.0 * GELU_CUBE * square
            )
            grads = (grad_hidden * slope).astype(jnp.bfloat16)
            hidden[step][...] = units
            grad_pre[step][...] = grads
            to_third = matmul_right_t(grads, in_weights)
            to_out = matmul(units, out_weights)
            if step == 0:
                grad_third[...] = to_third
                block_out[...] = residual_ref[...] + to_out
            else:
                grad_third[...] += to_third
                block_out[...] += to_out

    vmem = pl.BlockSpec(memory_space=pltpu.VMEM)
    whole = jax.ShapeDtypeStruct((tokens, width), jnp.float32)
    shape = (reps, chips, 2, rows, width)
    results = pl.pallas_call(
        kernel,
        out_shape=(whole, whole, *[low(tokens, width)] * (2 * reps)),
        in_specs=[pl.BlockSpec(memory_space=pltpu.SMEM)]
        + [vmem] * 3
        + [pl.BlockSpec(memory_space=pl.ANY)] * (len(in_flat) + len(out_flat)),
        out_specs=(vmem,) * (2 + 2 * reps),
        scratch_shapes=[
            pltpu.VMEM(shape, jnp.bfloat16),
            pltpu.VMEM(shape, jnp.bfloat16),
            pltpu.SemaphoreType.DMA((2, reps, 2 * chips + 2)),
        ],
        compiler_params=pltpu.CompilerParams(vmem_limit_bytes=56 * 2**20),
        cost_estimate=SMALL,
    )(place, third_low, residual, grad_branch, *in_flat, *out_flat)
    block_out, grad_third, *parts = results
    return block_out, grad_third, parts[:reps], parts[reps:]


def prepared(place, matrices, moments, shards, sub, waited):
    reps, rows, width = matrices[0].shape

    def kernel(place_ref, *refs):
        stacks, hidden_in, hidden_out = refs[0:2], refs[2], refs[3]
        old_stacks, old_in, old_out = refs[4:6], refs[6], refs[7]
        whole, *outs = refs[8 + len(waited) :]
        quarters, wide_old, square_old, sems = outs[:3], outs[3], outs[4], outs[5]
        my_rep = place_ref[0]
        copies = []

        def start(source, target):
            copy = pltpu.make_async_copy(source, target, sems.at[len(copies)])
            copy.start()
            copies.append(copy)

        for kind in range(2):
            start(old_stacks[kind].at[my_rep], square_old.at[kind])
        start(old_out.at[pl.ds(pl.multiple_of(my_rep * sub, sub), sub)], wide_old.at[1])
        for shard in range(shards):
            first = pl.multiple_of((shard * reps + my_rep) * sub, sub)
            start(
                old_in.at[:, pl.ds(first, sub)],
                wide_old.at[0, :, pl.ds(shard * sub, sub)],
            )
        for kind in range(2):
            whole[kind] = stacks[kind][...].astype(jnp.bfloat16)
        for step in range(reps):
            for shard in range(shards):
                first = (shard * reps + step) * sub
                whole[2, step, :, shard * sub : (shard + 1) * sub] = hidden_in[
                    :, first : first + sub
                ].astype(jnp.bfloat16)
            whole[3, step] = hidden_out[step * sub : (step + 1) * sub].astype(jnp.bfloat16)
        for kind in range(1, 4):
            quarters[kind - 1][...] = whole[kind, my_rep]
        for copy in copies:
            copy.wait()

    vmem = pl.BlockSpec(memory_space=pltpu.VMEM)
    anywhere = pl.BlockSpec(memory_space=pl.ANY)
    old = jax.ShapeDtypeStruct((2, rows, width), jnp.float32)
    whole, *parts, wide_old, square_old = pl.pallas_call(
        kernel,
        out_shape=(low(4, reps, rows, width), *[low(rows, width)] * 3, old, old),
        in_specs=[pl.BlockSpec(memory_space=pltpu.SMEM)]
        + [vmem] * 4
        + [anywhere] * (4 + len(waited)),
        out_specs=(vmem,) * 6,
        scratch_shapes=[pltpu.SemaphoreType.DMA((shards + 3,))],
        compiler_params=pltpu.CompilerParams(vmem_limit_bytes=56 * 2**20),
        cost_estimate=SMALL,
    )(place, *matrices, *moments, *waited)
    return whole, parts, wide_old, square_old


def branch_back(grad_query, weights, stream, gain, grad_stream, next_weights, *waited):
    rows, width = stream.shape

    def kernel(query_ref, weights_ref, stream_ref, gain_ref, grad_ref, next_ref, *refs):
        total_ref, branch_ref, mixed_ref, gain_grad, bias_grad = refs[len(waited) :]
        grad_out = matmul_right_t(query_ref[...], weights_ref[...])
        values = stream_ref[...]
        centered = values - jnp.mean(values, axis=-1, keepdims=True)
        inverse = lax.rsqrt(jnp.mean(centered * centered, axis=-1, keepdims=True) + NORM_EPSILON)
        unit_part = centered * inverse
        grad_unit = grad_out * gain_ref[...]
        grad_in = inverse * (
            grad_unit
            - jnp.mean(grad_unit, axis=-1, keepdims=True)
            - unit_part * jnp.mean(grad_unit * unit_part, axis=-1, keepdims=True)
        )
        total = grad_ref[...] + grad_in
        branch = total.astype(jnp.bfloat16)
        total_ref[...] = total
        branch_ref[...] = branch
        mixed_ref[...] = matmul_right_t(branch, next_ref[...]).astype(jnp.bfloat16)
        gain_grad[...] = jnp.sum(grad_out * unit_part, axis=0, keepdims=True)
        bias_grad[...] = jnp.sum(grad_out, axis=0, keepdims=True)

    vmem = pl.BlockSpec(memory_space=pltpu.VMEM)
    line = jax.ShapeDtypeStruct((1, width), jnp.float32)
    return pl.pallas_call(
        kernel,
        out_shape=(
            jax.ShapeDtypeStruct((rows, width), jnp.float32),
            low(rows, width),
            low(rows, width),
            line,
            line,
        ),
        in_specs=[vmem] * 6 + [pl.BlockSpec(memory_space=pl.ANY)] * len(waited),
        out_specs=(vmem,) * 5,
        compiler_params=pltpu.CompilerParams(vmem_limit_bytes=56 * 2**20),
        cost_estimate=SMALL,
    )(grad_query, weights, stream, gain, grad_stream, next_weights, *waited)


def on_device(
    tokens,
    states,
    cotangent,
    dec_len,
    enc_len,
    self_weights,
    cross_weights,
    fc_in,
    fc_out,
    norm_params,
    self_moment,
    cross_moment,
    fc_in_moment,
    fc_out_moment,
    norm_moment,
):
    reps = lax.axis_size("rep")
    shards = lax.axis_size("shard")
    chips = shards // 2
    my_rep = lax.axis_index("rep")
    my_place = lax.axis_index("shard")
    my_chip = my_place // 2
    my_core = lax.rem(my_place, 2)
    even = my_core == 0
    width = self_weights.shape[2]
    rows = self_weights.shape[1]
    hidden_width = fc_in.shape[1]
    sub = hidden_width // (shards * reps)

    def swap(values):
        return lax.ppermute(values, "shard", [(index, index ^ 1) for index in range(shards)])

    def from_chip(values, turn):
        pairs = [
            (2 * ((chip + turn) % chips) + core, 2 * chip + core)
            for chip in range(chips)
            for core in range(2)
        ]
        return lax.ppermute(values, "shard", pairs)

    def from_rep(values, step):
        return lax.ppermute(values, "rep", [(index ^ step, index) for index in range(reps)])

    low_bit = (my_rep & 1) == 1
    high_bit = (my_rep & 2) == 2

    def by_rep(steps):
        turned = [jnp.where(low_bit, steps[step ^ 1], steps[step]) for step in range(reps)]
        return [jnp.where(high_bit, turned[step ^ 2], turned[step]) for step in range(reps)]

    is_lower = my_chip < chips // 2
    place_now = jnp.stack([my_rep, my_chip, my_core, is_lower]).astype(jnp.int32)

    def first_blocks(quarter):
        return [from_chip(quarter, turn) for turn in range(1, chips)]

    total_rows = (chips - 1) * rows

    def run_phase(state, phase, waited):
        to_x, to_y, to_core = phase_blocks(
            state["arrived"] if phase < 4 else None,
            state["by_x"][-1] if phase > 0 else None,
            state["by_y"][-1] if phase > 0 else None,
            [*waited, *state["came"][-1:]],
        )
        if phase < 3:
            quarter = held_until(state["quarters"][phase], to_core)
            state["arrived"] = first_blocks(quarter)
        state["sent"].append(to_x)
        state["by_x"].append(from_rep(to_x, 1))
        state["by_y"].append(from_rep(to_y, 2))
        state["came"].append(swap(to_core))

    def shares_of(state, kind, last_pair=None):
        by_x, by_y, came = state["by_x"], state["by_y"], state["came"]
        size = total_rows if kind == 0 else total_rows + total_rows // 2
        next_size = total_rows // 2 if kind == 3 else total_rows + total_rows // 2
        behind = next_size - total_rows // 2
        before = [0, 2 * total_rows, 3 * total_rows, 3 * total_rows][kind]
        mine = [
            state["shards"],
            (state["sent"][kind], 0),
            (by_x[kind], 0),
            (by_y[kind], 0),
            (by_x[kind + 1], behind),
            (by_y[kind + 1], behind),
        ]
        last = last_pair or (came[kind + 2], came[kind + 2])
        siblings = [
            state["other_shards"],
            (came[kind], before),
            (came[kind + 1], 0),
            (came[kind + 1], size),
            (last[0], behind),
            (last[1], behind if last_pair else next_size + behind),
        ]
        return mine, siblings

    def of_rep(values):
        return lax.dynamic_index_in_dim(values, my_rep, 0, keepdims=False)

    def in_quarters(matrix):
        return matrix.reshape(rows, shards, reps, sub).transpose(2, 0, 1, 3).reshape(
            reps, rows, shards * sub
        )

    def in_shard(pieces):
        cut = jnp.stack(pieces).reshape(reps, rows, shards, sub)
        return cut.transpose(1, 2, 0, 3).reshape(rows, hidden_width)

    def prepare():
        matrices = [self_weights, cross_weights, fc_in, fc_out]
        moments = [self_moment, cross_moment, fc_in_moment, fc_out_moment]
        if sub % 128 == 0:
            return prepared(place_now, matrices, moments, shards, sub, [])
        whole = jnp.stack(
            [
                self_weights.astype(jnp.bfloat16),
                cross_weights.astype(jnp.bfloat16),
                in_quarters(fc_in.astype(jnp.bfloat16)),
                fc_out.reshape(reps, sub, width).astype(jnp.bfloat16),
            ]
        )
        wide_old = [of_rep(in_quarters(fc_in_moment)), of_rep(moments[3].reshape(reps, sub, width))]
        square_old = [of_rep(self_moment), of_rep(cross_moment)]
        quarters = [of_rep(whole[kind]) for kind in range(1, 4)]
        return whole, quarters, jnp.stack(wide_old), jnp.stack(square_old)

    state = {"by_x": [], "by_y": [], "came": [], "sent": []}
    state["arrived"] = first_blocks(of_rep(self_weights).astype(jnp.bfloat16))
    state["shards"], state["quarters"], wide_moments, square_moments = prepare()
    state["other_shards"] = swap(state["shards"])
    run_phase(state, 0, [state["shards"]])
    run_phase(state, 1, [state["other_shards"]])
    run_phase(state, 2, [])
    self_full = placed_blocks(place_now, shares_of(state, 0), 0, chips, [])

    def first_sums(kinds, others, *waited):
        received = [swap(other) for other in others]
        to_x, to_y, kept, later = weight_rows(place_now, kinds, received, waited)
        return kept, later, from_rep(to_x, 1), from_rep(to_y, 2)

    def second_sums(stage, *waited):
        kept, later, by_x, by_y = stage
        to_y, to_x = later_sums(later, by_x, by_y, waited)
        return (kept, by_x, by_y, from_rep(to_x, 1), from_rep(to_y, 2)), to_x

    def third_sums(stage, *waited):
        blocks = sorted_blocks(place_now, *stage, chips, waited)
        arrived = [from_chip(blocks[chips - turn], turn) for turn in range(1, chips)]
        return blocks[0], arrived

    def share_pair(pair, *waited):
        by_x, by_y = from_rep(pair, 1), from_rep(pair, 2)
        across = jnp.stack([from_rep(by_y[0], 1), from_rep(by_x[1], 2)])
        return [pair, by_x, by_y, across]

    def to_replicas(steps):
        return by_rep([step[0] for step in steps]), by_rep([step[1] for step in steps])

    source = tokens[0].astype(jnp.float32)
    encoded = states[0]
    gain_rows = norm_params[0]
    bias_rows = norm_params[1]
    first, first_unit, first_inv = normalize_parts(source, gain_rows[0], bias_rows[0])
    first_low = first.astype(jnp.bfloat16)
    query_rows = matmul(first_low, self_full[0]).astype(jnp.bfloat16)
    incoming_keys = matmul(first_low, self_full[1]).astype(jnp.bfloat16)
    incoming_values = matmul(first_low, self_full[2]).astype(jnp.bfloat16)
    run_phase(state, 3, [query_rows, incoming_keys, incoming_values])
    cross_full = placed_blocks(place_now, shares_of(state, 1), 1, chips, [])
    attended_values = attend_forward(query_rows, incoming_keys, incoming_values, dec_len, True)
    after_self = source + matmul(attended_values, self_full[3])
    second, second_unit, second_inv = normalize_parts(after_self, gain_rows[1], bias_rows[1])
    second_low = second.astype(jnp.bfloat16)
    cross_keys = matmul(encoded, cross_full[1]).astype(jnp.bfloat16)
    cross_values = matmul(encoded, cross_full[2]).astype(jnp.bfloat16)
    run_phase(state, 4, [cross_keys, cross_values, after_self])
    hidden_shares = [
        shares_of(state, 2),
        shares_of(state, 3, (swap(state["by_x"][-1]), swap(state["by_y"][-1]))),
    ]
    cross_query = matmul(second_low, cross_full[0]).astype(jnp.bfloat16)
    cross_mixed = attend_forward(cross_query, cross_keys, cross_values, enc_len, False)
    after_cross = after_self + matmul(cross_mixed, cross_full[3])
    third, third_unit, third_inv = normalize_parts(after_cross, gain_rows[2], bias_rows[2])
    third_low = third.astype(jnp.bfloat16)
    grad_out = cotangent[0].astype(jnp.float32)
    grad_branch = cotangent[0]
    block_out, grad_third, hidden, grad_pre = feed_forward(
        place_now, *hidden_shares, chips, third_low, after_cross, grad_branch
    )
    wide_kinds = [
        ([third_low] * reps, grad_pre, rows, False),
        (hidden, [grad_branch] * reps, sub, False),
    ]
    wide_other = weight_rows(place_now, wide_kinds)
    wide_stage = first_sums(wide_kinds, wide_other)
    grad_norm, third_gain, third_bias = normalize_back(
        grad_third, third_unit, third_inv, gain_rows[2]
    )
    grad_cross = grad_out + grad_norm
    cross_branch = grad_cross.astype(jnp.bfloat16)
    grad_mixed = matmul_right_t(cross_branch, cross_full[3]).astype(jnp.bfloat16)
    grad_cq, grad_ck, grad_cv = attend_backward(
        cross_query, cross_keys, cross_values, enc_len, False, grad_mixed, wide_stage[0]
    )
    cross_kind = (
        [second_low, encoded, encoded, cross_mixed],
        [grad_cq, grad_ck, grad_cv, cross_branch],
        rows,
        True,
    )
    cross_other = weight_rows(place_now, [cross_kind])[0]
    grad_self, self_branch, grad_mixed, second_gain, second_bias = branch_back(
        grad_cq,
        cross_full[0],
        after_self,
        gain_rows[1:2],
        grad_cross,
        self_full[3],
        cross_other,
    )
    second_gain, second_bias = second_gain[0], second_bias[0]
    grad_sq, grad_sk, grad_sv = attend_backward(
        query_rows, incoming_keys, incoming_values, dec_len, True, grad_mixed
    )
    self_kind = (
        [first_low, first_low, first_low, attended_values],
        [grad_sq, grad_sk, grad_sv, self_branch],
        rows,
        True,
    )
    wide_stage, wide_token = second_sums(wide_stage, grad_sq)
    cross_stage = first_sums([cross_kind], [cross_other], wide_token)
    self_other = weight_rows(place_now, [self_kind], None, [cross_stage[0]])[0]
    wide_stage = third_sums(wide_stage, self_other)
    cross_stage, cross_token = second_sums(cross_stage, wide_stage[0])
    self_stage = first_sums([self_kind], [self_other], cross_token)
    cross_stage = third_sums(cross_stage, self_stage[0])
    self_stage, self_token = second_sums(self_stage, cross_stage[0])
    wide_fresh = fresh_blocks(place_now, *wide_stage, wide_moments, self_token)
    wide_grads = wide_fresh[0]
    self_stage = third_sums(self_stage, wide_grads)

    def owned(grads_fresh):
        mine, *sent = grads_fresh[1:]
        arrived = [from_chip(sent[turn - 1], turn) for turn in range(1, chips)]
        mine = jnp.concatenate([mine, *arrived])
        return mine, swap(mine)

    def to_both(result):
        other = from_chip(result[1], chips // 2)
        return jnp.stack(
            [jnp.where(is_lower, result[0], other), jnp.where(is_lower, other, result[0])]
        )

    wide_own = owned(wide_fresh)
    to_x, to_y, kept, later = gram_parts(
        place_now, *wide_own, reps, self_stage[0]
    )
    gram_stage, gram_token = second_sums((kept, later, from_rep(to_x, 1), from_rep(to_y, 2)))
    kept, by_x, by_y, last_x, last_y = gram_stage
    quarter = jnp.concatenate(
        [add_low(kept[0, 0], by_x[0, 0], last_y[0]), add_low(kept[0, 1], by_y[0, 0], last_x[0])]
    )
    quarter_x, quarter_y = from_rep(quarter, 1), from_rep(quarter, 2)
    part = quarter.shape[0] // 2
    quarters = [
        quarter,
        quarter_x,
        quarter_y,
        from_rep(quarter_y[:part], 1),
        from_rep(quarter_x[part:], 2),
    ]
    square_fresh = fresh_blocks(
        place_now,
        jnp.concatenate([self_stage[0], cross_stage[0]]),
        [jnp.concatenate(pair) for pair in zip(self_stage[1], cross_stage[1])],
        square_moments,
    )
    square_grads = square_fresh[0]
    square_own = owned(square_fresh)
    wide_grads_shared = share_pair(wide_grads)
    square_grads_shared = share_pair(square_grads)
    wide_rows = gram_schulz(
        place_now, quarters, *wide_own, rows, wide_grads_shared[1]
    )
    wide_orth_shared = share_pair(to_both(wide_rows))
    square_rows = square_schulz(
        *square_own, rows, wide_rows, square_grads_shared[1], wide_grads_shared[3]
    )
    square_orth = held_until(
        to_both(square_rows), wide_orth_shared[3], square_grads_shared[3]
    )
    square_orth_shared = share_pair(square_orth)
    late_sq = held_until(grad_sq, gram_token)
    late_ck = held_until(grad_ck, gram_token)
    grad_states = matmul_right_t(late_ck, cross_full[1]) + matmul_right_t(grad_cv, cross_full[2])
    grad_first = (
        matmul_right_t(late_sq, self_full[0])
        + matmul_right_t(grad_sk, self_full[1])
        + matmul_right_t(grad_sv, self_full[2])
    )
    grad_norm, first_gain, first_bias = normalize_back(
        grad_first, first_unit, first_inv, gain_rows[0]
    )
    grad_tokens = grad_self + grad_norm
    norm_local = jnp.stack(
        [
            jnp.stack([first_gain, second_gain, third_gain]),
            jnp.stack([first_bias, second_bias, third_bias]),
        ]
    )
    norm_local = held_until(norm_local, quarters[-1])
    norm_total = norm_local + swap(norm_local)
    norm_total = norm_total + from_rep(norm_total, 1)
    norm_total = norm_total + from_rep(norm_total, 2)
    norm_total = sum([from_chip(norm_total, turn) for turn in range(1, chips)], norm_total)
    width_part = norm_moment.shape[2]
    norm_grad = lax.dynamic_slice_in_dim(norm_total, my_place * width_part, width_part, 2)

    wide_grads_shared[0] = held_until(wide_grads_shared[0], wide_rows)
    in_shared, out_shared = to_replicas(wide_grads_shared)
    self_shared, cross_shared = to_replicas(square_grads_shared)
    in_orth_shared, out_orth_shared = to_replicas(wide_orth_shared)
    self_orth_shared, cross_orth_shared = to_replicas(square_orth_shared)

    def stacked(pieces):
        return jnp.stack(pieces).astype(jnp.float32)

    def lengthwise(pieces):
        return jnp.concatenate(pieces).astype(jnp.float32)

    self_grad = stacked(self_shared)
    cross_grad = stacked(cross_shared)
    fc_in_grad = in_shard(in_shared).astype(jnp.float32)
    fc_out_grad = lengthwise(out_shared)
    self_orth = stacked(self_orth_shared)
    cross_orth = stacked(cross_orth_shared)
    in_orth = in_shard(in_orth_shared).astype(jnp.float32)
    out_orth = lengthwise(out_orth_shared)

    self_fresh = MOMENTUM_DECAY * self_moment + self_grad
    cross_fresh = MOMENTUM_DECAY * cross_moment + cross_grad
    in_fresh = MOMENTUM_DECAY * fc_in_moment + fc_in_grad
    out_fresh = MOMENTUM_DECAY * fc_out_moment + fc_out_grad
    norm_fresh = MOMENTUM_DECAY * norm_moment + norm_grad
    self_new = self_weights - MATRIX_RATE * stretch((width, width)) * self_orth
    cross_new = cross_weights - MATRIX_RATE * stretch((width, width)) * cross_orth
    in_new = fc_in - MATRIX_RATE * stretch((width, hidden_width)) * in_orth
    out_new = fc_out - MATRIX_RATE * stretch((hidden_width, width)) * out_orth
    own_params = lax.dynamic_slice_in_dim(norm_params, my_place * width_part, width_part, 2)
    total_tokens = reps * shards * tokens.shape[0] * tokens.shape[1]
    norm_new = own_params - VECTOR_RATE * norm_fresh / math.sqrt(total_tokens)
    return (
        block_out[None].astype(jnp.bfloat16),
        grad_tokens[None].astype(jnp.bfloat16),
        grad_states[None].astype(jnp.bfloat16),
        self_grad,
        cross_grad,
        fc_in_grad,
        fc_out_grad,
        norm_grad,
        self_fresh,
        cross_fresh,
        in_fresh,
        out_fresh,
        norm_fresh,
        self_new,
        cross_new,
        in_new,
        out_new,
        norm_new,
        self_new.astype(jnp.bfloat16),
        cross_new.astype(jnp.bfloat16),
        in_new.astype(jnp.bfloat16),
        out_new.astype(jnp.bfloat16),
    )


def solution(mesh):
    placed = (
        P(("rep", "shard"), None, None),
        P(("rep", "shard"), None, None),
        P(("rep", "shard"), None, None),
        P(("rep", "shard")),
        P(("rep", "shard")),
        P(None, "shard", None),
        P(None, "shard", None),
        P("shard", None),
        P("shard", None),
        P(),
        P(None, "shard", None),
        P(None, "shard", None),
        P("shard", None),
        P("shard", None),
        P(None, None, "shard"),
    )
    return jax.shard_map(
        on_device,
        mesh=mesh,
        in_specs=placed,
        out_specs=(
            P(("rep", "shard"), None, None),
            P(("rep", "shard"), None, None),
            P(("rep", "shard"), None, None),
            P(None, "shard", None),
            P(None, "shard", None),
            P("shard", None),
            P("shard", None),
            P(None, None, "shard"),
            P(None, "shard", None),
            P(None, "shard", None),
            P("shard", None),
            P("shard", None),
            P(None, None, "shard"),
            P(None, "shard", None),
            P(None, "shard", None),
            P("shard", None),
            P("shard", None),
            P(None, None, "shard"),
            P(None, "shard", None),
            P(None, "shard", None),
            P("shard", None),
            P("shard", None),
        ),
        check_vma=False,
    )
```

```python
import math

import jax
import jax.numpy as jnp
from jax import lax
from jax.experimental import pallas as pl
from jax.experimental.pallas import tpu as pltpu
from jax.sharding import PartitionSpec as P

HEADS = 16
HEAD_DIM = 64
NS_STEPS = 3


NORM_EPSILON = 1e-05
MOMENTUM_DECAY = 0.9
MATRIX_RATE = 0.6
VECTOR_RATE = 0.05
SCHULZ_FIRST = 3.4445
SCHULZ_SECOND = -4.775
SCHULZ_THIRD = 2.0315


def matmul(left, right):
    return jnp.dot(left, right, preferred_element_type=jnp.float32)


def matmul_left_t(left, right):
    return lax.dot_general(
        left, right, (((0,), (0,)), ((), ())), preferred_element_type=jnp.float32
    )


def matmul_right_t(left, right):
    return lax.dot_general(
        left, right, (((1,), (1,)), ((), ())), preferred_element_type=jnp.float32
    )


def normalize_parts(values, gain, bias):
    centered = values - jnp.mean(values, axis=-1, keepdims=True)
    inverse = lax.rsqrt(jnp.mean(centered * centered, axis=-1, keepdims=True) + NORM_EPSILON)
    unit_part = centered * inverse
    return (unit_part * gain + bias, unit_part, inverse)


def normalize_back(grad_out, unit_part, inverse, gain):
    grad_unit = grad_out * gain
    grad_in = inverse * (
        grad_unit
        - jnp.mean(grad_unit, axis=-1, keepdims=True)
        - unit_part * jnp.mean(grad_unit * unit_part, axis=-1, keepdims=True)
    )
    return (grad_in, jnp.sum(grad_out * unit_part, axis=0), jnp.sum(grad_out, axis=0))


PAIR = 2 * HEAD_DIM
SMALL = pl.CostEstimate(flops=1024, bytes_accessed=1024, transcendentals=0)


def attention_parts(count_ref, causal, query_part, keys, is_first):
    lane = lax.broadcasted_iota(jnp.int32, (1, PAIR), 1)
    own = (lane < HEAD_DIM) == is_first
    scores = matmul_right_t(jnp.where(own, query_part, 0), keys) * HEAD_DIM ** (-0.5)
    key_place = lax.broadcasted_iota(jnp.int32, scores.shape, 1)
    valid = key_place < count_ref[0]
    if causal:
        valid = valid & (key_place <= lax.broadcasted_iota(jnp.int32, scores.shape, 0))
    scores = jnp.where(valid, scores, -jnp.inf)
    exponent = jnp.exp(scores - jnp.max(scores, axis=-1, keepdims=True))
    return exponent / jnp.sum(exponent, axis=-1, keepdims=True), own


def head_pairs(width, body):
    def step(index, carry):
        body(pl.ds(pl.multiple_of(index * PAIR, PAIR), PAIR))
        return carry

    lax.fori_loop(0, width // PAIR, step, 0)


def attention_call(kernel, out_shapes, count, arrays, waited):
    rows, width = arrays[0].shape
    keys = arrays[1].shape[0]
    vmem = pl.BlockSpec(memory_space=pltpu.VMEM)
    return pl.pallas_call(
        kernel,
        out_shape=tuple(out_shapes),
        in_specs=[pl.BlockSpec(memory_space=pltpu.SMEM)]
        + [vmem] * len(arrays)
        + [pl.BlockSpec(memory_space=pl.ANY)] * len(waited),
        out_specs=tuple([vmem] * len(out_shapes)),
        compiler_params=pltpu.CompilerParams(vmem_limit_bytes=56 * 2**20),
        cost_estimate=SMALL,
    )(count, *arrays, *waited)


def attend_forward(query_rows, incoming_keys, incoming_values, count, causal, *waited):
    def kernel(count_ref, query_ref, key_ref, value_ref, *refs):
        mixed_ref = refs[-1]

        def one_pair(columns):
            query_part, keys = query_ref[:, columns], key_ref[:, columns]
            values = value_ref[:, columns]
            mixed = None
            for is_first in (True, False):
                weights, own = attention_parts(count_ref, causal, query_part, keys, is_first)
                here = matmul(weights.astype(jnp.bfloat16), values)
                mixed = here if mixed is None else jnp.where(own, here, mixed)
            mixed_ref[:, columns] = mixed.astype(jnp.bfloat16)

        head_pairs(query_ref.shape[1], one_pair)

    return attention_call(
        kernel,
        [low(*query_rows.shape)],
        count,
        [query_rows, incoming_keys, incoming_values],
        waited,
    )[0]


def attend_backward(
    query_rows, incoming_keys, incoming_values, count, causal, grad_mixed, *waited
):
    def kernel(count_ref, query_ref, key_ref, value_ref, grad_ref, *refs):
        grad_query, grad_keys, grad_values = refs[-3:]
        scale = HEAD_DIM ** (-0.5)

        def one_pair(columns):
            query_part, keys = query_ref[:, columns], key_ref[:, columns]
            values, grads = value_ref[:, columns], grad_ref[:, columns]
            found = None
            for is_first in (True, False):
                weights, own = attention_parts(count_ref, causal, query_part, keys, is_first)
                grad_prob = matmul_right_t(jnp.where(own, grads, 0), values)
                shift = jnp.sum(grad_prob * weights, axis=-1, keepdims=True)
                score_grad = (weights * (grad_prob - shift)).astype(jnp.bfloat16)
                here = (
                    matmul(score_grad, keys) * scale,
                    matmul_left_t(score_grad, query_part) * scale,
                    matmul_left_t(weights.astype(jnp.bfloat16), grads),
                )
                if found is None:
                    found = here
                else:
                    found = [jnp.where(own, new, old) for new, old in zip(here, found)]
            for ref, value in zip((grad_query, grad_keys, grad_values), found):
                ref[:, columns] = value.astype(jnp.bfloat16)

        head_pairs(query_ref.shape[1], one_pair)

    return attention_call(
        kernel,
        [low(*query_rows.shape), low(*incoming_keys.shape), low(*incoming_keys.shape)],
        count,
        [query_rows, incoming_keys, incoming_values, grad_mixed],
        waited,
    )


TILE = 256


def in_tiles(size, body):
    def step(index, carry):
        body(pl.ds(pl.multiple_of(index * TILE, TILE), TILE))
        return carry

    lax.fori_loop(0, size // TILE, step, 0)


def wide_view(ref, rows):
    return ref[rows, :].astype(jnp.float32)


def first_and_opposite(rows, total):
    return slice(0, rows), slice(total // 2, total // 2 + rows)


def square_schulz(mine, sibling, rows, *waited):
    size = mine.shape[1]
    half = mine.shape[0]

    def kernel(mine_ref, sibling_ref, *refs):
        result, current, gram, poly, total = refs[len(waited) :]
        current[:half], current[half:] = mine_ref[...], sibling_ref[...]
        total[...] = jnp.zeros_like(total)

        def add_squares(rows):
            part = wide_view(current, rows)
            total[...] += jnp.sum(part * part, axis=0, keepdims=True)

        in_tiles(size, add_squares)
        scale = 1.0 / (jnp.sqrt(jnp.sum(total[...])) + 1e-07)

        def scaled(rows):
            current[rows, :] = (wide_view(current, rows) * scale).astype(jnp.bfloat16)

        in_tiles(size, scaled)
        for sweep_index in range(NS_STEPS):

            def gram_rows(rows):
                gram[rows, :] = matmul_right_t(current[rows, :], current[...]).astype(
                    jnp.bfloat16
                )

            def poly_rows(rows):
                poly[rows, :] = (
                    SCHULZ_SECOND * wide_view(gram, rows)
                    + SCHULZ_THIRD * matmul(gram[rows, :], gram[...])
                ).astype(jnp.bfloat16)

            def next_rows(rows):
                gram[rows, :] = (
                    SCHULZ_FIRST * wide_view(current, rows) + matmul(poly[rows, :], current[...])
                ).astype(jnp.bfloat16)

            in_tiles(size, gram_rows)
            if sweep_index == NS_STEPS - 1:
                for block, here in enumerate(first_and_opposite(rows, half)):
                    poly_rows(here)
                    result[block] = (
                        SCHULZ_FIRST * wide_view(current, here)
                        + matmul(poly[here, :], current[...])
                    ).astype(jnp.bfloat16)
            else:
                in_tiles(size, poly_rows)
                in_tiles(size, next_rows)
                current[...] = gram[...]

    vmem = pl.BlockSpec(memory_space=pltpu.VMEM)
    return pl.pallas_call(
        kernel,
        out_shape=low(2, rows, size),
        in_specs=[vmem] * 2 + [pl.BlockSpec(memory_space=pl.ANY)] * len(waited),
        out_specs=vmem,
        scratch_shapes=[pltpu.VMEM((size, size), jnp.bfloat16)] * 3
        + [pltpu.VMEM((1, size), jnp.float32)],
        compiler_params=pltpu.CompilerParams(vmem_limit_bytes=56 * 2**20),
        cost_estimate=SMALL,
    )(mine, sibling, *waited)


def gram_parts(place, mine, sibling, reps, *waited):
    size = mine.shape[1]
    half = mine.shape[0]
    part = size // (2 * reps)

    def kernel(place_ref, mine_ref, sibling_ref, *refs):
        to_x, to_y, kept, later, both, gram = refs[len(waited) :]
        both[:half], both[half:] = mine_ref[...], sibling_ref[...]
        is_lower = place_ref[3] == 1

        def row_products(rows):
            gram[rows, :] = matmul_right_t(both[rows, :], both[...]).astype(jnp.bfloat16)

        def column_products(columns):
            gram[columns, :] = matmul_left_t(both[:, columns], both[...]).astype(jnp.bfloat16)

        @pl.when(is_lower)
        def _():
            in_tiles(size, row_products)

        @pl.when(jnp.logical_not(is_lower))
        def _():
            in_tiles(size, column_products)

        def piece(step, index):
            first_row = (place_ref[0] ^ step) * (2 * part) + index * part
            return gram[pl.ds(pl.multiple_of(first_row, part), part), :]

        to_x[0, 0], to_x[0, 1] = piece(1, 0), piece(3, 0)
        to_y[0, 0], to_y[0, 1] = piece(2, 1), piece(3, 1)
        kept[0, 0], kept[0, 1] = piece(0, 0), piece(0, 1)
        later[0, 0], later[0, 1] = piece(2, 0), piece(1, 1)

    vmem = pl.BlockSpec(memory_space=pltpu.VMEM)
    return pl.pallas_call(
        kernel,
        out_shape=tuple([low(1, 2, part, size)] * 4),
        in_specs=[pl.BlockSpec(memory_space=pltpu.SMEM)]
        + [vmem] * 2
        + [pl.BlockSpec(memory_space=pl.ANY)] * len(waited),
        out_specs=tuple([vmem] * 4),
        scratch_shapes=[pltpu.VMEM((size, size), jnp.bfloat16)] * 2,
        compiler_params=pltpu.CompilerParams(vmem_limit_bytes=56 * 2**20),
        cost_estimate=SMALL,
    )(place, mine, sibling, *waited)


def gram_schulz(place, quarters, mine, sibling, rows, *waited):
    size = mine.shape[1]
    half_rows = mine.shape[0]
    part = quarters[0].shape[0]

    def kernel(place_ref, q_ref, x_ref, y_ref, a_ref, b_ref, mine_ref, sibling_ref, *refs):
        result, gram, product, current, poly, half, unit = refs[len(waited) :]
        my_rep = place_ref[0]

        def put(step, offset, ref):
            first_row = (my_rep ^ step) * part + offset
            size_here = ref.shape[0]
            gram[pl.ds(pl.multiple_of(first_row, size_here), size_here), :] = ref[...]

        put(0, 0, q_ref)
        put(1, 0, x_ref)
        put(2, 0, y_ref)
        put(3, 0, a_ref)
        put(3, part // 2, b_ref)

        def trace_of(index, total):
            rows = pl.ds(pl.multiple_of(index * TILE, TILE), TILE)
            here = wide_view(gram, rows)
            row_number = lax.broadcasted_iota(jnp.int32, here.shape, 0) + index * TILE
            column_number = lax.broadcasted_iota(jnp.int32, here.shape, 1)
            return total + jnp.sum(jnp.where(row_number == column_number, here, 0.0))

        trace = lax.fori_loop(0, size // TILE, trace_of, jnp.float32(0.0))
        scale = (1.0 / (jnp.sqrt(jnp.full((8, 128), trace)) + 1e-07))[0:1, 0:1]
        unit[:half_rows] = (mine_ref[...].astype(jnp.float32) * scale).astype(jnp.bfloat16)
        unit[half_rows:] = (sibling_ref[...].astype(jnp.float32) * scale).astype(jnp.bfloat16)

        def scaled(rows):
            current[rows, :] = (wide_view(gram, rows) * (scale * scale)).astype(jnp.bfloat16)

        in_tiles(size, scaled)
        factor = 1.0
        for sweep_index in range(NS_STEPS):

            def poly_rows(rows):
                poly[rows, :] = (
                    SCHULZ_SECOND * wide_view(current, rows)
                    + SCHULZ_THIRD * matmul(current[rows, :], current[...])
                ).astype(jnp.bfloat16)

            def product_rows(rows):
                half[rows, :] = (
                    SCHULZ_FIRST * wide_view(product, rows)
                    + factor * wide_view(poly, rows)
                    + matmul(poly[rows, :], product[...])
                ).astype(jnp.bfloat16)

            def half_rows_of(rows):
                half[rows, :] = (
                    SCHULZ_FIRST * wide_view(current, rows) + matmul(poly[rows, :], current[...])
                ).astype(jnp.bfloat16)

            def current_rows(rows):
                current[rows, :] = (
                    SCHULZ_FIRST * wide_view(half, rows) + matmul(half[rows, :], poly[...])
                ).astype(jnp.bfloat16)

            in_tiles(size, poly_rows)
            if sweep_index == 0:
                product[...] = poly[...]
            else:
                in_tiles(size, product_rows)
                product[...] = half[...]
            factor = factor * SCHULZ_FIRST
            if sweep_index < NS_STEPS - 1:
                in_tiles(size, half_rows_of)
                in_tiles(size, current_rows)

        is_lower = place_ref[3] == 1
        for block, here in enumerate(first_and_opposite(rows, half_rows)):
            plain = factor * wide_view(unit, here)

            @pl.when(is_lower)
            def _():
                turned = matmul(product[here, :], unit[...])
                result[block] = (plain + turned).astype(jnp.bfloat16)

            @pl.when(jnp.logical_not(is_lower))
            def _():
                turned = matmul(unit[here, :], product[...])
                result[block] = (plain + turned).astype(jnp.bfloat16)

    vmem = pl.BlockSpec(memory_space=pltpu.VMEM)
    return pl.pallas_call(
        kernel,
        out_shape=low(2, rows, size),
        in_specs=[pl.BlockSpec(memory_space=pltpu.SMEM)]
        + [vmem] * 7
        + [pl.BlockSpec(memory_space=pl.ANY)] * len(waited),
        out_specs=vmem,
        scratch_shapes=[pltpu.VMEM((size, size), jnp.bfloat16)] * 6,
        compiler_params=pltpu.CompilerParams(vmem_limit_bytes=56 * 2**20),
        cost_estimate=SMALL,
    )(place, *quarters, mine, sibling, *waited)


def low(*shape):
    return jax.ShapeDtypeStruct(shape, jnp.bfloat16)


def fresh_blocks(place, own, arrived, moments, *waited):
    kinds, rows, width = own.shape
    chips = len(arrived) + 1

    def kernel(place_ref, own_ref, *refs):
        arrived_refs = refs[: chips - 1]
        moment_ref = refs[chips - 1]
        grad_ref, *out = refs[chips + len(waited) : -1]
        fresh_ref = refs[-1]
        for kind in range(kinds):
            grad_ref[kind] = add_low(own_ref[kind], *[ref[kind] for ref in arrived_refs])
            fresh_ref[kind] = (
                MOMENTUM_DECAY * moment_ref[kind] + grad_ref[kind].astype(jnp.float32)
            ).astype(jnp.bfloat16)
        for turn in range(chips):
            chip = lax.rem(place_ref[1] + chips - turn, chips)
            out[turn][...] = fresh_ref[jnp.where(chip < chips // 2, 0, 1)]

    vmem = pl.BlockSpec(memory_space=pltpu.VMEM)
    return pl.pallas_call(
        kernel,
        out_shape=tuple([low(kinds, rows, width)] + [low(rows, width)] * chips),
        in_specs=[pl.BlockSpec(memory_space=pltpu.SMEM)]
        + [vmem] * (chips + 1)
        + [pl.BlockSpec(memory_space=pl.ANY)] * len(waited),
        out_specs=tuple([vmem] * (chips + 1)),
        scratch_shapes=[pltpu.VMEM((kinds, rows, width), jnp.bfloat16)],
        compiler_params=pltpu.CompilerParams(vmem_limit_bytes=56 * 2**20),
        cost_estimate=SMALL,
    )(place, own, *arrived, moments, *waited)


def first_seen(arrays):
    kept, index = [], []
    for array in arrays:
        found = [place for place, other in enumerate(kept) if other is array]
        if not found:
            kept.append(array)
        index.append(found[0] if found else len(kept) - 1)
    return kept, index


def weight_rows(place, kinds, received=None, waited=()):
    count = len(kinds)
    steps = len(kinds[0][0])
    rows, width = kinds[0][0][0].shape[1] // 2, kinds[0][1][0].shape[1]
    half = rows // 2
    is_own = received is not None
    aligned = all(kind[2] % 128 == 0 for kind in kinds)
    lefts, left_index = first_seen([left for kind in kinds for left in kind[0]])
    rights, right_index = first_seen([right for kind in kinds for right in kind[1]])
    core_rows = [
        kinds[left_index.index(index) // steps][2] for index in range(len(lefts))
    ]
    if not aligned:
        def chosen(left, size):
            cut = left.reshape(left.shape[0], -1, 2, size)
            first_core = (place[2] == 0) if is_own else (place[2] == 1)
            return jnp.where(first_core, cut[:, :, 0], cut[:, :, 1]).reshape(left.shape[0], rows)

        lefts = [chosen(left, size) for left, size in zip(lefts, core_rows)]
    arrays = lefts + rights + (list(received) if is_own else [])

    def kernel(place_ref, *refs):
        left_refs = refs[: len(lefts)]
        right_refs = refs[len(lefts) : len(lefts) + len(rights)]
        received_refs = refs[len(lefts) + len(rights) : len(arrays)]
        rest = refs[len(arrays) + len(waited) :]
        core = place_ref[2] if is_own else 1 - place_ref[2]

        def columns(index):
            ref, size = left_refs[index], core_rows[index]
            if not aligned:
                return ref[...]
            parts = [
                ref[:, pl.ds(pl.multiple_of((2 * chip + core) * size, 128), size)]
                for chip in range(rows // size)
            ]
            return jnp.concatenate(parts, axis=1)

        for kind in range(count):
            for block in range(steps):
                spot = kind * steps + block
                total = matmul_left_t(
                    columns(left_index[spot]), right_refs[right_index[spot]][...]
                )
                step = (place_ref[0] ^ block) if kinds[kind][3] else block
                if is_own:
                    total = total + received_refs[kind][step].astype(jnp.float32)
                    rest[4][kind, step] = total.astype(jnp.bfloat16)
                else:
                    rest[kind][step] = total.astype(jnp.bfloat16)
            if is_own:
                to_x, to_y, kept, later, sums = rest
                to_x[kind, 0], to_x[kind, 1] = sums[kind, 1, :half], sums[kind, 3, :half]
                to_y[kind, 0], to_y[kind, 1] = sums[kind, 2, half:], sums[kind, 3, half:]
                kept[kind, 0], kept[kind, 1] = sums[kind, 0, :half], sums[kind, 0, half:]
                later[kind, 0], later[kind, 1] = sums[kind, 2, :half], sums[kind, 1, half:]

    if is_own:
        out_shapes = [low(count, 2, half, width)] * 4
    else:
        out_shapes = [low(steps, rows, width)] * count
    vmem = pl.BlockSpec(memory_space=pltpu.VMEM)
    flops = sum(2 * rows * width * left.shape[0] for kind in kinds for left in kind[0])
    return pl.pallas_call(
        kernel,
        out_shape=tuple(out_shapes),
        in_specs=[pl.BlockSpec(memory_space=pltpu.SMEM)]
        + [vmem] * len(arrays)
        + [pl.BlockSpec(memory_space=pl.ANY)] * len(waited),
        out_specs=tuple([vmem] * len(out_shapes)),
        scratch_shapes=(
            [pltpu.VMEM((count, steps, rows, width), jnp.bfloat16)] if is_own else []
        ),
        compiler_params=pltpu.CompilerParams(vmem_limit_bytes=56 * 2**20),
        cost_estimate=SMALL,
    )(place, *arrays, *waited)


def later_sums(later, by_x, by_y, waited):
    def kernel(later_ref, x_ref, y_ref, *refs):
        to_y, to_x = refs[-2:]
        for kind in range(later_ref.shape[0]):
            to_y[kind] = add_low(later_ref[kind, 0], x_ref[kind, 1])
            to_x[kind] = add_low(later_ref[kind, 1], y_ref[kind, 1])

    vmem = pl.BlockSpec(memory_space=pltpu.VMEM)
    shape = low(later.shape[0], *later.shape[2:])
    return pl.pallas_call(
        kernel,
        out_shape=(shape, shape),
        in_specs=[vmem] * 3 + [pl.BlockSpec(memory_space=pl.ANY)] * len(waited),
        out_specs=(vmem, vmem),
        compiler_params=pltpu.CompilerParams(vmem_limit_bytes=56 * 2**20),
        cost_estimate=SMALL,
    )(later, by_x, by_y, *waited)


def held_until(value, *waited):
    def kernel(*refs):
        del refs

    anywhere = pl.BlockSpec(memory_space=pl.ANY)
    return pl.pallas_call(
        kernel,
        out_shape=jax.ShapeDtypeStruct(value.shape, value.dtype),
        in_specs=[anywhere] * (1 + len(waited)),
        out_specs=anywhere,
        input_output_aliases={0: 0},
        compiler_params=pltpu.CompilerParams(
            vmem_limit_bytes=56 * 2**20, has_side_effects=True
        ),
        cost_estimate=SMALL,
    )(value, *waited)


def sorted_blocks(place, kept, by_x, by_y, last_x, last_y, chips, waited):
    kinds, _, half, width = kept.shape
    rows = 2 * half // chips

    def kernel(place_ref, kept_ref, x_ref, y_ref, last_x_ref, last_y_ref, *refs):
        out, whole = refs[len(waited) : -1], refs[-1]
        for kind in range(kinds):
            whole[: chips // 2] = add_low(
                kept_ref[kind, 0], x_ref[kind, 0], last_y_ref[kind]
            ).reshape(chips // 2, rows, width)
            whole[chips // 2 :] = add_low(
                kept_ref[kind, 1], y_ref[kind, 0], last_x_ref[kind]
            ).reshape(chips // 2, rows, width)
            for turn in range(chips):
                out[turn][kind] = whole[lax.rem(place_ref[1] + turn, chips)]

    vmem = pl.BlockSpec(memory_space=pltpu.VMEM)
    return pl.pallas_call(
        kernel,
        out_shape=tuple([low(kinds, rows, width)] * chips),
        in_specs=[pl.BlockSpec(memory_space=pltpu.SMEM)]
        + [vmem] * 5
        + [pl.BlockSpec(memory_space=pl.ANY)] * len(waited),
        out_specs=tuple([vmem] * chips),
        scratch_shapes=[pltpu.VMEM((chips, rows, width), jnp.bfloat16)],
        compiler_params=pltpu.CompilerParams(vmem_limit_bytes=56 * 2**20),
        cost_estimate=SMALL,
    )(place, kept, by_x, by_y, last_x, last_y, *waited)


def held_until(value, *waited):
    def kernel(*refs):
        del refs

    anywhere = pl.BlockSpec(memory_space=pl.ANY)
    return pl.pallas_call(
        kernel,
        out_shape=jax.ShapeDtypeStruct(value.shape, value.dtype),
        in_specs=[anywhere] * (1 + len(waited)),
        out_specs=anywhere,
        input_output_aliases={0: 0},
        compiler_params=pltpu.CompilerParams(
            vmem_limit_bytes=56 * 2**20, has_side_effects=True
        ),
        cost_estimate=SMALL,
    )(value, *waited)


def stretch(shape):
    return math.sqrt(max(shape[0], shape[1]) / min(shape[0], shape[1]))


def add_low(*terms):
    total = terms[0].astype(jnp.float32)
    for term in terms[1:]:
        total = total + term.astype(jnp.float32)
    return total.astype(jnp.bfloat16)


def phase_blocks(arrived, by_x, by_y, waited):
    given = [*(arrived or []), *([by_x, by_y] if by_x is not None else [])]
    width = given[0].shape[-1]
    if arrived:
        rows, turns = arrived[0].shape[0], len(arrived)
        total = rows * turns
        half = total // 2
    else:
        total, half = 0, by_x.shape[0] // 3
    send = total + (half if by_x is not None else 0)
    came = by_x.shape[0] if by_x is not None else 0
    out_shapes = [low(send, width)] * 2 + [low(2 * came + total, width)]

    def kernel(*refs):
        inputs = list(refs[: len(given)])
        to_x, to_y, to_core = refs[len(given) + len(waited) :]
        if arrived:
            for turn in range(turns):
                here = slice(turn * rows, (turn + 1) * rows)
                block = inputs.pop(0)[...]
                to_x[here] = to_y[here] = block
                first_row = 2 * came + turn * rows
                to_core[first_row : first_row + rows] = block
        if by_x is not None:
            x_ref, y_ref = inputs.pop(0), inputs.pop(0)
            to_x[total:] = y_ref[:half]
            to_y[total:] = x_ref[half : 2 * half]
            to_core[:came], to_core[came : 2 * came] = x_ref[...], y_ref[...]

    vmem = pl.BlockSpec(memory_space=pltpu.VMEM)
    return pl.pallas_call(
        kernel,
        out_shape=tuple(out_shapes),
        in_specs=[vmem] * len(given) + [pl.BlockSpec(memory_space=pl.ANY)] * len(waited),
        out_specs=tuple([vmem] * len(out_shapes)),
        compiler_params=pltpu.CompilerParams(vmem_limit_bytes=56 * 2**20),
        cost_estimate=SMALL,
    )(*given, *waited)


def block_shares(shares):
    flat = [part[0] if isinstance(part, tuple) else part for share in shares for part in share]
    starts = [part[1] for share in shares for part in share[1:]]
    return flat, starts


def start_blocks(place_ref, flat_refs, starts, out, sem_of, kind, chips, by_rep):
    reps, rows = flat_refs[0].shape[1:3]
    turns = chips - 1
    half = turns * rows // 2
    my_rep, my_chip, my_core = place_ref[0], place_ref[1], place_ref[2]
    cuts = []
    for turn in range(turns):
        low_end, high_end = turn * rows, (turn + 1) * rows
        middle = min(max(half, low_end), high_end)
        if middle > low_end:
            cuts.append((0, low_end, turn, 0, middle - low_end))
        if high_end > middle:
            cuts.append((1, middle - half, turn, middle - low_end, high_end - middle))
    copies = [[] for step in range(reps)]

    def start(step, source, target):
        copy = pltpu.make_async_copy(source, target, sem_of(step, len(copies[step])))
        copy.start()
        copies[step].append(copy)

    for step in range(reps):
        from_rep = my_rep ^ step
        to_rep = from_rep if by_rep else step
        for side in range(2):
            core = my_core if side == 0 else 1 - my_core
            own, *moved = flat_refs[6 * side : 6 * side + 6]
            first_rows = starts[5 * side : 5 * side + 5]
            start(step, own.at[kind, from_rep], out.at[to_rep, my_chip, core])
            if step < reps - 1:
                for turn in range(turns):
                    start(
                        step,
                        moved[step].at[pl.ds(first_rows[step] + turn * rows, rows)],
                        out.at[to_rep, lax.rem(my_chip + 1 + turn, chips), core],
                    )
            else:
                for part, source_row, turn, target_row, count in cuts:
                    start(
                        step,
                        moved[3 + part].at[pl.ds(first_rows[3 + part] + source_row, count)],
                        out.at[
                            to_rep,
                            lax.rem(my_chip + 1 + turn, chips),
                            core,
                            pl.ds(target_row, count),
                        ],
                    )
    return copies


def placed_blocks(place, shares, kind, chips, waited):
    reps, rows, width = shares[0][0].shape[1:]
    flat, starts = block_shares(shares)

    def kernel(place_ref, *refs):
        results = refs[len(flat) + len(waited) : -3]
        out, sems, out_sems = refs[-3:]
        copies = start_blocks(
            place_ref,
            refs[: len(flat)],
            starts,
            out,
            lambda step, index: sems.at[step, index],
            kind,
            chips,
            True,
        )
        for step in range(reps):
            for copy in copies[step]:
                copy.wait()
        writes = [
            pltpu.make_async_copy(out.at[step], results[step], out_sems.at[step])
            for step in range(reps)
        ]
        for write in writes:
            write.start()
        for write in writes:
            write.wait()

    shape = (reps, chips, 2, rows, width)
    anywhere = pl.BlockSpec(memory_space=pl.ANY)
    full = pl.pallas_call(
        kernel,
        out_shape=tuple([low(*shape[1:])] * reps),
        in_specs=[pl.BlockSpec(memory_space=pltpu.SMEM)] + [anywhere] * (len(flat) + len(waited)),
        out_specs=tuple([anywhere] * reps),
        scratch_shapes=[
            pltpu.VMEM(shape, jnp.bfloat16),
            pltpu.SemaphoreType.DMA((reps, 2 * chips + 2)),
            pltpu.SemaphoreType.DMA((reps,)),
        ],
        compiler_params=pltpu.CompilerParams(vmem_limit_bytes=56 * 2**20),
        cost_estimate=SMALL,
    )(place, *flat, *waited)
    return [matrix.reshape(-1, width) for matrix in full]


GELU_SCALE = math.sqrt(2.0 / math.pi)
GELU_CUBE = 0.044715


def feed_forward(place, in_shares, out_shares, chips, third_low, residual, grad_branch):
    reps, rows, width = in_shares[0][0].shape[1:]
    in_flat, in_starts = block_shares(in_shares)
    out_flat, out_starts = block_shares(out_shares)
    tokens = third_low.shape[0]

    def kernel(place_ref, third_ref, residual_ref, branch_ref, *refs):
        in_refs = refs[: len(in_flat)]
        out_refs = refs[len(in_flat) : len(in_flat) + len(out_flat)]
        block_out, grad_third, *parts = refs[len(in_flat) + len(out_flat) : -3]
        hidden, grad_pre = parts[:reps], parts[reps:]
        in_full, out_full, sems = refs[-3:]
        in_copies = start_blocks(
            place_ref, in_refs, in_starts, in_full,
            lambda step, index: sems.at[0, step, index], 2, chips, False,
        )
        out_copies = start_blocks(
            place_ref, out_refs, out_starts, out_full,
            lambda step, index: sems.at[1, step, index], 3, chips, False,
        )
        for step in range(reps):
            for copy in in_copies[step]:
                copy.wait()
            in_weights = in_full[step].reshape(-1, width)
            pre = matmul(third_ref[...], in_weights)
            for copy in out_copies[step]:
                copy.wait()
            out_weights = out_full[step].reshape(-1, width)
            grad_hidden = matmul_right_t(branch_ref[...], out_weights)
            square = pre * pre
            bent = jnp.tanh(GELU_SCALE * pre * (1.0 + GELU_CUBE * square))
            units = (0.5 * pre * (1.0 + bent)).astype(jnp.bfloat16)
            slope = 0.5 * (1.0 + bent) + 0.5 * pre * (1.0 - bent * bent) * GELU_SCALE * (
                1.0 + 3.0 * GELU_CUBE * square
            )
            grads = (grad_hidden * slope).astype(jnp.bfloat16)
            hidden[step][...] = units
            grad_pre[step][...] = grads
            to_third = matmul_right_t(grads, in_weights)
            to_out = matmul(units, out_weights)
            if step == 0:
                grad_third[...] = to_third
                block_out[...] = residual_ref[...] + to_out
            else:
                grad_third[...] += to_third
                block_out[...] += to_out

    vmem = pl.BlockSpec(memory_space=pltpu.VMEM)
    whole = jax.ShapeDtypeStruct((tokens, width), jnp.float32)
    shape = (reps, chips, 2, rows, width)
    results = pl.pallas_call(
        kernel,
        out_shape=(whole, whole, *[low(tokens, width)] * (2 * reps)),
        in_specs=[pl.BlockSpec(memory_space=pltpu.SMEM)]
        + [vmem] * 3
        + [pl.BlockSpec(memory_space=pl.ANY)] * (len(in_flat) + len(out_flat)),
        out_specs=(vmem,) * (2 + 2 * reps),
        scratch_shapes=[
            pltpu.VMEM(shape, jnp.bfloat16),
            pltpu.VMEM(shape, jnp.bfloat16),
            pltpu.SemaphoreType.DMA((2, reps, 2 * chips + 2)),
        ],
        compiler_params=pltpu.CompilerParams(vmem_limit_bytes=56 * 2**20),
        cost_estimate=SMALL,
    )(place, third_low, residual, grad_branch, *in_flat, *out_flat)
    block_out, grad_third, *parts = results
    return block_out, grad_third, parts[:reps], parts[reps:]


def prepared(place, matrices, moments, shards, sub, waited):
    reps, rows, width = matrices[0].shape

    def kernel(place_ref, *refs):
        stacks, hidden_in, hidden_out = refs[0:2], refs[2], refs[3]
        old_stacks, old_in, old_out = refs[4:6], refs[6], refs[7]
        whole, *outs = refs[8 + len(waited) :]
        quarters, wide_old, square_old, sems = outs[:3], outs[3], outs[4], outs[5]
        my_rep = place_ref[0]
        copies = []

        def start(source, target):
            copy = pltpu.make_async_copy(source, target, sems.at[len(copies)])
            copy.start()
            copies.append(copy)

        for kind in range(2):
            start(old_stacks[kind].at[my_rep], square_old.at[kind])
        start(old_out.at[pl.ds(pl.multiple_of(my_rep * sub, sub), sub)], wide_old.at[1])
        for shard in range(shards):
            first = pl.multiple_of((shard * reps + my_rep) * sub, sub)
            start(
                old_in.at[:, pl.ds(first, sub)],
                wide_old.at[0, :, pl.ds(shard * sub, sub)],
            )
        for kind in range(2):
            whole[kind] = stacks[kind][...].astype(jnp.bfloat16)
        for step in range(reps):
            for shard in range(shards):
                first = (shard * reps + step) * sub
                whole[2, step, :, shard * sub : (shard + 1) * sub] = hidden_in[
                    :, first : first + sub
                ].astype(jnp.bfloat16)
            whole[3, step] = hidden_out[step * sub : (step + 1) * sub].astype(jnp.bfloat16)
        for kind in range(1, 4):
            quarters[kind - 1][...] = whole[kind, my_rep]
        for copy in copies:
            copy.wait()

    vmem = pl.BlockSpec(memory_space=pltpu.VMEM)
    anywhere = pl.BlockSpec(memory_space=pl.ANY)
    old = jax.ShapeDtypeStruct((2, rows, width), jnp.float32)
    whole, *parts, wide_old, square_old = pl.pallas_call(
        kernel,
        out_shape=(low(4, reps, rows, width), *[low(rows, width)] * 3, old, old),
        in_specs=[pl.BlockSpec(memory_space=pltpu.SMEM)]
        + [vmem] * 4
        + [anywhere] * (4 + len(waited)),
        out_specs=(vmem,) * 6,
        scratch_shapes=[pltpu.SemaphoreType.DMA((shards + 3,))],
        compiler_params=pltpu.CompilerParams(vmem_limit_bytes=56 * 2**20),
        cost_estimate=SMALL,
    )(place, *matrices, *moments, *waited)
    return whole, parts, wide_old, square_old


def branch_back(grad_query, weights, stream, gain, grad_stream, next_weights, *waited):
    rows, width = stream.shape

    def kernel(query_ref, weights_ref, stream_ref, gain_ref, grad_ref, next_ref, *refs):
        total_ref, branch_ref, mixed_ref, gain_grad, bias_grad = refs[len(waited) :]
        grad_out = matmul_right_t(query_ref[...], weights_ref[...])
        values = stream_ref[...]
        centered = values - jnp.mean(values, axis=-1, keepdims=True)
        inverse = lax.rsqrt(jnp.mean(centered * centered, axis=-1, keepdims=True) + NORM_EPSILON)
        unit_part = centered * inverse
        grad_unit = grad_out * gain_ref[...]
        grad_in = inverse * (
            grad_unit
            - jnp.mean(grad_unit, axis=-1, keepdims=True)
            - unit_part * jnp.mean(grad_unit * unit_part, axis=-1, keepdims=True)
        )
        total = grad_ref[...] + grad_in
        branch = total.astype(jnp.bfloat16)
        total_ref[...] = total
        branch_ref[...] = branch
        mixed_ref[...] = matmul_right_t(branch, next_ref[...]).astype(jnp.bfloat16)
        gain_grad[...] = jnp.sum(grad_out * unit_part, axis=0, keepdims=True)
        bias_grad[...] = jnp.sum(grad_out, axis=0, keepdims=True)

    vmem = pl.BlockSpec(memory_space=pltpu.VMEM)
    line = jax.ShapeDtypeStruct((1, width), jnp.float32)
    return pl.pallas_call(
        kernel,
        out_shape=(
            jax.ShapeDtypeStruct((rows, width), jnp.float32),
            low(rows, width),
            low(rows, width),
            line,
            line,
        ),
        in_specs=[vmem] * 6 + [pl.BlockSpec(memory_space=pl.ANY)] * len(waited),
        out_specs=(vmem,) * 5,
        compiler_params=pltpu.CompilerParams(vmem_limit_bytes=56 * 2**20),
        cost_estimate=SMALL,
    )(grad_query, weights, stream, gain, grad_stream, next_weights, *waited)


def on_device(
    tokens,
    states,
    cotangent,
    dec_len,
    enc_len,
    self_weights,
    cross_weights,
    fc_in,
    fc_out,
    norm_params,
    self_moment,
    cross_moment,
    fc_in_moment,
    fc_out_moment,
    norm_moment,
):
    reps = lax.axis_size("rep")
    shards = lax.axis_size("shard")
    chips = shards // 2
    my_rep = lax.axis_index("rep")
    my_place = lax.axis_index("shard")
    my_chip = my_place // 2
    my_core = lax.rem(my_place, 2)
    even = my_core == 0
    width = self_weights.shape[2]
    rows = self_weights.shape[1]
    hidden_width = fc_in.shape[1]
    sub = hidden_width // (shards * reps)

    def swap(values):
        return lax.ppermute(values, "shard", [(index, index ^ 1) for index in range(shards)])

    def from_chip(values, turn):
        pairs = [
            (2 * ((chip + turn) % chips) + core, 2 * chip + core)
            for chip in range(chips)
            for core in range(2)
        ]
        return lax.ppermute(values, "shard", pairs)

    def from_rep(values, step):
        return lax.ppermute(values, "rep", [(index ^ step, index) for index in range(reps)])

    low_bit = (my_rep & 1) == 1
    high_bit = (my_rep & 2) == 2

    def by_rep(steps):
        turned = [jnp.where(low_bit, steps[step ^ 1], steps[step]) for step in range(reps)]
        return [jnp.where(high_bit, turned[step ^ 2], turned[step]) for step in range(reps)]

    is_lower = my_chip < chips // 2
    place_now = jnp.stack([my_rep, my_chip, my_core, is_lower]).astype(jnp.int32)

    def first_blocks(quarter):
        return [from_chip(quarter, turn) for turn in range(1, chips)]

    total_rows = (chips - 1) * rows

    def run_phase(state, phase, waited):
        to_x, to_y, to_core = phase_blocks(
            state["arrived"] if phase < 4 else None,
            state["by_x"][-1] if phase > 0 else None,
            state["by_y"][-1] if phase > 0 else None,
            [*waited, *state["came"][-1:]],
        )
        if phase < 3:
            quarter = held_until(state["quarters"][phase], to_core)
            state["arrived"] = first_blocks(quarter)
        state["sent"].append(to_x)
        state["by_x"].append(from_rep(to_x, 1))
        state["by_y"].append(from_rep(to_y, 2))
        state["came"].append(swap(to_core))

    def shares_of(state, kind, last_pair=None):
        by_x, by_y, came = state["by_x"], state["by_y"], state["came"]
        size = total_rows if kind == 0 else total_rows + total_rows // 2
        next_size = total_rows // 2 if kind == 3 else total_rows + total_rows // 2
        behind = next_size - total_rows // 2
        before = [0, 2 * total_rows, 3 * total_rows, 3 * total_rows][kind]
        mine = [
            state["shards"],
            (state["sent"][kind], 0),
            (by_x[kind], 0),
            (by_y[kind], 0),
            (by_x[kind + 1], behind),
            (by_y[kind + 1], behind),
        ]
        last = last_pair or (came[kind + 2], came[kind + 2])
        siblings = [
            state["other_shards"],
            (came[kind], before),
            (came[kind + 1], 0),
            (came[kind + 1], size),
            (last[0], behind),
            (last[1], behind if last_pair else next_size + behind),
        ]
        return mine, siblings

    def of_rep(values):
        return lax.dynamic_index_in_dim(values, my_rep, 0, keepdims=False)

    def in_quarters(matrix):
        return matrix.reshape(rows, shards, reps, sub).transpose(2, 0, 1, 3).reshape(
            reps, rows, shards * sub
        )

    def in_shard(pieces):
        cut = jnp.stack(pieces).reshape(reps, rows, shards, sub)
        return cut.transpose(1, 2, 0, 3).reshape(rows, hidden_width)

    def prepare():
        matrices = [self_weights, cross_weights, fc_in, fc_out]
        moments = [self_moment, cross_moment, fc_in_moment, fc_out_moment]
        if sub % 128 == 0:
            return prepared(place_now, matrices, moments, shards, sub, [])
        whole = jnp.stack(
            [
                self_weights.astype(jnp.bfloat16),
                cross_weights.astype(jnp.bfloat16),
                in_quarters(fc_in.astype(jnp.bfloat16)),
                fc_out.reshape(reps, sub, width).astype(jnp.bfloat16),
            ]
        )
        wide_old = [of_rep(in_quarters(fc_in_moment)), of_rep(moments[3].reshape(reps, sub, width))]
        square_old = [of_rep(self_moment), of_rep(cross_moment)]
        quarters = [of_rep(whole[kind]) for kind in range(1, 4)]
        return whole, quarters, jnp.stack(wide_old), jnp.stack(square_old)

    state = {"by_x": [], "by_y": [], "came": [], "sent": []}
    state["arrived"] = first_blocks(of_rep(self_weights).astype(jnp.bfloat16))
    state["shards"], state["quarters"], wide_moments, square_moments = prepare()
    state["other_shards"] = swap(state["shards"])
    run_phase(state, 0, [state["shards"]])
    run_phase(state, 1, [])
    run_phase(state, 2, [state["other_shards"]])
    self_full = placed_blocks(place_now, shares_of(state, 0), 0, chips, [])

    def first_sums(kinds, others, *waited):
        received = [swap(other) for other in others]
        to_x, to_y, kept, later = weight_rows(place_now, kinds, received, waited)
        return kept, later, from_rep(to_x, 1), from_rep(to_y, 2)

    def second_sums(stage, *waited):
        kept, later, by_x, by_y = stage
        to_y, to_x = later_sums(later, by_x, by_y, waited)
        return (kept, by_x, by_y, from_rep(to_x, 1), from_rep(to_y, 2)), to_x

    def third_sums(stage, *waited):
        blocks = sorted_blocks(place_now, *stage, chips, waited)
        arrived = [from_chip(blocks[chips - turn], turn) for turn in range(1, chips)]
        return blocks[0], arrived

    def share_pair(pair, *waited):
        by_x, by_y = from_rep(pair, 1), from_rep(pair, 2)
        across = jnp.stack([from_rep(by_y[0], 1), from_rep(by_x[1], 2)])
        return [pair, by_x, by_y, across]

    def to_replicas(steps):
        return by_rep([step[0] for step in steps]), by_rep([step[1] for step in steps])

    source = tokens[0].astype(jnp.float32)
    encoded = states[0]
    gain_rows = norm_params[0]
    bias_rows = norm_params[1]
    first, first_unit, first_inv = normalize_parts(source, gain_rows[0], bias_rows[0])
    first_low = first.astype(jnp.bfloat16)
    query_rows = matmul(first_low, self_full[0]).astype(jnp.bfloat16)
    incoming_keys = matmul(first_low, self_full[1]).astype(jnp.bfloat16)
    incoming_values = matmul(first_low, self_full[2]).astype(jnp.bfloat16)
    run_phase(state, 3, [query_rows, incoming_keys, incoming_values])
    cross_full = placed_blocks(place_now, shares_of(state, 1), 1, chips, [])
    attended_values = attend_forward(query_rows, incoming_keys, incoming_values, dec_len, True)
    after_self = source + matmul(attended_values, self_full[3])
    second, second_unit, second_inv = normalize_parts(after_self, gain_rows[1], bias_rows[1])
    second_low = second.astype(jnp.bfloat16)
    cross_keys = matmul(encoded, cross_full[1]).astype(jnp.bfloat16)
    cross_values = matmul(encoded, cross_full[2]).astype(jnp.bfloat16)
    run_phase(state, 4, [cross_keys, cross_values, after_self])
    hidden_shares = [
        shares_of(state, 2),
        shares_of(state, 3, (swap(state["by_x"][-1]), swap(state["by_y"][-1]))),
    ]
    cross_query = matmul(second_low, cross_full[0]).astype(jnp.bfloat16)
    cross_mixed = attend_forward(cross_query, cross_keys, cross_values, enc_len, False)
    after_cross = after_self + matmul(cross_mixed, cross_full[3])
    third, third_unit, third_inv = normalize_parts(after_cross, gain_rows[2], bias_rows[2])
    third_low = third.astype(jnp.bfloat16)
    grad_out = cotangent[0].astype(jnp.float32)
    grad_branch = cotangent[0]
    block_out, grad_third, hidden, grad_pre = feed_forward(
        place_now, *hidden_shares, chips, third_low, after_cross, grad_branch
    )
    wide_kinds = [
        ([third_low] * reps, grad_pre, rows, False),
        (hidden, [grad_branch] * reps, sub, False),
    ]
    in_other = weight_rows(place_now, wide_kinds[:1])[0]
    out_other = weight_rows(place_now, wide_kinds[1:], None, [in_other])[0]
    grad_norm, third_gain, third_bias = normalize_back(
        grad_third, third_unit, third_inv, gain_rows[2]
    )
    grad_cross = grad_out + grad_norm
    cross_branch = grad_cross.astype(jnp.bfloat16)
    grad_mixed = matmul_right_t(cross_branch, cross_full[3]).astype(jnp.bfloat16)
    grad_cq, grad_ck, grad_cv = attend_backward(
        cross_query, cross_keys, cross_values, enc_len, False, grad_mixed
    )
    wide_stage = first_sums(wide_kinds, [in_other, out_other], grad_cq)
    cross_kind = (
        [second_low, encoded, encoded, cross_mixed],
        [grad_cq, grad_ck, grad_cv, cross_branch],
        rows,
        True,
    )
    cross_other = weight_rows(place_now, [cross_kind], None, [wide_stage[0]])[0]
    grad_self, self_branch, grad_mixed, second_gain, second_bias = branch_back(
        grad_cq,
        cross_full[0],
        after_self,
        gain_rows[1:2],
        grad_cross,
        self_full[3],
        cross_other,
    )
    second_gain, second_bias = second_gain[0], second_bias[0]
    grad_sq, grad_sk, grad_sv = attend_backward(
        query_rows, incoming_keys, incoming_values, dec_len, True, grad_mixed
    )
    self_kind = (
        [first_low, first_low, first_low, attended_values],
        [grad_sq, grad_sk, grad_sv, self_branch],
        rows,
        True,
    )
    wide_stage, wide_token = second_sums(wide_stage, grad_sq)
    cross_stage = first_sums([cross_kind], [cross_other], wide_token)
    self_other = weight_rows(place_now, [self_kind], None, [cross_stage[0]])[0]
    wide_stage = third_sums(wide_stage, self_other)
    cross_stage, cross_token = second_sums(cross_stage, wide_stage[0])
    self_stage = first_sums([self_kind], [self_other], cross_token)
    first_sums_done = self_stage[0]
    cross_stage = third_sums(cross_stage, self_stage[0])
    self_stage, self_token = second_sums(self_stage, cross_stage[0])
    wide_fresh = fresh_blocks(place_now, *wide_stage, wide_moments, self_token)
    wide_grads = wide_fresh[0]
    self_stage = third_sums(self_stage, wide_grads)

    def owned(grads_fresh):
        mine, *sent = grads_fresh[1:]
        arrived = [from_chip(sent[turn - 1], turn) for turn in range(1, chips)]
        mine = jnp.concatenate([mine, *arrived])
        return mine, swap(mine)

    def to_both(result):
        other = from_chip(result[1], chips // 2)
        return jnp.stack(
            [jnp.where(is_lower, result[0], other), jnp.where(is_lower, other, result[0])]
        )

    wide_own = owned(wide_fresh)
    to_x, to_y, kept, later = gram_parts(
        place_now, *wide_own, reps, self_stage[0]
    )
    gram_stage, gram_token = second_sums((kept, later, from_rep(to_x, 1), from_rep(to_y, 2)))
    kept, by_x, by_y, last_x, last_y = gram_stage
    quarter = jnp.concatenate(
        [add_low(kept[0, 0], by_x[0, 0], last_y[0]), add_low(kept[0, 1], by_y[0, 0], last_x[0])]
    )
    quarter_x, quarter_y = from_rep(quarter, 1), from_rep(quarter, 2)
    part = quarter.shape[0] // 2
    quarters = [
        quarter,
        quarter_x,
        quarter_y,
        from_rep(quarter_y[:part], 1),
        from_rep(quarter_x[part:], 2),
    ]
    square_fresh = fresh_blocks(
        place_now,
        jnp.concatenate([self_stage[0], cross_stage[0]]),
        [jnp.concatenate(pair) for pair in zip(self_stage[1], cross_stage[1])],
        square_moments,
        gram_token,
    )
    square_grads = square_fresh[0]
    square_own = owned(square_fresh)
    grads = jnp.concatenate([wide_grads, square_grads])
    grads_x, grads_y = from_rep(grads, 1), from_rep(grads, 2)
    wide_rows = gram_schulz(place_now, quarters, *wide_own, rows, square_grads)
    wide_orth = to_both(wide_rows)
    wide_orth_shared = share_pair(wide_orth)
    square_rows = square_schulz(*square_own, rows, wide_orth, grads_x, grads_y)
    grads_across = [from_rep(grads_y[:2], 1), from_rep(grads_x[2:], 2)]
    square_orth = held_until(
        to_both(square_rows), wide_orth_shared[1], wide_orth_shared[2], *grads_across
    )
    square_orth_shared = share_pair(square_orth)

    late_sq = held_until(grad_sq, first_sums_done)
    late_ck = held_until(grad_ck, first_sums_done)
    grad_states = matmul_right_t(late_ck, cross_full[1]) + matmul_right_t(grad_cv, cross_full[2])
    grad_first = (
        matmul_right_t(late_sq, self_full[0])
        + matmul_right_t(grad_sk, self_full[1])
        + matmul_right_t(grad_sv, self_full[2])
    )
    grad_norm, first_gain, first_bias = normalize_back(
        grad_first, first_unit, first_inv, gain_rows[0]
    )
    grad_tokens = grad_self + grad_norm
    norm_local = jnp.stack(
        [
            jnp.stack([first_gain, second_gain, third_gain]),
            jnp.stack([first_bias, second_bias, third_bias]),
        ]
    )
    norm_local = held_until(norm_local, square_orth)
    norm_total = norm_local + swap(norm_local)
    norm_total = norm_total + from_rep(norm_total, 1)
    norm_total = norm_total + from_rep(norm_total, 2)
    norm_total = sum([from_chip(norm_total, turn) for turn in range(1, chips)], norm_total)
    width_part = norm_moment.shape[2]
    norm_grad = lax.dynamic_slice_in_dim(norm_total, my_place * width_part, width_part, 2)

    late_grads = held_until(grads, square_orth)
    wide_grads_shared = [late_grads[:2], grads_x[:2], grads_y[:2], grads_across[0]]
    square_grads_shared = [late_grads[2:], grads_x[2:], grads_y[2:], grads_across[1]]
    wide_orth_shared[0] = held_until(wide_orth_shared[0], square_orth)
    in_shared, out_shared = to_replicas(wide_grads_shared)
    self_shared, cross_shared = to_replicas(square_grads_shared)
    in_orth_shared, out_orth_shared = to_replicas(wide_orth_shared)
    self_orth_shared, cross_orth_shared = to_replicas(square_orth_shared)

    def stacked(pieces):
        return jnp.stack(pieces).astype(jnp.float32)

    def lengthwise(pieces):
        return jnp.concatenate(pieces).astype(jnp.float32)

    self_grad = stacked(self_shared)
    cross_grad = stacked(cross_shared)
    fc_in_grad = in_shard(in_shared).astype(jnp.float32)
    fc_out_grad = lengthwise(out_shared)
    self_orth = stacked(self_orth_shared)
    cross_orth = stacked(cross_orth_shared)
    in_orth = in_shard(in_orth_shared).astype(jnp.float32)
    out_orth = lengthwise(out_orth_shared)

    self_fresh = MOMENTUM_DECAY * self_moment + self_grad
    cross_fresh = MOMENTUM_DECAY * cross_moment + cross_grad
    in_fresh = MOMENTUM_DECAY * fc_in_moment + fc_in_grad
    out_fresh = MOMENTUM_DECAY * fc_out_moment + fc_out_grad
    norm_fresh = MOMENTUM_DECAY * norm_moment + norm_grad
    self_new = self_weights - MATRIX_RATE * stretch((width, width)) * self_orth
    cross_new = cross_weights - MATRIX_RATE * stretch((width, width)) * cross_orth
    in_new = fc_in - MATRIX_RATE * stretch((width, hidden_width)) * in_orth
    out_new = fc_out - MATRIX_RATE * stretch((hidden_width, width)) * out_orth
    own_params = lax.dynamic_slice_in_dim(norm_params, my_place * width_part, width_part, 2)
    total_tokens = reps * shards * tokens.shape[0] * tokens.shape[1]
    norm_new = own_params - VECTOR_RATE * norm_fresh / math.sqrt(total_tokens)
    return (
        block_out[None].astype(jnp.bfloat16),
        grad_tokens[None].astype(jnp.bfloat16),
        grad_states[None].astype(jnp.bfloat16),
        self_grad,
        cross_grad,
        fc_in_grad,
        fc_out_grad,
        norm_grad,
        self_fresh,
        cross_fresh,
        in_fresh,
        out_fresh,
        norm_fresh,
        self_new,
        cross_new,
        in_new,
        out_new,
        norm_new,
        self_new.astype(jnp.bfloat16),
        cross_new.astype(jnp.bfloat16),
        in_new.astype(jnp.bfloat16),
        out_new.astype(jnp.bfloat16),
    )


def solution(mesh):
    placed = (
        P(("rep", "shard"), None, None),
        P(("rep", "shard"), None, None),
        P(("rep", "shard"), None, None),
        P(("rep", "shard")),
        P(("rep", "shard")),
        P(None, "shard", None),
        P(None, "shard", None),
        P("shard", None),
        P("shard", None),
        P(),
        P(None, "shard", None),
        P(None, "shard", None),
        P("shard", None),
        P("shard", None),
        P(None, None, "shard"),
    )
    return jax.shard_map(
        on_device,
        mesh=mesh,
        in_specs=placed,
        out_specs=(
            P(("rep", "shard"), None, None),
            P(("rep", "shard"), None, None),
            P(("rep", "shard"), None, None),
            P(None, "shard", None),
            P(None, "shard", None),
            P("shard", None),
            P("shard", None),
            P(None, None, "shard"),
            P(None, "shard", None),
            P(None, "shard", None),
            P("shard", None),
            P("shard", None),
            P(None, None, "shard"),
            P(None, "shard", None),
            P(None, "shard", None),
            P("shard", None),
            P("shard", None),
            P(None, None, "shard"),
            P(None, "shard", None),
            P(None, "shard", None),
            P("shard", None),
            P("shard", None),
        ),
        check_vma=False,
    )
```

```python
import math

import jax
import jax.numpy as jnp
from jax import lax
from jax.experimental import pallas as pl
from jax.experimental.pallas import tpu as pltpu
from jax.sharding import PartitionSpec as P

HEADS = 16
HEAD_DIM = 64
NS_STEPS = 3


NORM_EPSILON = 1e-05
MOMENTUM_DECAY = 0.9
MATRIX_RATE = 0.6
VECTOR_RATE = 0.05
SCHULZ_FIRST = 3.4445
SCHULZ_SECOND = -4.775
SCHULZ_THIRD = 2.0315


def matmul(left, right):
    return jnp.dot(left, right, preferred_element_type=jnp.float32)


def matmul_left_t(left, right):
    return lax.dot_general(
        left, right, (((0,), (0,)), ((), ())), preferred_element_type=jnp.float32
    )


def matmul_right_t(left, right):
    return lax.dot_general(
        left, right, (((1,), (1,)), ((), ())), preferred_element_type=jnp.float32
    )


def normalize_parts(values, gain, bias):
    centered = values - jnp.mean(values, axis=-1, keepdims=True)
    inverse = lax.rsqrt(jnp.mean(centered * centered, axis=-1, keepdims=True) + NORM_EPSILON)
    unit_part = centered * inverse
    return (unit_part * gain + bias, unit_part, inverse)


def normalize_back(grad_out, unit_part, inverse, gain):
    grad_unit = grad_out * gain
    grad_in = inverse * (
        grad_unit
        - jnp.mean(grad_unit, axis=-1, keepdims=True)
        - unit_part * jnp.mean(grad_unit * unit_part, axis=-1, keepdims=True)
    )
    return (grad_in, jnp.sum(grad_out * unit_part, axis=0), jnp.sum(grad_out, axis=0))


PAIR = 2 * HEAD_DIM
SMALL = pl.CostEstimate(flops=1024, bytes_accessed=1024, transcendentals=0)


def attention_parts(count_ref, causal, query_part, keys, is_first):
    lane = lax.broadcasted_iota(jnp.int32, (1, PAIR), 1)
    own = (lane < HEAD_DIM) == is_first
    scores = matmul_right_t(jnp.where(own, query_part, 0), keys) * HEAD_DIM ** (-0.5)
    key_place = lax.broadcasted_iota(jnp.int32, scores.shape, 1)
    valid = key_place < count_ref[0]
    if causal:
        valid = valid & (key_place <= lax.broadcasted_iota(jnp.int32, scores.shape, 0))
    scores = jnp.where(valid, scores, -jnp.inf)
    exponent = jnp.exp(scores - jnp.max(scores, axis=-1, keepdims=True))
    return exponent / jnp.sum(exponent, axis=-1, keepdims=True), own


def head_pairs(width, body):
    def step(index, carry):
        body(pl.ds(pl.multiple_of(index * PAIR, PAIR), PAIR))
        return carry

    lax.fori_loop(0, width // PAIR, step, 0)


def attention_call(kernel, out_shapes, count, arrays, waited):
    rows, width = arrays[0].shape
    keys = arrays[1].shape[0]
    vmem = pl.BlockSpec(memory_space=pltpu.VMEM)
    return pl.pallas_call(
        kernel,
        out_shape=tuple(out_shapes),
        in_specs=[pl.BlockSpec(memory_space=pltpu.SMEM)]
        + [vmem] * len(arrays)
        + [pl.BlockSpec(memory_space=pl.ANY)] * len(waited),
        out_specs=tuple([vmem] * len(out_shapes)),
        compiler_params=pltpu.CompilerParams(vmem_limit_bytes=56 * 2**20),
        cost_estimate=SMALL,
    )(count, *arrays, *waited)


def attend_forward(query_rows, incoming_keys, incoming_values, count, causal, *waited):
    def kernel(count_ref, query_ref, key_ref, value_ref, *refs):
        mixed_ref = refs[-1]

        def one_pair(columns):
            query_part, keys = query_ref[:, columns], key_ref[:, columns]
            values = value_ref[:, columns]
            mixed = None
            for is_first in (True, False):
                weights, own = attention_parts(count_ref, causal, query_part, keys, is_first)
                here = matmul(weights.astype(jnp.bfloat16), values)
                mixed = here if mixed is None else jnp.where(own, here, mixed)
            mixed_ref[:, columns] = mixed.astype(jnp.bfloat16)

        head_pairs(query_ref.shape[1], one_pair)

    return attention_call(
        kernel,
        [low(*query_rows.shape)],
        count,
        [query_rows, incoming_keys, incoming_values],
        waited,
    )[0]


def attend_backward(
    query_rows, incoming_keys, incoming_values, count, causal, grad_mixed, *waited
):
    def kernel(count_ref, query_ref, key_ref, value_ref, grad_ref, *refs):
        grad_query, grad_keys, grad_values = refs[-3:]
        scale = HEAD_DIM ** (-0.5)

        def one_pair(columns):
            query_part, keys = query_ref[:, columns], key_ref[:, columns]
            values, grads = value_ref[:, columns], grad_ref[:, columns]
            found = None
            for is_first in (True, False):
                weights, own = attention_parts(count_ref, causal, query_part, keys, is_first)
                grad_prob = matmul_right_t(jnp.where(own, grads, 0), values)
                shift = jnp.sum(grad_prob * weights, axis=-1, keepdims=True)
                score_grad = (weights * (grad_prob - shift)).astype(jnp.bfloat16)
                here = (
                    matmul(score_grad, keys) * scale,
                    matmul_left_t(score_grad, query_part) * scale,
                    matmul_left_t(weights.astype(jnp.bfloat16), grads),
                )
                if found is None:
                    found = here
                else:
                    found = [jnp.where(own, new, old) for new, old in zip(here, found)]
            for ref, value in zip((grad_query, grad_keys, grad_values), found):
                ref[:, columns] = value.astype(jnp.bfloat16)

        head_pairs(query_ref.shape[1], one_pair)

    return attention_call(
        kernel,
        [low(*query_rows.shape), low(*incoming_keys.shape), low(*incoming_keys.shape)],
        count,
        [query_rows, incoming_keys, incoming_values, grad_mixed],
        waited,
    )


TILE = 256


def in_tiles(size, body):
    def step(index, carry):
        body(pl.ds(pl.multiple_of(index * TILE, TILE), TILE))
        return carry

    lax.fori_loop(0, size // TILE, step, 0)


def wide_view(ref, rows):
    return ref[rows, :].astype(jnp.float32)


def first_and_opposite(rows, total):
    return slice(0, rows), slice(total // 2, total // 2 + rows)


def square_schulz(mine, sibling, rows, *waited):
    size = mine.shape[1]
    half = mine.shape[0]

    def kernel(mine_ref, sibling_ref, *refs):
        result, current, gram, poly, total = refs[len(waited) :]
        current[:half], current[half:] = mine_ref[...], sibling_ref[...]
        total[...] = jnp.zeros_like(total)

        def add_squares(rows):
            part = wide_view(current, rows)
            total[...] += jnp.sum(part * part, axis=0, keepdims=True)

        in_tiles(size, add_squares)
        scale = 1.0 / (jnp.sqrt(jnp.sum(total[...])) + 1e-07)

        def scaled(rows):
            current[rows, :] = (wide_view(current, rows) * scale).astype(jnp.bfloat16)

        in_tiles(size, scaled)
        for sweep_index in range(NS_STEPS):

            def gram_rows(rows):
                gram[rows, :] = matmul_right_t(current[rows, :], current[...]).astype(
                    jnp.bfloat16
                )

            def poly_rows(rows):
                poly[rows, :] = (
                    SCHULZ_SECOND * wide_view(gram, rows)
                    + SCHULZ_THIRD * matmul(gram[rows, :], gram[...])
                ).astype(jnp.bfloat16)

            def next_rows(rows):
                gram[rows, :] = (
                    SCHULZ_FIRST * wide_view(current, rows) + matmul(poly[rows, :], current[...])
                ).astype(jnp.bfloat16)

            in_tiles(size, gram_rows)
            if sweep_index == NS_STEPS - 1:
                for block, here in enumerate(first_and_opposite(rows, half)):
                    poly_rows(here)
                    result[block] = (
                        SCHULZ_FIRST * wide_view(current, here)
                        + matmul(poly[here, :], current[...])
                    ).astype(jnp.bfloat16)
            else:
                in_tiles(size, poly_rows)
                in_tiles(size, next_rows)
                current[...] = gram[...]

    vmem = pl.BlockSpec(memory_space=pltpu.VMEM)
    return pl.pallas_call(
        kernel,
        out_shape=low(2, rows, size),
        in_specs=[vmem] * 2 + [pl.BlockSpec(memory_space=pl.ANY)] * len(waited),
        out_specs=vmem,
        scratch_shapes=[pltpu.VMEM((size, size), jnp.bfloat16)] * 3
        + [pltpu.VMEM((1, size), jnp.float32)],
        compiler_params=pltpu.CompilerParams(vmem_limit_bytes=56 * 2**20),
        cost_estimate=SMALL,
    )(mine, sibling, *waited)


def gram_parts(place, mine, sibling, reps, *waited):
    size = mine.shape[1]
    half = mine.shape[0]
    part = size // (2 * reps)

    def kernel(place_ref, mine_ref, sibling_ref, *refs):
        to_x, to_y, kept, later, both, gram = refs[len(waited) :]
        both[:half], both[half:] = mine_ref[...], sibling_ref[...]
        is_lower = place_ref[3] == 1

        def row_products(rows):
            gram[rows, :] = matmul_right_t(both[rows, :], both[...]).astype(jnp.bfloat16)

        def column_products(columns):
            gram[columns, :] = matmul_left_t(both[:, columns], both[...]).astype(jnp.bfloat16)

        @pl.when(is_lower)
        def _():
            in_tiles(size, row_products)

        @pl.when(jnp.logical_not(is_lower))
        def _():
            in_tiles(size, column_products)

        def piece(step, index):
            first_row = (place_ref[0] ^ step) * (2 * part) + index * part
            return gram[pl.ds(pl.multiple_of(first_row, part), part), :]

        to_x[0, 0], to_x[0, 1] = piece(1, 0), piece(3, 0)
        to_y[0, 0], to_y[0, 1] = piece(2, 1), piece(3, 1)
        kept[0, 0], kept[0, 1] = piece(0, 0), piece(0, 1)
        later[0, 0], later[0, 1] = piece(2, 0), piece(1, 1)

    vmem = pl.BlockSpec(memory_space=pltpu.VMEM)
    return pl.pallas_call(
        kernel,
        out_shape=tuple([low(1, 2, part, size)] * 4),
        in_specs=[pl.BlockSpec(memory_space=pltpu.SMEM)]
        + [vmem] * 2
        + [pl.BlockSpec(memory_space=pl.ANY)] * len(waited),
        out_specs=tuple([vmem] * 4),
        scratch_shapes=[pltpu.VMEM((size, size), jnp.bfloat16)] * 2,
        compiler_params=pltpu.CompilerParams(vmem_limit_bytes=56 * 2**20),
        cost_estimate=SMALL,
    )(place, mine, sibling, *waited)


def gram_schulz(place, quarters, mine, sibling, rows, *waited):
    size = mine.shape[1]
    half_rows = mine.shape[0]
    part = quarters[0].shape[0]

    def kernel(place_ref, q_ref, x_ref, y_ref, a_ref, b_ref, mine_ref, sibling_ref, *refs):
        result, gram, product, current, poly, half, unit = refs[len(waited) :]
        my_rep = place_ref[0]

        def put(step, offset, ref):
            first_row = (my_rep ^ step) * part + offset
            size_here = ref.shape[0]
            gram[pl.ds(pl.multiple_of(first_row, size_here), size_here), :] = ref[...]

        put(0, 0, q_ref)
        put(1, 0, x_ref)
        put(2, 0, y_ref)
        put(3, 0, a_ref)
        put(3, part // 2, b_ref)

        def trace_of(index, total):
            rows = pl.ds(pl.multiple_of(index * TILE, TILE), TILE)
            here = wide_view(gram, rows)
            row_number = lax.broadcasted_iota(jnp.int32, here.shape, 0) + index * TILE
            column_number = lax.broadcasted_iota(jnp.int32, here.shape, 1)
            return total + jnp.sum(jnp.where(row_number == column_number, here, 0.0))

        trace = lax.fori_loop(0, size // TILE, trace_of, jnp.float32(0.0))
        scale = (1.0 / (jnp.sqrt(jnp.full((8, 128), trace)) + 1e-07))[0:1, 0:1]
        unit[:half_rows] = (mine_ref[...].astype(jnp.float32) * scale).astype(jnp.bfloat16)
        unit[half_rows:] = (sibling_ref[...].astype(jnp.float32) * scale).astype(jnp.bfloat16)

        def scaled(rows):
            current[rows, :] = (wide_view(gram, rows) * (scale * scale)).astype(jnp.bfloat16)

        in_tiles(size, scaled)
        factor = 1.0
        for sweep_index in range(NS_STEPS):

            def poly_rows(rows):
                poly[rows, :] = (
                    SCHULZ_SECOND * wide_view(current, rows)
                    + SCHULZ_THIRD * matmul(current[rows, :], current[...])
                ).astype(jnp.bfloat16)

            def product_rows(rows):
                half[rows, :] = (
                    SCHULZ_FIRST * wide_view(product, rows)
                    + factor * wide_view(poly, rows)
                    + matmul(poly[rows, :], product[...])
                ).astype(jnp.bfloat16)

            def half_rows_of(rows):
                half[rows, :] = (
                    SCHULZ_FIRST * wide_view(current, rows) + matmul(poly[rows, :], current[...])
                ).astype(jnp.bfloat16)

            def current_rows(rows):
                current[rows, :] = (
                    SCHULZ_FIRST * wide_view(half, rows) + matmul(half[rows, :], poly[...])
                ).astype(jnp.bfloat16)

            in_tiles(size, poly_rows)
            if sweep_index == 0:
                product[...] = poly[...]
            else:
                in_tiles(size, product_rows)
                product[...] = half[...]
            factor = factor * SCHULZ_FIRST
            if sweep_index < NS_STEPS - 1:
                in_tiles(size, half_rows_of)
                in_tiles(size, current_rows)

        is_lower = place_ref[3] == 1
        for block, here in enumerate(first_and_opposite(rows, half_rows)):
            plain = factor * wide_view(unit, here)

            @pl.when(is_lower)
            def _():
                turned = matmul(product[here, :], unit[...])
                result[block] = (plain + turned).astype(jnp.bfloat16)

            @pl.when(jnp.logical_not(is_lower))
            def _():
                turned = matmul(unit[here, :], product[...])
                result[block] = (plain + turned).astype(jnp.bfloat16)

    vmem = pl.BlockSpec(memory_space=pltpu.VMEM)
    return pl.pallas_call(
        kernel,
        out_shape=low(2, rows, size),
        in_specs=[pl.BlockSpec(memory_space=pltpu.SMEM)]
        + [vmem] * 7
        + [pl.BlockSpec(memory_space=pl.ANY)] * len(waited),
        out_specs=vmem,
        scratch_shapes=[pltpu.VMEM((size, size), jnp.bfloat16)] * 6,
        compiler_params=pltpu.CompilerParams(vmem_limit_bytes=56 * 2**20),
        cost_estimate=SMALL,
    )(place, *quarters, mine, sibling, *waited)


def low(*shape):
    return jax.ShapeDtypeStruct(shape, jnp.bfloat16)


def fresh_blocks(place, own, arrived, moments, *waited):
    kinds, rows, width = own.shape
    chips = len(arrived) + 1

    def kernel(place_ref, own_ref, *refs):
        arrived_refs = refs[: chips - 1]
        moment_ref = refs[chips - 1]
        grad_ref, *out = refs[chips + len(waited) : -1]
        fresh_ref = refs[-1]
        for kind in range(kinds):
            grad_ref[kind] = add_low(own_ref[kind], *[ref[kind] for ref in arrived_refs])
            fresh_ref[kind] = (
                MOMENTUM_DECAY * moment_ref[kind] + grad_ref[kind].astype(jnp.float32)
            ).astype(jnp.bfloat16)
        for turn in range(chips):
            chip = lax.rem(place_ref[1] + chips - turn, chips)
            out[turn][...] = fresh_ref[jnp.where(chip < chips // 2, 0, 1)]

    vmem = pl.BlockSpec(memory_space=pltpu.VMEM)
    return pl.pallas_call(
        kernel,
        out_shape=tuple([low(kinds, rows, width)] + [low(rows, width)] * chips),
        in_specs=[pl.BlockSpec(memory_space=pltpu.SMEM)]
        + [vmem] * (chips + 1)
        + [pl.BlockSpec(memory_space=pl.ANY)] * len(waited),
        out_specs=tuple([vmem] * (chips + 1)),
        scratch_shapes=[pltpu.VMEM((kinds, rows, width), jnp.bfloat16)],
        compiler_params=pltpu.CompilerParams(vmem_limit_bytes=56 * 2**20),
        cost_estimate=SMALL,
    )(place, own, *arrived, moments, *waited)


def first_seen(arrays):
    kept, index = [], []
    for array in arrays:
        found = [place for place, other in enumerate(kept) if other is array]
        if not found:
            kept.append(array)
        index.append(found[0] if found else len(kept) - 1)
    return kept, index


def weight_rows(place, kinds, received=None, waited=()):
    count = len(kinds)
    steps = len(kinds[0][0])
    rows, width = kinds[0][0][0].shape[1] // 2, kinds[0][1][0].shape[1]
    half = rows // 2
    is_own = received is not None
    aligned = all(kind[2] % 128 == 0 for kind in kinds)
    lefts, left_index = first_seen([left for kind in kinds for left in kind[0]])
    rights, right_index = first_seen([right for kind in kinds for right in kind[1]])
    core_rows = [
        kinds[left_index.index(index) // steps][2] for index in range(len(lefts))
    ]
    if not aligned:
        def chosen(left, size):
            cut = left.reshape(left.shape[0], -1, 2, size)
            first_core = (place[2] == 0) if is_own else (place[2] == 1)
            return jnp.where(first_core, cut[:, :, 0], cut[:, :, 1]).reshape(left.shape[0], rows)

        lefts = [chosen(left, size) for left, size in zip(lefts, core_rows)]
    arrays = lefts + rights + (list(received) if is_own else [])

    def kernel(place_ref, *refs):
        left_refs = refs[: len(lefts)]
        right_refs = refs[len(lefts) : len(lefts) + len(rights)]
        received_refs = refs[len(lefts) + len(rights) : len(arrays)]
        rest = refs[len(arrays) + len(waited) :]
        core = place_ref[2] if is_own else 1 - place_ref[2]

        def columns(index):
            ref, size = left_refs[index], core_rows[index]
            if not aligned:
                return ref[...]
            parts = [
                ref[:, pl.ds(pl.multiple_of((2 * chip + core) * size, 128), size)]
                for chip in range(rows // size)
            ]
            return jnp.concatenate(parts, axis=1)

        for kind in range(count):
            for block in range(steps):
                spot = kind * steps + block
                total = matmul_left_t(
                    columns(left_index[spot]), right_refs[right_index[spot]][...]
                )
                step = (place_ref[0] ^ block) if kinds[kind][3] else block
                if is_own:
                    total = total + received_refs[kind][step].astype(jnp.float32)
                    rest[4][kind, step] = total.astype(jnp.bfloat16)
                else:
                    rest[kind][step] = total.astype(jnp.bfloat16)
            if is_own:
                to_x, to_y, kept, later, sums = rest
                to_x[kind, 0], to_x[kind, 1] = sums[kind, 1, :half], sums[kind, 3, :half]
                to_y[kind, 0], to_y[kind, 1] = sums[kind, 2, half:], sums[kind, 3, half:]
                kept[kind, 0], kept[kind, 1] = sums[kind, 0, :half], sums[kind, 0, half:]
                later[kind, 0], later[kind, 1] = sums[kind, 2, :half], sums[kind, 1, half:]

    if is_own:
        out_shapes = [low(count, 2, half, width)] * 4
    else:
        out_shapes = [low(steps, rows, width)] * count
    vmem = pl.BlockSpec(memory_space=pltpu.VMEM)
    flops = sum(2 * rows * width * left.shape[0] for kind in kinds for left in kind[0])
    return pl.pallas_call(
        kernel,
        out_shape=tuple(out_shapes),
        in_specs=[pl.BlockSpec(memory_space=pltpu.SMEM)]
        + [vmem] * len(arrays)
        + [pl.BlockSpec(memory_space=pl.ANY)] * len(waited),
        out_specs=tuple([vmem] * len(out_shapes)),
        scratch_shapes=(
            [pltpu.VMEM((count, steps, rows, width), jnp.bfloat16)] if is_own else []
        ),
        compiler_params=pltpu.CompilerParams(vmem_limit_bytes=56 * 2**20),
        cost_estimate=SMALL,
    )(place, *arrays, *waited)


def later_sums(later, by_x, by_y, waited):
    def kernel(later_ref, x_ref, y_ref, *refs):
        to_y, to_x = refs[-2:]
        for kind in range(later_ref.shape[0]):
            to_y[kind] = add_low(later_ref[kind, 0], x_ref[kind, 1])
            to_x[kind] = add_low(later_ref[kind, 1], y_ref[kind, 1])

    vmem = pl.BlockSpec(memory_space=pltpu.VMEM)
    shape = low(later.shape[0], *later.shape[2:])
    return pl.pallas_call(
        kernel,
        out_shape=(shape, shape),
        in_specs=[vmem] * 3 + [pl.BlockSpec(memory_space=pl.ANY)] * len(waited),
        out_specs=(vmem, vmem),
        compiler_params=pltpu.CompilerParams(vmem_limit_bytes=56 * 2**20),
        cost_estimate=SMALL,
    )(later, by_x, by_y, *waited)


def held_until(value, *waited):
    def kernel(*refs):
        del refs

    anywhere = pl.BlockSpec(memory_space=pl.ANY)
    return pl.pallas_call(
        kernel,
        out_shape=jax.ShapeDtypeStruct(value.shape, value.dtype),
        in_specs=[anywhere] * (1 + len(waited)),
        out_specs=anywhere,
        input_output_aliases={0: 0},
        compiler_params=pltpu.CompilerParams(
            vmem_limit_bytes=56 * 2**20, has_side_effects=True
        ),
        cost_estimate=SMALL,
    )(value, *waited)


def sorted_blocks(place, kept, by_x, by_y, last_x, last_y, chips, waited):
    kinds, _, half, width = kept.shape
    rows = 2 * half // chips

    def kernel(place_ref, kept_ref, x_ref, y_ref, last_x_ref, last_y_ref, *refs):
        out, whole = refs[len(waited) : -1], refs[-1]
        for kind in range(kinds):
            whole[: chips // 2] = add_low(
                kept_ref[kind, 0], x_ref[kind, 0], last_y_ref[kind]
            ).reshape(chips // 2, rows, width)
            whole[chips // 2 :] = add_low(
                kept_ref[kind, 1], y_ref[kind, 0], last_x_ref[kind]
            ).reshape(chips // 2, rows, width)
            for turn in range(chips):
                out[turn][kind] = whole[lax.rem(place_ref[1] + turn, chips)]

    vmem = pl.BlockSpec(memory_space=pltpu.VMEM)
    return pl.pallas_call(
        kernel,
        out_shape=tuple([low(kinds, rows, width)] * chips),
        in_specs=[pl.BlockSpec(memory_space=pltpu.SMEM)]
        + [vmem] * 5
        + [pl.BlockSpec(memory_space=pl.ANY)] * len(waited),
        out_specs=tuple([vmem] * chips),
        scratch_shapes=[pltpu.VMEM((chips, rows, width), jnp.bfloat16)],
        compiler_params=pltpu.CompilerParams(vmem_limit_bytes=56 * 2**20),
        cost_estimate=SMALL,
    )(place, kept, by_x, by_y, last_x, last_y, *waited)


def held_until(value, *waited):
    def kernel(*refs):
        del refs

    anywhere = pl.BlockSpec(memory_space=pl.ANY)
    return pl.pallas_call(
        kernel,
        out_shape=jax.ShapeDtypeStruct(value.shape, value.dtype),
        in_specs=[anywhere] * (1 + len(waited)),
        out_specs=anywhere,
        input_output_aliases={0: 0},
        compiler_params=pltpu.CompilerParams(
            vmem_limit_bytes=56 * 2**20, has_side_effects=True
        ),
        cost_estimate=SMALL,
    )(value, *waited)


def stretch(shape):
    return math.sqrt(max(shape[0], shape[1]) / min(shape[0], shape[1]))


def add_low(*terms):
    total = terms[0].astype(jnp.float32)
    for term in terms[1:]:
        total = total + term.astype(jnp.float32)
    return total.astype(jnp.bfloat16)


def phase_blocks(arrived, by_x, by_y, waited):
    given = [*(arrived or []), *([by_x, by_y] if by_x is not None else [])]
    width = given[0].shape[-1]
    if arrived:
        rows, turns = arrived[0].shape[0], len(arrived)
        total = rows * turns
        half = total // 2
    else:
        total, half = 0, by_x.shape[0] // 3
    send = total + (half if by_x is not None else 0)
    came = by_x.shape[0] if by_x is not None else 0
    out_shapes = [low(send, width)] * 2 + [low(2 * came + total, width)]

    def kernel(*refs):
        inputs = list(refs[: len(given)])
        to_x, to_y, to_core = refs[len(given) + len(waited) :]
        if arrived:
            for turn in range(turns):
                here = slice(turn * rows, (turn + 1) * rows)
                block = inputs.pop(0)[...]
                to_x[here] = to_y[here] = block
                first_row = 2 * came + turn * rows
                to_core[first_row : first_row + rows] = block
        if by_x is not None:
            x_ref, y_ref = inputs.pop(0), inputs.pop(0)
            to_x[total:] = y_ref[:half]
            to_y[total:] = x_ref[half : 2 * half]
            to_core[:came], to_core[came : 2 * came] = x_ref[...], y_ref[...]

    vmem = pl.BlockSpec(memory_space=pltpu.VMEM)
    return pl.pallas_call(
        kernel,
        out_shape=tuple(out_shapes),
        in_specs=[vmem] * len(given) + [pl.BlockSpec(memory_space=pl.ANY)] * len(waited),
        out_specs=tuple([vmem] * len(out_shapes)),
        compiler_params=pltpu.CompilerParams(vmem_limit_bytes=56 * 2**20),
        cost_estimate=SMALL,
    )(*given, *waited)


def block_shares(shares):
    flat = [part[0] if isinstance(part, tuple) else part for share in shares for part in share]
    starts = [part[1] for share in shares for part in share[1:]]
    return flat, starts


def start_blocks(place_ref, flat_refs, starts, out, sem_of, kind, chips, by_rep):
    reps, rows = flat_refs[0].shape[1:3]
    turns = chips - 1
    half = turns * rows // 2
    my_rep, my_chip, my_core = place_ref[0], place_ref[1], place_ref[2]
    cuts = []
    for turn in range(turns):
        low_end, high_end = turn * rows, (turn + 1) * rows
        middle = min(max(half, low_end), high_end)
        if middle > low_end:
            cuts.append((0, low_end, turn, 0, middle - low_end))
        if high_end > middle:
            cuts.append((1, middle - half, turn, middle - low_end, high_end - middle))
    copies = [[] for step in range(reps)]

    def start(step, source, target):
        copy = pltpu.make_async_copy(source, target, sem_of(step, len(copies[step])))
        copy.start()
        copies[step].append(copy)

    for step in range(reps):
        from_rep = my_rep ^ step
        to_rep = from_rep if by_rep else step
        for side in range(2):
            core = my_core if side == 0 else 1 - my_core
            own, *moved = flat_refs[6 * side : 6 * side + 6]
            first_rows = starts[5 * side : 5 * side + 5]
            start(step, own.at[kind, from_rep], out.at[to_rep, my_chip, core])
            if step < reps - 1:
                for turn in range(turns):
                    start(
                        step,
                        moved[step].at[pl.ds(first_rows[step] + turn * rows, rows)],
                        out.at[to_rep, lax.rem(my_chip + 1 + turn, chips), core],
                    )
            else:
                for part, source_row, turn, target_row, count in cuts:
                    start(
                        step,
                        moved[3 + part].at[pl.ds(first_rows[3 + part] + source_row, count)],
                        out.at[
                            to_rep,
                            lax.rem(my_chip + 1 + turn, chips),
                            core,
                            pl.ds(target_row, count),
                        ],
                    )
    return copies


def placed_blocks(place, shares, kind, chips, waited):
    reps, rows, width = shares[0][0].shape[1:]
    flat, starts = block_shares(shares)

    def kernel(place_ref, *refs):
        results = refs[len(flat) + len(waited) : -3]
        out, sems, out_sems = refs[-3:]
        copies = start_blocks(
            place_ref,
            refs[: len(flat)],
            starts,
            out,
            lambda step, index: sems.at[step, index],
            kind,
            chips,
            True,
        )
        for step in range(reps):
            for copy in copies[step]:
                copy.wait()
        writes = [
            pltpu.make_async_copy(out.at[step], results[step], out_sems.at[step])
            for step in range(reps)
        ]
        for write in writes:
            write.start()
        for write in writes:
            write.wait()

    shape = (reps, chips, 2, rows, width)
    anywhere = pl.BlockSpec(memory_space=pl.ANY)
    full = pl.pallas_call(
        kernel,
        out_shape=tuple([low(*shape[1:])] * reps),
        in_specs=[pl.BlockSpec(memory_space=pltpu.SMEM)] + [anywhere] * (len(flat) + len(waited)),
        out_specs=tuple([anywhere] * reps),
        scratch_shapes=[
            pltpu.VMEM(shape, jnp.bfloat16),
            pltpu.SemaphoreType.DMA((reps, 2 * chips + 2)),
            pltpu.SemaphoreType.DMA((reps,)),
        ],
        compiler_params=pltpu.CompilerParams(vmem_limit_bytes=56 * 2**20),
        cost_estimate=SMALL,
    )(place, *flat, *waited)
    return [matrix.reshape(-1, width) for matrix in full]


GELU_SCALE = math.sqrt(2.0 / math.pi)
GELU_CUBE = 0.044715


def feed_forward(place, in_shares, out_shares, chips, third_low, residual, grad_branch):
    reps, rows, width = in_shares[0][0].shape[1:]
    in_flat, in_starts = block_shares(in_shares)
    out_flat, out_starts = block_shares(out_shares)
    tokens = third_low.shape[0]

    def kernel(place_ref, third_ref, residual_ref, branch_ref, *refs):
        in_refs = refs[: len(in_flat)]
        out_refs = refs[len(in_flat) : len(in_flat) + len(out_flat)]
        block_out, grad_third, *parts = refs[len(in_flat) + len(out_flat) : -3]
        hidden, grad_pre = parts[:reps], parts[reps:]
        in_full, out_full, sems = refs[-3:]
        in_copies = start_blocks(
            place_ref, in_refs, in_starts, in_full,
            lambda step, index: sems.at[0, step, index], 2, chips, False,
        )
        out_copies = start_blocks(
            place_ref, out_refs, out_starts, out_full,
            lambda step, index: sems.at[1, step, index], 3, chips, False,
        )
        for step in range(reps):
            for copy in in_copies[step]:
                copy.wait()
            in_weights = in_full[step].reshape(-1, width)
            pre = matmul(third_ref[...], in_weights)
            for copy in out_copies[step]:
                copy.wait()
            out_weights = out_full[step].reshape(-1, width)
            grad_hidden = matmul_right_t(branch_ref[...], out_weights)
            square = pre * pre
            bent = jnp.tanh(GELU_SCALE * pre * (1.0 + GELU_CUBE * square))
            units = (0.5 * pre * (1.0 + bent)).astype(jnp.bfloat16)
            slope = 0.5 * (1.0 + bent) + 0.5 * pre * (1.0 - bent * bent) * GELU_SCALE * (
                1.0 + 3.0 * GELU_CUBE * square
            )
            grads = (grad_hidden * slope).astype(jnp.bfloat16)
            hidden[step][...] = units
            grad_pre[step][...] = grads
            to_third = matmul_right_t(grads, in_weights)
            to_out = matmul(units, out_weights)
            if step == 0:
                grad_third[...] = to_third
                block_out[...] = residual_ref[...] + to_out
            else:
                grad_third[...] += to_third
                block_out[...] += to_out

    vmem = pl.BlockSpec(memory_space=pltpu.VMEM)
    whole = jax.ShapeDtypeStruct((tokens, width), jnp.float32)
    shape = (reps, chips, 2, rows, width)
    results = pl.pallas_call(
        kernel,
        out_shape=(whole, whole, *[low(tokens, width)] * (2 * reps)),
        in_specs=[pl.BlockSpec(memory_space=pltpu.SMEM)]
        + [vmem] * 3
        + [pl.BlockSpec(memory_space=pl.ANY)] * (len(in_flat) + len(out_flat)),
        out_specs=(vmem,) * (2 + 2 * reps),
        scratch_shapes=[
            pltpu.VMEM(shape, jnp.bfloat16),
            pltpu.VMEM(shape, jnp.bfloat16),
            pltpu.SemaphoreType.DMA((2, reps, 2 * chips + 2)),
        ],
        compiler_params=pltpu.CompilerParams(vmem_limit_bytes=56 * 2**20),
        cost_estimate=SMALL,
    )(place, third_low, residual, grad_branch, *in_flat, *out_flat)
    block_out, grad_third, *parts = results
    return block_out, grad_third, parts[:reps], parts[reps:]


def prepared(place, matrices, moments, shards, sub, waited):
    reps, rows, width = matrices[0].shape

    def kernel(place_ref, *refs):
        stacks, hidden_in, hidden_out = refs[0:2], refs[2], refs[3]
        old_stacks, old_in, old_out = refs[4:6], refs[6], refs[7]
        whole, *outs = refs[8 + len(waited) :]
        quarters, wide_old, square_old, sems = outs[:3], outs[3], outs[4], outs[5]
        my_rep = place_ref[0]
        copies = []

        def start(source, target):
            copy = pltpu.make_async_copy(source, target, sems.at[len(copies)])
            copy.start()
            copies.append(copy)

        for kind in range(2):
            start(old_stacks[kind].at[my_rep], square_old.at[kind])
        start(old_out.at[pl.ds(pl.multiple_of(my_rep * sub, sub), sub)], wide_old.at[1])
        for shard in range(shards):
            first = pl.multiple_of((shard * reps + my_rep) * sub, sub)
            start(
                old_in.at[:, pl.ds(first, sub)],
                wide_old.at[0, :, pl.ds(shard * sub, sub)],
            )
        for kind in range(2):
            whole[kind] = stacks[kind][...].astype(jnp.bfloat16)
        for step in range(reps):
            for shard in range(shards):
                first = (shard * reps + step) * sub
                whole[2, step, :, shard * sub : (shard + 1) * sub] = hidden_in[
                    :, first : first + sub
                ].astype(jnp.bfloat16)
            whole[3, step] = hidden_out[step * sub : (step + 1) * sub].astype(jnp.bfloat16)
        for kind in range(1, 4):
            quarters[kind - 1][...] = whole[kind, my_rep]
        for copy in copies:
            copy.wait()

    vmem = pl.BlockSpec(memory_space=pltpu.VMEM)
    anywhere = pl.BlockSpec(memory_space=pl.ANY)
    old = jax.ShapeDtypeStruct((2, rows, width), jnp.float32)
    whole, *parts, wide_old, square_old = pl.pallas_call(
        kernel,
        out_shape=(low(4, reps, rows, width), *[low(rows, width)] * 3, old, old),
        in_specs=[pl.BlockSpec(memory_space=pltpu.SMEM)]
        + [vmem] * 4
        + [anywhere] * (4 + len(waited)),
        out_specs=(vmem,) * 6,
        scratch_shapes=[pltpu.SemaphoreType.DMA((shards + 3,))],
        compiler_params=pltpu.CompilerParams(vmem_limit_bytes=56 * 2**20),
        cost_estimate=SMALL,
    )(place, *matrices, *moments, *waited)
    return whole, parts, wide_old, square_old


def branch_back(grad_query, weights, stream, gain, grad_stream, next_weights, *waited):
    rows, width = stream.shape

    def kernel(query_ref, weights_ref, stream_ref, gain_ref, grad_ref, next_ref, *refs):
        total_ref, branch_ref, mixed_ref, gain_grad, bias_grad = refs[len(waited) :]
        grad_out = matmul_right_t(query_ref[...], weights_ref[...])
        values = stream_ref[...]
        centered = values - jnp.mean(values, axis=-1, keepdims=True)
        inverse = lax.rsqrt(jnp.mean(centered * centered, axis=-1, keepdims=True) + NORM_EPSILON)
        unit_part = centered * inverse
        grad_unit = grad_out * gain_ref[...]
        grad_in = inverse * (
            grad_unit
            - jnp.mean(grad_unit, axis=-1, keepdims=True)
            - unit_part * jnp.mean(grad_unit * unit_part, axis=-1, keepdims=True)
        )
        total = grad_ref[...] + grad_in
        branch = total.astype(jnp.bfloat16)
        total_ref[...] = total
        branch_ref[...] = branch
        mixed_ref[...] = matmul_right_t(branch, next_ref[...]).astype(jnp.bfloat16)
        gain_grad[...] = jnp.sum(grad_out * unit_part, axis=0, keepdims=True)
        bias_grad[...] = jnp.sum(grad_out, axis=0, keepdims=True)

    vmem = pl.BlockSpec(memory_space=pltpu.VMEM)
    line = jax.ShapeDtypeStruct((1, width), jnp.float32)
    return pl.pallas_call(
        kernel,
        out_shape=(
            jax.ShapeDtypeStruct((rows, width), jnp.float32),
            low(rows, width),
            low(rows, width),
            line,
            line,
        ),
        in_specs=[vmem] * 6 + [pl.BlockSpec(memory_space=pl.ANY)] * len(waited),
        out_specs=(vmem,) * 5,
        compiler_params=pltpu.CompilerParams(vmem_limit_bytes=56 * 2**20),
        cost_estimate=SMALL,
    )(grad_query, weights, stream, gain, grad_stream, next_weights, *waited)


def on_device(
    tokens,
    states,
    cotangent,
    dec_len,
    enc_len,
    self_weights,
    cross_weights,
    fc_in,
    fc_out,
    norm_params,
    self_moment,
    cross_moment,
    fc_in_moment,
    fc_out_moment,
    norm_moment,
):
    reps = lax.axis_size("rep")
    shards = lax.axis_size("shard")
    chips = shards // 2
    my_rep = lax.axis_index("rep")
    my_place = lax.axis_index("shard")
    my_chip = my_place // 2
    my_core = lax.rem(my_place, 2)
    even = my_core == 0
    width = self_weights.shape[2]
    rows = self_weights.shape[1]
    hidden_width = fc_in.shape[1]
    sub = hidden_width // (shards * reps)

    def swap(values):
        return lax.ppermute(values, "shard", [(index, index ^ 1) for index in range(shards)])

    def from_chip(values, turn):
        pairs = [
            (2 * ((chip + turn) % chips) + core, 2 * chip + core)
            for chip in range(chips)
            for core in range(2)
        ]
        return lax.ppermute(values, "shard", pairs)

    def from_rep(values, step):
        return lax.ppermute(values, "rep", [(index ^ step, index) for index in range(reps)])

    low_bit = (my_rep & 1) == 1
    high_bit = (my_rep & 2) == 2

    def by_rep(steps):
        turned = [jnp.where(low_bit, steps[step ^ 1], steps[step]) for step in range(reps)]
        return [jnp.where(high_bit, turned[step ^ 2], turned[step]) for step in range(reps)]

    is_lower = my_chip < chips // 2
    place_now = jnp.stack([my_rep, my_chip, my_core, is_lower]).astype(jnp.int32)

    def first_blocks(quarter):
        return [from_chip(quarter, turn) for turn in range(1, chips)]

    total_rows = (chips - 1) * rows

    def run_phase(state, phase, waited):
        to_x, to_y, to_core = phase_blocks(
            state["arrived"] if phase < 4 else None,
            state["by_x"][-1] if phase > 0 else None,
            state["by_y"][-1] if phase > 0 else None,
            [*waited, *state["came"][-1:]],
        )
        if phase < 3:
            quarter = held_until(state["quarters"][phase], to_core)
            state["arrived"] = first_blocks(quarter)
        state["sent"].append(to_x)
        state["by_x"].append(from_rep(to_x, 1))
        state["by_y"].append(from_rep(to_y, 2))
        state["came"].append(swap(to_core))

    def shares_of(state, kind, last_pair=None):
        by_x, by_y, came = state["by_x"], state["by_y"], state["came"]
        size = total_rows if kind == 0 else total_rows + total_rows // 2
        next_size = total_rows // 2 if kind == 3 else total_rows + total_rows // 2
        behind = next_size - total_rows // 2
        before = [0, 2 * total_rows, 3 * total_rows, 3 * total_rows][kind]
        mine = [
            state["shards"],
            (state["sent"][kind], 0),
            (by_x[kind], 0),
            (by_y[kind], 0),
            (by_x[kind + 1], behind),
            (by_y[kind + 1], behind),
        ]
        last = last_pair or (came[kind + 2], came[kind + 2])
        siblings = [
            state["other_shards"],
            (came[kind], before),
            (came[kind + 1], 0),
            (came[kind + 1], size),
            (last[0], behind),
            (last[1], behind if last_pair else next_size + behind),
        ]
        return mine, siblings

    def of_rep(values):
        return lax.dynamic_index_in_dim(values, my_rep, 0, keepdims=False)

    def in_quarters(matrix):
        return matrix.reshape(rows, shards, reps, sub).transpose(2, 0, 1, 3).reshape(
            reps, rows, shards * sub
        )

    def in_shard(pieces):
        cut = jnp.stack(pieces).reshape(reps, rows, shards, sub)
        return cut.transpose(1, 2, 0, 3).reshape(rows, hidden_width)

    def prepare():
        matrices = [self_weights, cross_weights, fc_in, fc_out]
        moments = [self_moment, cross_moment, fc_in_moment, fc_out_moment]
        if sub % 128 == 0:
            return prepared(place_now, matrices, moments, shards, sub, [])
        whole = jnp.stack(
            [
                self_weights.astype(jnp.bfloat16),
                cross_weights.astype(jnp.bfloat16),
                in_quarters(fc_in.astype(jnp.bfloat16)),
                fc_out.reshape(reps, sub, width).astype(jnp.bfloat16),
            ]
        )
        wide_old = [of_rep(in_quarters(fc_in_moment)), of_rep(moments[3].reshape(reps, sub, width))]
        square_old = [of_rep(self_moment), of_rep(cross_moment)]
        quarters = [of_rep(whole[kind]) for kind in range(1, 4)]
        return whole, quarters, jnp.stack(wide_old), jnp.stack(square_old)

    state = {"by_x": [], "by_y": [], "came": [], "sent": []}
    state["arrived"] = first_blocks(of_rep(self_weights).astype(jnp.bfloat16))
    state["shards"], state["quarters"], wide_moments, square_moments = prepare()
    state["other_shards"] = swap(state["shards"])
    run_phase(state, 0, [state["shards"]])
    run_phase(state, 1, [state["other_shards"]])
    run_phase(state, 2, [])
    self_full = placed_blocks(place_now, shares_of(state, 0), 0, chips, [])

    def first_sums(kinds, others, *waited):
        received = [swap(other) for other in others]
        to_x, to_y, kept, later = weight_rows(place_now, kinds, received, waited)
        return kept, later, from_rep(to_x, 1), from_rep(to_y, 2)

    def second_sums(stage, *waited):
        kept, later, by_x, by_y = stage
        to_y, to_x = later_sums(later, by_x, by_y, waited)
        return (kept, by_x, by_y, from_rep(to_x, 1), from_rep(to_y, 2)), to_x

    def third_sums(stage, *waited):
        blocks = sorted_blocks(place_now, *stage, chips, waited)
        arrived = [from_chip(blocks[chips - turn], turn) for turn in range(1, chips)]
        return blocks[0], arrived

    def share_pair(pair, *waited):
        by_x, by_y = from_rep(pair, 1), from_rep(pair, 2)
        across = jnp.stack([from_rep(by_y[0], 1), from_rep(by_x[1], 2)])
        return [pair, by_x, by_y, across]

    def to_replicas(steps):
        return by_rep([step[0] for step in steps]), by_rep([step[1] for step in steps])

    source = tokens[0].astype(jnp.float32)
    encoded = states[0]
    gain_rows = norm_params[0]
    bias_rows = norm_params[1]
    first, first_unit, first_inv = normalize_parts(source, gain_rows[0], bias_rows[0])
    first_low = first.astype(jnp.bfloat16)
    query_rows = matmul(first_low, self_full[0]).astype(jnp.bfloat16)
    incoming_keys = matmul(first_low, self_full[1]).astype(jnp.bfloat16)
    incoming_values = matmul(first_low, self_full[2]).astype(jnp.bfloat16)
    run_phase(state, 3, [query_rows, incoming_keys, incoming_values])
    cross_full = placed_blocks(place_now, shares_of(state, 1), 1, chips, [])
    attended_values = attend_forward(query_rows, incoming_keys, incoming_values, dec_len, True)
    after_self = source + matmul(attended_values, self_full[3])
    second, second_unit, second_inv = normalize_parts(after_self, gain_rows[1], bias_rows[1])
    second_low = second.astype(jnp.bfloat16)
    cross_keys = matmul(encoded, cross_full[1]).astype(jnp.bfloat16)
    cross_values = matmul(encoded, cross_full[2]).astype(jnp.bfloat16)
    run_phase(state, 4, [cross_keys, cross_values, after_self])
    hidden_shares = [
        shares_of(state, 2),
        shares_of(state, 3, (swap(state["by_x"][-1]), swap(state["by_y"][-1]))),
    ]
    cross_query = matmul(second_low, cross_full[0]).astype(jnp.bfloat16)
    cross_mixed = attend_forward(cross_query, cross_keys, cross_values, enc_len, False)
    after_cross = after_self + matmul(cross_mixed, cross_full[3])
    third, third_unit, third_inv = normalize_parts(after_cross, gain_rows[2], bias_rows[2])
    third_low = third.astype(jnp.bfloat16)
    grad_out = cotangent[0].astype(jnp.float32)
    grad_branch = cotangent[0]
    block_out, grad_third, hidden, grad_pre = feed_forward(
        place_now, *hidden_shares, chips, third_low, after_cross, grad_branch
    )
    wide_kinds = [
        ([third_low] * reps, grad_pre, rows, False),
        (hidden, [grad_branch] * reps, sub, False),
    ]
    in_other = weight_rows(place_now, wide_kinds[:1])[0]
    out_other = weight_rows(place_now, wide_kinds[1:], None, [in_other])[0]
    grad_norm, third_gain, third_bias = normalize_back(
        grad_third, third_unit, third_inv, gain_rows[2]
    )
    grad_cross = grad_out + grad_norm
    cross_branch = grad_cross.astype(jnp.bfloat16)
    grad_mixed = matmul_right_t(cross_branch, cross_full[3]).astype(jnp.bfloat16)
    grad_cq, grad_ck, grad_cv = attend_backward(
        cross_query, cross_keys, cross_values, enc_len, False, grad_mixed
    )
    wide_stage = first_sums(wide_kinds, [in_other, out_other], grad_cq)
    cross_kind = (
        [second_low, encoded, encoded, cross_mixed],
        [grad_cq, grad_ck, grad_cv, cross_branch],
        rows,
        True,
    )
    cross_other = weight_rows(place_now, [cross_kind], None, [wide_stage[0]])[0]
    grad_self, self_branch, grad_mixed, second_gain, second_bias = branch_back(
        grad_cq,
        cross_full[0],
        after_self,
        gain_rows[1:2],
        grad_cross,
        self_full[3],
        cross_other,
    )
    second_gain, second_bias = second_gain[0], second_bias[0]
    grad_sq, grad_sk, grad_sv = attend_backward(
        query_rows, incoming_keys, incoming_values, dec_len, True, grad_mixed
    )
    self_kind = (
        [first_low, first_low, first_low, attended_values],
        [grad_sq, grad_sk, grad_sv, self_branch],
        rows,
        True,
    )
    wide_stage, wide_token = second_sums(wide_stage, grad_sq)
    cross_stage = first_sums([cross_kind], [cross_other], wide_token)
    self_other = weight_rows(place_now, [self_kind], None, [cross_stage[0]])[0]
    wide_stage = third_sums(wide_stage, self_other)
    cross_stage, cross_token = second_sums(cross_stage, wide_stage[0])
    self_stage = first_sums([self_kind], [self_other], cross_token, *cross_stage[3:])
    wide_fresh = fresh_blocks(place_now, *wide_stage, wide_moments, self_stage[0])
    wide_grads = wide_fresh[0]
    cross_stage = third_sums(cross_stage, wide_grads)
    self_stage, self_token = second_sums(self_stage, cross_stage[0])

    def owned(grads_fresh):
        mine, *sent = grads_fresh[1:]
        arrived = [from_chip(sent[turn - 1], turn) for turn in range(1, chips)]
        mine = jnp.concatenate([mine, *arrived])
        return mine, swap(mine)

    def to_both(result):
        other = from_chip(result[1], chips // 2)
        return jnp.stack(
            [jnp.where(is_lower, result[0], other), jnp.where(is_lower, other, result[0])]
        )

    wide_own = owned(wide_fresh)
    to_x, to_y, kept, later = gram_parts(place_now, *wide_own, reps, self_token)
    self_stage = third_sums(self_stage, kept, *cross_stage[1])
    gram_stage, gram_token = second_sums((kept, later, from_rep(to_x, 1), from_rep(to_y, 2)))
    kept, by_x, by_y, last_x, last_y = gram_stage
    quarter = jnp.concatenate(
        [add_low(kept[0, 0], by_x[0, 0], last_y[0]), add_low(kept[0, 1], by_y[0, 0], last_x[0])]
    )
    quarter_x, quarter_y = from_rep(quarter, 1), from_rep(quarter, 2)
    part = quarter.shape[0] // 2
    quarters = [
        quarter,
        quarter_x,
        quarter_y,
        from_rep(quarter_y[:part], 1),
        from_rep(quarter_x[part:], 2),
    ]
    square_fresh = fresh_blocks(
        place_now,
        jnp.concatenate([self_stage[0], cross_stage[0]]),
        [jnp.concatenate(pair) for pair in zip(self_stage[1], cross_stage[1])],
        square_moments,
        gram_token,
    )
    square_grads = square_fresh[0]
    square_own = owned(square_fresh)
    grads = jnp.concatenate([wide_grads, square_grads])
    grads_x, grads_y = from_rep(grads, 1), from_rep(grads, 2)
    wide_rows = gram_schulz(place_now, quarters, *wide_own, rows, square_grads)
    wide_orth = to_both(wide_rows)
    wide_orth_shared = share_pair(wide_orth)
    square_rows = square_schulz(*square_own, rows, wide_orth, grads_x, grads_y)
    grads_across = [from_rep(grads_y[:2], 1), from_rep(grads_x[2:], 2)]
    late_sq = held_until(grad_sq, square_rows)
    late_ck = held_until(grad_ck, square_rows)
    grad_states = matmul_right_t(late_ck, cross_full[1]) + matmul_right_t(grad_cv, cross_full[2])
    grad_first = (
        matmul_right_t(late_sq, self_full[0])
        + matmul_right_t(grad_sk, self_full[1])
        + matmul_right_t(grad_sv, self_full[2])
    )
    grad_norm, first_gain, first_bias = normalize_back(
        grad_first, first_unit, first_inv, gain_rows[0]
    )
    grad_tokens = grad_self + grad_norm
    norm_local = jnp.stack(
        [
            jnp.stack([first_gain, second_gain, third_gain]),
            jnp.stack([first_bias, second_bias, third_bias]),
        ]
    )
    norm_local = held_until(norm_local, square_rows)
    norm_total = norm_local + swap(norm_local)
    norm_total = norm_total + from_rep(norm_total, 1)
    norm_total = norm_total + from_rep(norm_total, 2)
    norm_total = sum([from_chip(norm_total, turn) for turn in range(1, chips)], norm_total)
    width_part = norm_moment.shape[2]
    norm_grad = lax.dynamic_slice_in_dim(norm_total, my_place * width_part, width_part, 2)

    late_grads = held_until(grads, square_rows)
    wide_grads_shared = [late_grads[:2], grads_x[:2], grads_y[:2], grads_across[0]]
    square_grads_shared = [late_grads[2:], grads_x[2:], grads_y[2:], grads_across[1]]
    in_shared, out_shared = to_replicas(wide_grads_shared)
    self_shared, cross_shared = to_replicas(square_grads_shared)

    def stacked(pieces):
        return jnp.stack(pieces).astype(jnp.float32)

    def lengthwise(pieces):
        return jnp.concatenate(pieces).astype(jnp.float32)

    self_grad = stacked(self_shared)
    cross_grad = stacked(cross_shared)
    fc_in_grad = in_shard(in_shared).astype(jnp.float32)
    fc_out_grad = lengthwise(out_shared)
    self_fresh = MOMENTUM_DECAY * self_moment + self_grad
    cross_fresh = MOMENTUM_DECAY * cross_moment + cross_grad
    in_fresh = MOMENTUM_DECAY * fc_in_moment + fc_in_grad
    out_fresh = MOMENTUM_DECAY * fc_out_moment + fc_out_grad

    square_orth = held_until(
        to_both(square_rows),
        wide_orth_shared[1],
        wide_orth_shared[2],
        self_fresh,
        cross_fresh,
        in_fresh,
        out_fresh,
    )
    square_orth_shared = share_pair(square_orth)
    wide_orth_shared[0] = held_until(wide_orth_shared[0], *square_orth_shared[1:3])
    in_orth_shared, out_orth_shared = to_replicas(wide_orth_shared)
    self_orth_shared, cross_orth_shared = to_replicas(square_orth_shared)
    self_orth = stacked(self_orth_shared)
    cross_orth = stacked(cross_orth_shared)
    in_orth = in_shard(in_orth_shared).astype(jnp.float32)
    out_orth = lengthwise(out_orth_shared)
    norm_fresh = MOMENTUM_DECAY * norm_moment + norm_grad
    self_new = self_weights - MATRIX_RATE * stretch((width, width)) * self_orth
    cross_new = cross_weights - MATRIX_RATE * stretch((width, width)) * cross_orth
    in_new = fc_in - MATRIX_RATE * stretch((width, hidden_width)) * in_orth
    out_new = fc_out - MATRIX_RATE * stretch((hidden_width, width)) * out_orth
    own_params = lax.dynamic_slice_in_dim(norm_params, my_place * width_part, width_part, 2)
    total_tokens = reps * shards * tokens.shape[0] * tokens.shape[1]
    norm_new = own_params - VECTOR_RATE * norm_fresh / math.sqrt(total_tokens)
    return (
        block_out[None].astype(jnp.bfloat16),
        grad_tokens[None].astype(jnp.bfloat16),
        grad_states[None].astype(jnp.bfloat16),
        self_grad,
        cross_grad,
        fc_in_grad,
        fc_out_grad,
        norm_grad,
        self_fresh,
        cross_fresh,
        in_fresh,
        out_fresh,
        norm_fresh,
        self_new,
        cross_new,
        in_new,
        out_new,
        norm_new,
        self_new.astype(jnp.bfloat16),
        cross_new.astype(jnp.bfloat16),
        in_new.astype(jnp.bfloat16),
        out_new.astype(jnp.bfloat16),
    )


def solution(mesh):
    placed = (
        P(("rep", "shard"), None, None),
        P(("rep", "shard"), None, None),
        P(("rep", "shard"), None, None),
        P(("rep", "shard")),
        P(("rep", "shard")),
        P(None, "shard", None),
        P(None, "shard", None),
        P("shard", None),
        P("shard", None),
        P(),
        P(None, "shard", None),
        P(None, "shard", None),
        P("shard", None),
        P("shard", None),
        P(None, None, "shard"),
    )
    return jax.shard_map(
        on_device,
        mesh=mesh,
        in_specs=placed,
        out_specs=(
            P(("rep", "shard"), None, None),
            P(("rep", "shard"), None, None),
            P(("rep", "shard"), None, None),
            P(None, "shard", None),
            P(None, "shard", None),
            P("shard", None),
            P("shard", None),
            P(None, None, "shard"),
            P(None, "shard", None),
            P(None, "shard", None),
            P("shard", None),
            P("shard", None),
            P(None, None, "shard"),
            P(None, "shard", None),
            P(None, "shard", None),
            P("shard", None),
            P("shard", None),
            P(None, None, "shard"),
            P(None, "shard", None),
            P(None, "shard", None),
            P("shard", None),
            P("shard", None),
        ),
        check_vma=False,
    )
```

```python
import math

import jax
import jax.numpy as jnp
from jax import lax
from jax.experimental import pallas as pl
from jax.experimental.pallas import tpu as pltpu
from jax.sharding import PartitionSpec as P

HEADS = 16
HEAD_DIM = 64
NS_STEPS = 3


NORM_EPSILON = 1e-05
MOMENTUM_DECAY = 0.9
MATRIX_RATE = 0.6
VECTOR_RATE = 0.05
SCHULZ_FIRST = 3.4445
SCHULZ_SECOND = -4.775
SCHULZ_THIRD = 2.0315


def matmul(left, right):
    return jnp.dot(left, right, preferred_element_type=jnp.float32)


def matmul_left_t(left, right):
    return lax.dot_general(
        left, right, (((0,), (0,)), ((), ())), preferred_element_type=jnp.float32
    )


def matmul_right_t(left, right):
    return lax.dot_general(
        left, right, (((1,), (1,)), ((), ())), preferred_element_type=jnp.float32
    )


def normalize_parts(values, gain, bias):
    centered = values - jnp.mean(values, axis=-1, keepdims=True)
    inverse = lax.rsqrt(jnp.mean(centered * centered, axis=-1, keepdims=True) + NORM_EPSILON)
    unit_part = centered * inverse
    return (unit_part * gain + bias, unit_part, inverse)


def normalize_back(grad_out, unit_part, inverse, gain):
    grad_unit = grad_out * gain
    grad_in = inverse * (
        grad_unit
        - jnp.mean(grad_unit, axis=-1, keepdims=True)
        - unit_part * jnp.mean(grad_unit * unit_part, axis=-1, keepdims=True)
    )
    return (grad_in, jnp.sum(grad_out * unit_part, axis=0), jnp.sum(grad_out, axis=0))


PAIR = 2 * HEAD_DIM
SMALL = pl.CostEstimate(flops=1024, bytes_accessed=1024, transcendentals=0)


def attention_parts(count_ref, causal, query_part, keys, is_first):
    lane = lax.broadcasted_iota(jnp.int32, (1, PAIR), 1)
    own = (lane < HEAD_DIM) == is_first
    scores = matmul_right_t(jnp.where(own, query_part, 0), keys) * HEAD_DIM ** (-0.5)
    key_place = lax.broadcasted_iota(jnp.int32, scores.shape, 1)
    valid = key_place < count_ref[0]
    if causal:
        valid = valid & (key_place <= lax.broadcasted_iota(jnp.int32, scores.shape, 0))
    scores = jnp.where(valid, scores, -jnp.inf)
    exponent = jnp.exp(scores - jnp.max(scores, axis=-1, keepdims=True))
    return exponent / jnp.sum(exponent, axis=-1, keepdims=True), own


def head_pairs(width, body):
    def step(index, carry):
        body(pl.ds(pl.multiple_of(index * PAIR, PAIR), PAIR))
        return carry

    lax.fori_loop(0, width // PAIR, step, 0)


def attention_call(kernel, out_shapes, count, arrays, waited):
    rows, width = arrays[0].shape
    keys = arrays[1].shape[0]
    vmem = pl.BlockSpec(memory_space=pltpu.VMEM)
    return pl.pallas_call(
        kernel,
        out_shape=tuple(out_shapes),
        in_specs=[pl.BlockSpec(memory_space=pltpu.SMEM)]
        + [vmem] * len(arrays)
        + [pl.BlockSpec(memory_space=pl.ANY)] * len(waited),
        out_specs=tuple([vmem] * len(out_shapes)),
        compiler_params=pltpu.CompilerParams(vmem_limit_bytes=56 * 2**20),
        cost_estimate=SMALL,
    )(count, *arrays, *waited)


def attend_forward(query_rows, incoming_keys, incoming_values, count, causal, *waited):
    def kernel(count_ref, query_ref, key_ref, value_ref, *refs):
        mixed_ref = refs[-1]

        def one_pair(columns):
            query_part, keys = query_ref[:, columns], key_ref[:, columns]
            values = value_ref[:, columns]
            mixed = None
            for is_first in (True, False):
                weights, own = attention_parts(count_ref, causal, query_part, keys, is_first)
                here = matmul(weights.astype(jnp.bfloat16), values)
                mixed = here if mixed is None else jnp.where(own, here, mixed)
            mixed_ref[:, columns] = mixed.astype(jnp.bfloat16)

        head_pairs(query_ref.shape[1], one_pair)

    return attention_call(
        kernel,
        [low(*query_rows.shape)],
        count,
        [query_rows, incoming_keys, incoming_values],
        waited,
    )[0]


def attend_backward(
    query_rows, incoming_keys, incoming_values, count, causal, grad_mixed, *waited
):
    def kernel(count_ref, query_ref, key_ref, value_ref, grad_ref, *refs):
        grad_query, grad_keys, grad_values = refs[-3:]
        scale = HEAD_DIM ** (-0.5)

        def one_pair(columns):
            query_part, keys = query_ref[:, columns], key_ref[:, columns]
            values, grads = value_ref[:, columns], grad_ref[:, columns]
            found = None
            for is_first in (True, False):
                weights, own = attention_parts(count_ref, causal, query_part, keys, is_first)
                grad_prob = matmul_right_t(jnp.where(own, grads, 0), values)
                shift = jnp.sum(grad_prob * weights, axis=-1, keepdims=True)
                score_grad = (weights * (grad_prob - shift)).astype(jnp.bfloat16)
                here = (
                    matmul(score_grad, keys) * scale,
                    matmul_left_t(score_grad, query_part) * scale,
                    matmul_left_t(weights.astype(jnp.bfloat16), grads),
                )
                if found is None:
                    found = here
                else:
                    found = [jnp.where(own, new, old) for new, old in zip(here, found)]
            for ref, value in zip((grad_query, grad_keys, grad_values), found):
                ref[:, columns] = value.astype(jnp.bfloat16)

        head_pairs(query_ref.shape[1], one_pair)

    return attention_call(
        kernel,
        [low(*query_rows.shape), low(*incoming_keys.shape), low(*incoming_keys.shape)],
        count,
        [query_rows, incoming_keys, incoming_values, grad_mixed],
        waited,
    )


TILE = 256


def in_tiles(size, body):
    def step(index, carry):
        body(pl.ds(pl.multiple_of(index * TILE, TILE), TILE))
        return carry

    lax.fori_loop(0, size // TILE, step, 0)


def wide_view(ref, rows):
    return ref[rows, :].astype(jnp.float32)


def first_and_opposite(rows, total):
    return slice(0, rows), slice(total // 2, total // 2 + rows)


def square_schulz(mine, sibling, rows, *waited):
    size = mine.shape[1]
    half = mine.shape[0]

    def kernel(mine_ref, sibling_ref, *refs):
        result, current, gram, poly, total = refs[len(waited) :]
        current[:half], current[half:] = mine_ref[...], sibling_ref[...]
        total[...] = jnp.zeros_like(total)

        def add_squares(rows):
            part = wide_view(current, rows)
            total[...] += jnp.sum(part * part, axis=0, keepdims=True)

        in_tiles(size, add_squares)
        scale = 1.0 / (jnp.sqrt(jnp.sum(total[...])) + 1e-07)

        def scaled(rows):
            current[rows, :] = (wide_view(current, rows) * scale).astype(jnp.bfloat16)

        in_tiles(size, scaled)
        for sweep_index in range(NS_STEPS):

            def gram_rows(rows):
                gram[rows, :] = matmul_right_t(current[rows, :], current[...]).astype(
                    jnp.bfloat16
                )

            def poly_rows(rows):
                poly[rows, :] = (
                    SCHULZ_SECOND * wide_view(gram, rows)
                    + SCHULZ_THIRD * matmul(gram[rows, :], gram[...])
                ).astype(jnp.bfloat16)

            def next_rows(rows):
                gram[rows, :] = (
                    SCHULZ_FIRST * wide_view(current, rows) + matmul(poly[rows, :], current[...])
                ).astype(jnp.bfloat16)

            in_tiles(size, gram_rows)
            if sweep_index == NS_STEPS - 1:
                for block, here in enumerate(first_and_opposite(rows, half)):
                    poly_rows(here)
                    result[block] = (
                        SCHULZ_FIRST * wide_view(current, here)
                        + matmul(poly[here, :], current[...])
                    ).astype(jnp.bfloat16)
            else:
                in_tiles(size, poly_rows)
                in_tiles(size, next_rows)
                current[...] = gram[...]

    vmem = pl.BlockSpec(memory_space=pltpu.VMEM)
    return pl.pallas_call(
        kernel,
        out_shape=low(2, rows, size),
        in_specs=[vmem] * 2 + [pl.BlockSpec(memory_space=pl.ANY)] * len(waited),
        out_specs=vmem,
        scratch_shapes=[pltpu.VMEM((size, size), jnp.bfloat16)] * 3
        + [pltpu.VMEM((1, size), jnp.float32)],
        compiler_params=pltpu.CompilerParams(vmem_limit_bytes=56 * 2**20),
        cost_estimate=SMALL,
    )(mine, sibling, *waited)


def gram_parts(place, mine, sibling, reps, *waited):
    size = mine.shape[1]
    half = mine.shape[0]
    part = size // (2 * reps)

    def kernel(place_ref, mine_ref, sibling_ref, *refs):
        to_x, to_y, kept, later, both, gram = refs[len(waited) :]
        both[:half], both[half:] = mine_ref[...], sibling_ref[...]
        is_lower = place_ref[3] == 1

        def row_products(rows):
            gram[rows, :] = matmul_right_t(both[rows, :], both[...]).astype(jnp.bfloat16)

        def column_products(columns):
            gram[columns, :] = matmul_left_t(both[:, columns], both[...]).astype(jnp.bfloat16)

        @pl.when(is_lower)
        def _():
            in_tiles(size, row_products)

        @pl.when(jnp.logical_not(is_lower))
        def _():
            in_tiles(size, column_products)

        def piece(step, index):
            first_row = (place_ref[0] ^ step) * (2 * part) + index * part
            return gram[pl.ds(pl.multiple_of(first_row, part), part), :]

        to_x[0, 0], to_x[0, 1] = piece(1, 0), piece(3, 0)
        to_y[0, 0], to_y[0, 1] = piece(2, 1), piece(3, 1)
        kept[0, 0], kept[0, 1] = piece(0, 0), piece(0, 1)
        later[0, 0], later[0, 1] = piece(2, 0), piece(1, 1)

    vmem = pl.BlockSpec(memory_space=pltpu.VMEM)
    return pl.pallas_call(
        kernel,
        out_shape=tuple([low(1, 2, part, size)] * 4),
        in_specs=[pl.BlockSpec(memory_space=pltpu.SMEM)]
        + [vmem] * 2
        + [pl.BlockSpec(memory_space=pl.ANY)] * len(waited),
        out_specs=tuple([vmem] * 4),
        scratch_shapes=[pltpu.VMEM((size, size), jnp.bfloat16)] * 2,
        compiler_params=pltpu.CompilerParams(vmem_limit_bytes=56 * 2**20),
        cost_estimate=SMALL,
    )(place, mine, sibling, *waited)


def gram_schulz(place, quarters, mine, sibling, rows, *waited):
    size = mine.shape[1]
    half_rows = mine.shape[0]
    part = quarters[0].shape[0]

    def kernel(place_ref, q_ref, x_ref, y_ref, a_ref, b_ref, mine_ref, sibling_ref, *refs):
        result, gram, product, current, poly, half, unit = refs[len(waited) :]
        my_rep = place_ref[0]

        def put(step, offset, ref):
            first_row = (my_rep ^ step) * part + offset
            size_here = ref.shape[0]
            gram[pl.ds(pl.multiple_of(first_row, size_here), size_here), :] = ref[...]

        put(0, 0, q_ref)
        put(1, 0, x_ref)
        put(2, 0, y_ref)
        put(3, 0, a_ref)
        put(3, part // 2, b_ref)

        def trace_of(index, total):
            rows = pl.ds(pl.multiple_of(index * TILE, TILE), TILE)
            here = wide_view(gram, rows)
            row_number = lax.broadcasted_iota(jnp.int32, here.shape, 0) + index * TILE
            column_number = lax.broadcasted_iota(jnp.int32, here.shape, 1)
            return total + jnp.sum(jnp.where(row_number == column_number, here, 0.0))

        trace = lax.fori_loop(0, size // TILE, trace_of, jnp.float32(0.0))
        scale = (1.0 / (jnp.sqrt(jnp.full((8, 128), trace)) + 1e-07))[0:1, 0:1]
        unit[:half_rows] = (mine_ref[...].astype(jnp.float32) * scale).astype(jnp.bfloat16)
        unit[half_rows:] = (sibling_ref[...].astype(jnp.float32) * scale).astype(jnp.bfloat16)

        def scaled(rows):
            current[rows, :] = (wide_view(gram, rows) * (scale * scale)).astype(jnp.bfloat16)

        in_tiles(size, scaled)
        factor = 1.0
        for sweep_index in range(NS_STEPS):

            def poly_rows(rows):
                poly[rows, :] = (
                    SCHULZ_SECOND * wide_view(current, rows)
                    + SCHULZ_THIRD * matmul(current[rows, :], current[...])
                ).astype(jnp.bfloat16)

            def product_rows(rows):
                half[rows, :] = (
                    SCHULZ_FIRST * wide_view(product, rows)
                    + factor * wide_view(poly, rows)
                    + matmul(poly[rows, :], product[...])
                ).astype(jnp.bfloat16)

            def half_rows_of(rows):
                half[rows, :] = (
                    SCHULZ_FIRST * wide_view(current, rows) + matmul(poly[rows, :], current[...])
                ).astype(jnp.bfloat16)

            def current_rows(rows):
                current[rows, :] = (
                    SCHULZ_FIRST * wide_view(half, rows) + matmul(half[rows, :], poly[...])
                ).astype(jnp.bfloat16)

            in_tiles(size, poly_rows)
            if sweep_index == 0:
                product[...] = poly[...]
            else:
                in_tiles(size, product_rows)
                product[...] = half[...]
            factor = factor * SCHULZ_FIRST
            if sweep_index < NS_STEPS - 1:
                in_tiles(size, half_rows_of)
                in_tiles(size, current_rows)

        is_lower = place_ref[3] == 1
        for block, here in enumerate(first_and_opposite(rows, half_rows)):
            plain = factor * wide_view(unit, here)

            @pl.when(is_lower)
            def _():
                turned = matmul(product[here, :], unit[...])
                result[block] = (plain + turned).astype(jnp.bfloat16)

            @pl.when(jnp.logical_not(is_lower))
            def _():
                turned = matmul(unit[here, :], product[...])
                result[block] = (plain + turned).astype(jnp.bfloat16)

    vmem = pl.BlockSpec(memory_space=pltpu.VMEM)
    return pl.pallas_call(
        kernel,
        out_shape=low(2, rows, size),
        in_specs=[pl.BlockSpec(memory_space=pltpu.SMEM)]
        + [vmem] * 7
        + [pl.BlockSpec(memory_space=pl.ANY)] * len(waited),
        out_specs=vmem,
        scratch_shapes=[pltpu.VMEM((size, size), jnp.bfloat16)] * 6,
        compiler_params=pltpu.CompilerParams(vmem_limit_bytes=56 * 2**20),
        cost_estimate=SMALL,
    )(place, *quarters, mine, sibling, *waited)


def low(*shape):
    return jax.ShapeDtypeStruct(shape, jnp.bfloat16)


def fresh_blocks(place, own, arrived, moments, *waited):
    kinds, rows, width = own.shape
    chips = len(arrived) + 1

    def kernel(place_ref, own_ref, *refs):
        arrived_refs = refs[: chips - 1]
        moment_ref = refs[chips - 1]
        grad_ref, *out = refs[chips + len(waited) : -1]
        fresh_ref = refs[-1]
        for kind in range(kinds):
            grad_ref[kind] = add_low(own_ref[kind], *[ref[kind] for ref in arrived_refs])
            fresh_ref[kind] = (
                MOMENTUM_DECAY * moment_ref[kind] + grad_ref[kind].astype(jnp.float32)
            ).astype(jnp.bfloat16)
        for turn in range(chips):
            chip = lax.rem(place_ref[1] + chips - turn, chips)
            out[turn][...] = fresh_ref[jnp.where(chip < chips // 2, 0, 1)]

    vmem = pl.BlockSpec(memory_space=pltpu.VMEM)
    return pl.pallas_call(
        kernel,
        out_shape=tuple([low(kinds, rows, width)] + [low(rows, width)] * chips),
        in_specs=[pl.BlockSpec(memory_space=pltpu.SMEM)]
        + [vmem] * (chips + 1)
        + [pl.BlockSpec(memory_space=pl.ANY)] * len(waited),
        out_specs=tuple([vmem] * (chips + 1)),
        scratch_shapes=[pltpu.VMEM((kinds, rows, width), jnp.bfloat16)],
        compiler_params=pltpu.CompilerParams(vmem_limit_bytes=56 * 2**20),
        cost_estimate=SMALL,
    )(place, own, *arrived, moments, *waited)


def first_seen(arrays):
    kept, index = [], []
    for array in arrays:
        found = [place for place, other in enumerate(kept) if other is array]
        if not found:
            kept.append(array)
        index.append(found[0] if found else len(kept) - 1)
    return kept, index


def weight_rows(place, kinds, received=None, waited=()):
    count = len(kinds)
    steps = len(kinds[0][0])
    rows, width = kinds[0][0][0].shape[1] // 2, kinds[0][1][0].shape[1]
    half = rows // 2
    is_own = received is not None
    aligned = all(kind[2] % 128 == 0 for kind in kinds)
    lefts, left_index = first_seen([left for kind in kinds for left in kind[0]])
    rights, right_index = first_seen([right for kind in kinds for right in kind[1]])
    core_rows = [
        kinds[left_index.index(index) // steps][2] for index in range(len(lefts))
    ]
    if not aligned:
        def chosen(left, size):
            cut = left.reshape(left.shape[0], -1, 2, size)
            first_core = (place[2] == 0) if is_own else (place[2] == 1)
            return jnp.where(first_core, cut[:, :, 0], cut[:, :, 1]).reshape(left.shape[0], rows)

        lefts = [chosen(left, size) for left, size in zip(lefts, core_rows)]
    arrays = lefts + rights + (list(received) if is_own else [])

    def kernel(place_ref, *refs):
        left_refs = refs[: len(lefts)]
        right_refs = refs[len(lefts) : len(lefts) + len(rights)]
        received_refs = refs[len(lefts) + len(rights) : len(arrays)]
        rest = refs[len(arrays) + len(waited) :]
        core = place_ref[2] if is_own else 1 - place_ref[2]

        def columns(index):
            ref, size = left_refs[index], core_rows[index]
            if not aligned:
                return ref[...]
            parts = [
                ref[:, pl.ds(pl.multiple_of((2 * chip + core) * size, 128), size)]
                for chip in range(rows // size)
            ]
            return jnp.concatenate(parts, axis=1)

        for kind in range(count):
            for block in range(steps):
                spot = kind * steps + block
                total = matmul_left_t(
                    columns(left_index[spot]), right_refs[right_index[spot]][...]
                )
                step = (place_ref[0] ^ block) if kinds[kind][3] else block
                if is_own:
                    total = total + received_refs[kind][step].astype(jnp.float32)
                    rest[4][kind, step] = total.astype(jnp.bfloat16)
                else:
                    rest[kind][step] = total.astype(jnp.bfloat16)
            if is_own:
                to_x, to_y, kept, later, sums = rest
                to_x[kind, 0], to_x[kind, 1] = sums[kind, 1, :half], sums[kind, 3, :half]
                to_y[kind, 0], to_y[kind, 1] = sums[kind, 2, half:], sums[kind, 3, half:]
                kept[kind, 0], kept[kind, 1] = sums[kind, 0, :half], sums[kind, 0, half:]
                later[kind, 0], later[kind, 1] = sums[kind, 2, :half], sums[kind, 1, half:]

    if is_own:
        out_shapes = [low(count, 2, half, width)] * 4
    else:
        out_shapes = [low(steps, rows, width)] * count
    vmem = pl.BlockSpec(memory_space=pltpu.VMEM)
    flops = sum(2 * rows * width * left.shape[0] for kind in kinds for left in kind[0])
    return pl.pallas_call(
        kernel,
        out_shape=tuple(out_shapes),
        in_specs=[pl.BlockSpec(memory_space=pltpu.SMEM)]
        + [vmem] * len(arrays)
        + [pl.BlockSpec(memory_space=pl.ANY)] * len(waited),
        out_specs=tuple([vmem] * len(out_shapes)),
        scratch_shapes=(
            [pltpu.VMEM((count, steps, rows, width), jnp.bfloat16)] if is_own else []
        ),
        compiler_params=pltpu.CompilerParams(vmem_limit_bytes=56 * 2**20),
        cost_estimate=SMALL,
    )(place, *arrays, *waited)


def later_sums(later, by_x, by_y, waited):
    def kernel(later_ref, x_ref, y_ref, *refs):
        to_y, to_x = refs[-2:]
        for kind in range(later_ref.shape[0]):
            to_y[kind] = add_low(later_ref[kind, 0], x_ref[kind, 1])
            to_x[kind] = add_low(later_ref[kind, 1], y_ref[kind, 1])

    vmem = pl.BlockSpec(memory_space=pltpu.VMEM)
    shape = low(later.shape[0], *later.shape[2:])
    return pl.pallas_call(
        kernel,
        out_shape=(shape, shape),
        in_specs=[vmem] * 3 + [pl.BlockSpec(memory_space=pl.ANY)] * len(waited),
        out_specs=(vmem, vmem),
        compiler_params=pltpu.CompilerParams(vmem_limit_bytes=56 * 2**20),
        cost_estimate=SMALL,
    )(later, by_x, by_y, *waited)


def held_until(value, *waited):
    def kernel(*refs):
        del refs

    anywhere = pl.BlockSpec(memory_space=pl.ANY)
    return pl.pallas_call(
        kernel,
        out_shape=jax.ShapeDtypeStruct(value.shape, value.dtype),
        in_specs=[anywhere] * (1 + len(waited)),
        out_specs=anywhere,
        input_output_aliases={0: 0},
        compiler_params=pltpu.CompilerParams(
            vmem_limit_bytes=56 * 2**20, has_side_effects=True
        ),
        cost_estimate=SMALL,
    )(value, *waited)


def sorted_blocks(place, kept, by_x, by_y, last_x, last_y, chips, waited):
    kinds, _, half, width = kept.shape
    rows = 2 * half // chips

    def kernel(place_ref, kept_ref, x_ref, y_ref, last_x_ref, last_y_ref, *refs):
        out, whole = refs[len(waited) : -1], refs[-1]
        for kind in range(kinds):
            whole[: chips // 2] = add_low(
                kept_ref[kind, 0], x_ref[kind, 0], last_y_ref[kind]
            ).reshape(chips // 2, rows, width)
            whole[chips // 2 :] = add_low(
                kept_ref[kind, 1], y_ref[kind, 0], last_x_ref[kind]
            ).reshape(chips // 2, rows, width)
            for turn in range(chips):
                out[turn][kind] = whole[lax.rem(place_ref[1] + turn, chips)]

    vmem = pl.BlockSpec(memory_space=pltpu.VMEM)
    return pl.pallas_call(
        kernel,
        out_shape=tuple([low(kinds, rows, width)] * chips),
        in_specs=[pl.BlockSpec(memory_space=pltpu.SMEM)]
        + [vmem] * 5
        + [pl.BlockSpec(memory_space=pl.ANY)] * len(waited),
        out_specs=tuple([vmem] * chips),
        scratch_shapes=[pltpu.VMEM((chips, rows, width), jnp.bfloat16)],
        compiler_params=pltpu.CompilerParams(vmem_limit_bytes=56 * 2**20),
        cost_estimate=SMALL,
    )(place, kept, by_x, by_y, last_x, last_y, *waited)


def held_until(value, *waited):
    def kernel(*refs):
        del refs

    anywhere = pl.BlockSpec(memory_space=pl.ANY)
    return pl.pallas_call(
        kernel,
        out_shape=jax.ShapeDtypeStruct(value.shape, value.dtype),
        in_specs=[anywhere] * (1 + len(waited)),
        out_specs=anywhere,
        input_output_aliases={0: 0},
        compiler_params=pltpu.CompilerParams(
            vmem_limit_bytes=56 * 2**20, has_side_effects=True
        ),
        cost_estimate=SMALL,
    )(value, *waited)


def stretch(shape):
    return math.sqrt(max(shape[0], shape[1]) / min(shape[0], shape[1]))


def add_low(*terms):
    total = terms[0].astype(jnp.float32)
    for term in terms[1:]:
        total = total + term.astype(jnp.float32)
    return total.astype(jnp.bfloat16)


def phase_blocks(arrived, by_x, by_y, waited):
    given = [*(arrived or []), *([by_x, by_y] if by_x is not None else [])]
    width = given[0].shape[-1]
    if arrived:
        rows, turns = arrived[0].shape[0], len(arrived)
        total = rows * turns
        half = total // 2
    else:
        total, half = 0, by_x.shape[0] // 3
    send = total + (half if by_x is not None else 0)
    came = by_x.shape[0] if by_x is not None else 0
    out_shapes = [low(send, width)] * 2 + [low(2 * came + total, width)]

    def kernel(*refs):
        inputs = list(refs[: len(given)])
        to_x, to_y, to_core = refs[len(given) + len(waited) :]
        if arrived:
            for turn in range(turns):
                here = slice(turn * rows, (turn + 1) * rows)
                block = inputs.pop(0)[...]
                to_x[here] = to_y[here] = block
                first_row = 2 * came + turn * rows
                to_core[first_row : first_row + rows] = block
        if by_x is not None:
            x_ref, y_ref = inputs.pop(0), inputs.pop(0)
            to_x[total:] = y_ref[:half]
            to_y[total:] = x_ref[half : 2 * half]
            to_core[:came], to_core[came : 2 * came] = x_ref[...], y_ref[...]

    vmem = pl.BlockSpec(memory_space=pltpu.VMEM)
    return pl.pallas_call(
        kernel,
        out_shape=tuple(out_shapes),
        in_specs=[vmem] * len(given) + [pl.BlockSpec(memory_space=pl.ANY)] * len(waited),
        out_specs=tuple([vmem] * len(out_shapes)),
        compiler_params=pltpu.CompilerParams(vmem_limit_bytes=56 * 2**20),
        cost_estimate=SMALL,
    )(*given, *waited)


def block_shares(shares):
    flat = [part[0] if isinstance(part, tuple) else part for share in shares for part in share]
    starts = [part[1] for share in shares for part in share[1:]]
    return flat, starts


def start_blocks(place_ref, flat_refs, starts, out, sem_of, kind, chips, by_rep):
    reps, rows = flat_refs[0].shape[1:3]
    turns = chips - 1
    half = turns * rows // 2
    my_rep, my_chip, my_core = place_ref[0], place_ref[1], place_ref[2]
    cuts = []
    for turn in range(turns):
        low_end, high_end = turn * rows, (turn + 1) * rows
        middle = min(max(half, low_end), high_end)
        if middle > low_end:
            cuts.append((0, low_end, turn, 0, middle - low_end))
        if high_end > middle:
            cuts.append((1, middle - half, turn, middle - low_end, high_end - middle))
    copies = [[] for step in range(reps)]

    def start(step, source, target):
        copy = pltpu.make_async_copy(source, target, sem_of(step, len(copies[step])))
        copy.start()
        copies[step].append(copy)

    for step in range(reps):
        from_rep = my_rep ^ step
        to_rep = from_rep if by_rep else step
        for side in range(2):
            core = my_core if side == 0 else 1 - my_core
            own, *moved = flat_refs[6 * side : 6 * side + 6]
            first_rows = starts[5 * side : 5 * side + 5]
            start(step, own.at[kind, from_rep], out.at[to_rep, my_chip, core])
            if step < reps - 1:
                for turn in range(turns):
                    start(
                        step,
                        moved[step].at[pl.ds(first_rows[step] + turn * rows, rows)],
                        out.at[to_rep, lax.rem(my_chip + 1 + turn, chips), core],
                    )
            else:
                for part, source_row, turn, target_row, count in cuts:
                    start(
                        step,
                        moved[3 + part].at[pl.ds(first_rows[3 + part] + source_row, count)],
                        out.at[
                            to_rep,
                            lax.rem(my_chip + 1 + turn, chips),
                            core,
                            pl.ds(target_row, count),
                        ],
                    )
    return copies


def placed_blocks(place, shares, kind, chips, waited):
    reps, rows, width = shares[0][0].shape[1:]
    flat, starts = block_shares(shares)

    def kernel(place_ref, *refs):
        results = refs[len(flat) + len(waited) : -3]
        out, sems, out_sems = refs[-3:]
        copies = start_blocks(
            place_ref,
            refs[: len(flat)],
            starts,
            out,
            lambda step, index: sems.at[step, index],
            kind,
            chips,
            True,
        )
        for step in range(reps):
            for copy in copies[step]:
                copy.wait()
        writes = [
            pltpu.make_async_copy(out.at[step], results[step], out_sems.at[step])
            for step in range(reps)
        ]
        for write in writes:
            write.start()
        for write in writes:
            write.wait()

    shape = (reps, chips, 2, rows, width)
    anywhere = pl.BlockSpec(memory_space=pl.ANY)
    full = pl.pallas_call(
        kernel,
        out_shape=tuple([low(*shape[1:])] * reps),
        in_specs=[pl.BlockSpec(memory_space=pltpu.SMEM)] + [anywhere] * (len(flat) + len(waited)),
        out_specs=tuple([anywhere] * reps),
        scratch_shapes=[
            pltpu.VMEM(shape, jnp.bfloat16),
            pltpu.SemaphoreType.DMA((reps, 2 * chips + 2)),
            pltpu.SemaphoreType.DMA((reps,)),
        ],
        compiler_params=pltpu.CompilerParams(vmem_limit_bytes=56 * 2**20),
        cost_estimate=SMALL,
    )(place, *flat, *waited)
    return [matrix.reshape(-1, width) for matrix in full]


GELU_SCALE = math.sqrt(2.0 / math.pi)
GELU_CUBE = 0.044715


def feed_forward(place, in_shares, out_shares, chips, third_low, residual, grad_branch):
    reps, rows, width = in_shares[0][0].shape[1:]
    in_flat, in_starts = block_shares(in_shares)
    out_flat, out_starts = block_shares(out_shares)
    tokens = third_low.shape[0]

    def kernel(place_ref, third_ref, residual_ref, branch_ref, *refs):
        in_refs = refs[: len(in_flat)]
        out_refs = refs[len(in_flat) : len(in_flat) + len(out_flat)]
        block_out, grad_third, *parts = refs[len(in_flat) + len(out_flat) : -3]
        hidden, grad_pre = parts[:reps], parts[reps:]
        in_full, out_full, sems = refs[-3:]
        in_copies = start_blocks(
            place_ref, in_refs, in_starts, in_full,
            lambda step, index: sems.at[0, step, index], 2, chips, False,
        )
        out_copies = start_blocks(
            place_ref, out_refs, out_starts, out_full,
            lambda step, index: sems.at[1, step, index], 3, chips, False,
        )
        for step in range(reps):
            for copy in in_copies[step]:
                copy.wait()
            in_weights = in_full[step].reshape(-1, width)
            pre = matmul(third_ref[...], in_weights)
            for copy in out_copies[step]:
                copy.wait()
            out_weights = out_full[step].reshape(-1, width)
            grad_hidden = matmul_right_t(branch_ref[...], out_weights)
            square = pre * pre
            bent = jnp.tanh(GELU_SCALE * pre * (1.0 + GELU_CUBE * square))
            units = (0.5 * pre * (1.0 + bent)).astype(jnp.bfloat16)
            slope = 0.5 * (1.0 + bent) + 0.5 * pre * (1.0 - bent * bent) * GELU_SCALE * (
                1.0 + 3.0 * GELU_CUBE * square
            )
            grads = (grad_hidden * slope).astype(jnp.bfloat16)
            hidden[step][...] = units
            grad_pre[step][...] = grads
            to_third = matmul_right_t(grads, in_weights)
            to_out = matmul(units, out_weights)
            if step == 0:
                grad_third[...] = to_third
                block_out[...] = residual_ref[...] + to_out
            else:
                grad_third[...] += to_third
                block_out[...] += to_out

    vmem = pl.BlockSpec(memory_space=pltpu.VMEM)
    whole = jax.ShapeDtypeStruct((tokens, width), jnp.float32)
    shape = (reps, chips, 2, rows, width)
    results = pl.pallas_call(
        kernel,
        out_shape=(whole, whole, *[low(tokens, width)] * (2 * reps)),
        in_specs=[pl.BlockSpec(memory_space=pltpu.SMEM)]
        + [vmem] * 3
        + [pl.BlockSpec(memory_space=pl.ANY)] * (len(in_flat) + len(out_flat)),
        out_specs=(vmem,) * (2 + 2 * reps),
        scratch_shapes=[
            pltpu.VMEM(shape, jnp.bfloat16),
            pltpu.VMEM(shape, jnp.bfloat16),
            pltpu.SemaphoreType.DMA((2, reps, 2 * chips + 2)),
        ],
        compiler_params=pltpu.CompilerParams(vmem_limit_bytes=56 * 2**20),
        cost_estimate=SMALL,
    )(place, third_low, residual, grad_branch, *in_flat, *out_flat)
    block_out, grad_third, *parts = results
    return block_out, grad_third, parts[:reps], parts[reps:]


def prepared(place, matrices, moments, shards, sub, waited):
    reps, rows, width = matrices[0].shape

    def kernel(place_ref, *refs):
        stacks, hidden_in, hidden_out = refs[0:2], refs[2], refs[3]
        old_stacks, old_in, old_out = refs[4:6], refs[6], refs[7]
        whole, *outs = refs[8 + len(waited) :]
        quarters, wide_old, square_old, sems = outs[:3], outs[3], outs[4], outs[5]
        my_rep = place_ref[0]
        copies = []

        def start(source, target):
            copy = pltpu.make_async_copy(source, target, sems.at[len(copies)])
            copy.start()
            copies.append(copy)

        for kind in range(2):
            start(old_stacks[kind].at[my_rep], square_old.at[kind])
        start(old_out.at[pl.ds(pl.multiple_of(my_rep * sub, sub), sub)], wide_old.at[1])
        for shard in range(shards):
            first = pl.multiple_of((shard * reps + my_rep) * sub, sub)
            start(
                old_in.at[:, pl.ds(first, sub)],
                wide_old.at[0, :, pl.ds(shard * sub, sub)],
            )
        for kind in range(2):
            whole[kind] = stacks[kind][...].astype(jnp.bfloat16)
        for step in range(reps):
            for shard in range(shards):
                first = (shard * reps + step) * sub
                whole[2, step, :, shard * sub : (shard + 1) * sub] = hidden_in[
                    :, first : first + sub
                ].astype(jnp.bfloat16)
            whole[3, step] = hidden_out[step * sub : (step + 1) * sub].astype(jnp.bfloat16)
        for kind in range(1, 4):
            quarters[kind - 1][...] = whole[kind, my_rep]
        for copy in copies:
            copy.wait()

    vmem = pl.BlockSpec(memory_space=pltpu.VMEM)
    anywhere = pl.BlockSpec(memory_space=pl.ANY)
    old = jax.ShapeDtypeStruct((2, rows, width), jnp.float32)
    whole, *parts, wide_old, square_old = pl.pallas_call(
        kernel,
        out_shape=(low(4, reps, rows, width), *[low(rows, width)] * 3, old, old),
        in_specs=[pl.BlockSpec(memory_space=pltpu.SMEM)]
        + [vmem] * 4
        + [anywhere] * (4 + len(waited)),
        out_specs=(vmem,) * 6,
        scratch_shapes=[pltpu.SemaphoreType.DMA((shards + 3,))],
        compiler_params=pltpu.CompilerParams(vmem_limit_bytes=56 * 2**20),
        cost_estimate=SMALL,
    )(place, *matrices, *moments, *waited)
    return whole, parts, wide_old, square_old


def branch_back(grad_query, weights, stream, gain, grad_stream, next_weights, *waited):
    rows, width = stream.shape

    def kernel(query_ref, weights_ref, stream_ref, gain_ref, grad_ref, next_ref, *refs):
        total_ref, branch_ref, mixed_ref, gain_grad, bias_grad = refs[len(waited) :]
        grad_out = matmul_right_t(query_ref[...], weights_ref[...])
        values = stream_ref[...]
        centered = values - jnp.mean(values, axis=-1, keepdims=True)
        inverse = lax.rsqrt(jnp.mean(centered * centered, axis=-1, keepdims=True) + NORM_EPSILON)
        unit_part = centered * inverse
        grad_unit = grad_out * gain_ref[...]
        grad_in = inverse * (
            grad_unit
            - jnp.mean(grad_unit, axis=-1, keepdims=True)
            - unit_part * jnp.mean(grad_unit * unit_part, axis=-1, keepdims=True)
        )
        total = grad_ref[...] + grad_in
        branch = total.astype(jnp.bfloat16)
        total_ref[...] = total
        branch_ref[...] = branch
        mixed_ref[...] = matmul_right_t(branch, next_ref[...]).astype(jnp.bfloat16)
        gain_grad[...] = jnp.sum(grad_out * unit_part, axis=0, keepdims=True)
        bias_grad[...] = jnp.sum(grad_out, axis=0, keepdims=True)

    vmem = pl.BlockSpec(memory_space=pltpu.VMEM)
    line = jax.ShapeDtypeStruct((1, width), jnp.float32)
    return pl.pallas_call(
        kernel,
        out_shape=(
            jax.ShapeDtypeStruct((rows, width), jnp.float32),
            low(rows, width),
            low(rows, width),
            line,
            line,
        ),
        in_specs=[vmem] * 6 + [pl.BlockSpec(memory_space=pl.ANY)] * len(waited),
        out_specs=(vmem,) * 5,
        compiler_params=pltpu.CompilerParams(vmem_limit_bytes=56 * 2**20),
        cost_estimate=SMALL,
    )(grad_query, weights, stream, gain, grad_stream, next_weights, *waited)


def on_device(
    tokens,
    states,
    cotangent,
    dec_len,
    enc_len,
    self_weights,
    cross_weights,
    fc_in,
    fc_out,
    norm_params,
    self_moment,
    cross_moment,
    fc_in_moment,
    fc_out_moment,
    norm_moment,
):
    reps = lax.axis_size("rep")
    shards = lax.axis_size("shard")
    chips = shards // 2
    my_rep = lax.axis_index("rep")
    my_place = lax.axis_index("shard")
    my_chip = my_place // 2
    my_core = lax.rem(my_place, 2)
    even = my_core == 0
    width = self_weights.shape[2]
    rows = self_weights.shape[1]
    hidden_width = fc_in.shape[1]
    sub = hidden_width // (shards * reps)

    def swap(values):
        return lax.ppermute(values, "shard", [(index, index ^ 1) for index in range(shards)])

    def from_chip(values, turn):
        pairs = [
            (2 * ((chip + turn) % chips) + core, 2 * chip + core)
            for chip in range(chips)
            for core in range(2)
        ]
        return lax.ppermute(values, "shard", pairs)

    def from_rep(values, step):
        return lax.ppermute(values, "rep", [(index ^ step, index) for index in range(reps)])

    low_bit = (my_rep & 1) == 1
    high_bit = (my_rep & 2) == 2

    def by_rep(steps):
        turned = [jnp.where(low_bit, steps[step ^ 1], steps[step]) for step in range(reps)]
        return [jnp.where(high_bit, turned[step ^ 2], turned[step]) for step in range(reps)]

    is_lower = my_chip < chips // 2
    place_now = jnp.stack([my_rep, my_chip, my_core, is_lower]).astype(jnp.int32)

    def first_blocks(quarter):
        return [from_chip(quarter, turn) for turn in range(1, chips)]

    total_rows = (chips - 1) * rows

    def run_phase(state, phase, waited):
        to_x, to_y, to_core = phase_blocks(
            state["arrived"] if phase < 4 else None,
            state["by_x"][-1] if phase > 0 else None,
            state["by_y"][-1] if phase > 0 else None,
            [*waited, *state["came"][-1:]],
        )
        if phase < 3:
            quarter = held_until(state["quarters"][phase], to_core)
            state["arrived"] = first_blocks(quarter)
        state["sent"].append(to_x)
        state["by_x"].append(from_rep(to_x, 1))
        state["by_y"].append(from_rep(to_y, 2))
        state["came"].append(swap(to_core))

    def shares_of(state, kind, last_pair=None):
        by_x, by_y, came = state["by_x"], state["by_y"], state["came"]
        size = total_rows if kind == 0 else total_rows + total_rows // 2
        next_size = total_rows // 2 if kind == 3 else total_rows + total_rows // 2
        behind = next_size - total_rows // 2
        before = [0, 2 * total_rows, 3 * total_rows, 3 * total_rows][kind]
        mine = [
            state["shards"],
            (state["sent"][kind], 0),
            (by_x[kind], 0),
            (by_y[kind], 0),
            (by_x[kind + 1], behind),
            (by_y[kind + 1], behind),
        ]
        last = last_pair or (came[kind + 2], came[kind + 2])
        siblings = [
            state["other_shards"],
            (came[kind], before),
            (came[kind + 1], 0),
            (came[kind + 1], size),
            (last[0], behind),
            (last[1], behind if last_pair else next_size + behind),
        ]
        return mine, siblings

    def of_rep(values):
        return lax.dynamic_index_in_dim(values, my_rep, 0, keepdims=False)

    def in_quarters(matrix):
        return matrix.reshape(rows, shards, reps, sub).transpose(2, 0, 1, 3).reshape(
            reps, rows, shards * sub
        )

    def in_shard(pieces):
        cut = jnp.stack(pieces).reshape(reps, rows, shards, sub)
        return cut.transpose(1, 2, 0, 3).reshape(rows, hidden_width)

    def prepare():
        matrices = [self_weights, cross_weights, fc_in, fc_out]
        moments = [self_moment, cross_moment, fc_in_moment, fc_out_moment]
        if sub % 128 == 0:
            return prepared(place_now, matrices, moments, shards, sub, [])
        whole = jnp.stack(
            [
                self_weights.astype(jnp.bfloat16),
                cross_weights.astype(jnp.bfloat16),
                in_quarters(fc_in.astype(jnp.bfloat16)),
                fc_out.reshape(reps, sub, width).astype(jnp.bfloat16),
            ]
        )
        wide_old = [of_rep(in_quarters(fc_in_moment)), of_rep(moments[3].reshape(reps, sub, width))]
        square_old = [of_rep(self_moment), of_rep(cross_moment)]
        quarters = [of_rep(whole[kind]) for kind in range(1, 4)]
        return whole, quarters, jnp.stack(wide_old), jnp.stack(square_old)

    state = {"by_x": [], "by_y": [], "came": [], "sent": []}
    state["arrived"] = first_blocks(of_rep(self_weights).astype(jnp.bfloat16))
    state["shards"], state["quarters"], wide_moments, square_moments = prepare()
    state["other_shards"] = swap(state["shards"])
    run_phase(state, 0, [state["shards"]])
    run_phase(state, 1, [state["other_shards"]])
    run_phase(state, 2, [])
    self_full = placed_blocks(place_now, shares_of(state, 0), 0, chips, [])

    def first_sums(kinds, others, *waited):
        received = [swap(other) for other in others]
        to_x, to_y, kept, later = weight_rows(place_now, kinds, received, waited)
        return kept, later, from_rep(to_x, 1), from_rep(to_y, 2)

    def second_sums(stage, *waited):
        kept, later, by_x, by_y = stage
        to_y, to_x = later_sums(later, by_x, by_y, waited)
        return (kept, by_x, by_y, from_rep(to_x, 1), from_rep(to_y, 2)), to_x

    def third_sums(stage, *waited):
        blocks = sorted_blocks(place_now, *stage, chips, waited)
        arrived = [from_chip(blocks[chips - turn], turn) for turn in range(1, chips)]
        return blocks[0], arrived

    def share_pair(pair, *waited):
        by_x, by_y = from_rep(pair, 1), from_rep(pair, 2)
        across = jnp.stack([from_rep(by_y[0], 1), from_rep(by_x[1], 2)])
        return [pair, by_x, by_y, across]

    def to_replicas(steps):
        return by_rep([step[0] for step in steps]), by_rep([step[1] for step in steps])

    source = tokens[0].astype(jnp.float32)
    encoded = states[0]
    gain_rows = norm_params[0]
    bias_rows = norm_params[1]
    first, first_unit, first_inv = normalize_parts(source, gain_rows[0], bias_rows[0])
    first_low = first.astype(jnp.bfloat16)
    query_rows = matmul(first_low, self_full[0]).astype(jnp.bfloat16)
    incoming_keys = matmul(first_low, self_full[1]).astype(jnp.bfloat16)
    incoming_values = matmul(first_low, self_full[2]).astype(jnp.bfloat16)
    run_phase(state, 3, [query_rows, incoming_keys, incoming_values])
    cross_full = placed_blocks(place_now, shares_of(state, 1), 1, chips, [])
    attended_values = attend_forward(query_rows, incoming_keys, incoming_values, dec_len, True)
    after_self = source + matmul(attended_values, self_full[3])
    second, second_unit, second_inv = normalize_parts(after_self, gain_rows[1], bias_rows[1])
    second_low = second.astype(jnp.bfloat16)
    cross_keys = matmul(encoded, cross_full[1]).astype(jnp.bfloat16)
    cross_values = matmul(encoded, cross_full[2]).astype(jnp.bfloat16)
    run_phase(state, 4, [cross_keys, cross_values, after_self])
    hidden_shares = [
        shares_of(state, 2),
        shares_of(state, 3, (swap(state["by_x"][-1]), swap(state["by_y"][-1]))),
    ]
    cross_query = matmul(second_low, cross_full[0]).astype(jnp.bfloat16)
    cross_mixed = attend_forward(cross_query, cross_keys, cross_values, enc_len, False)
    after_cross = after_self + matmul(cross_mixed, cross_full[3])
    third, third_unit, third_inv = normalize_parts(after_cross, gain_rows[2], bias_rows[2])
    third_low = third.astype(jnp.bfloat16)
    grad_out = cotangent[0].astype(jnp.float32)
    grad_branch = cotangent[0]
    block_out, grad_third, hidden, grad_pre = feed_forward(
        place_now, *hidden_shares, chips, third_low, after_cross, grad_branch
    )
    wide_kinds = [
        ([third_low] * reps, grad_pre, rows, False),
        (hidden, [grad_branch] * reps, sub, False),
    ]
    in_other = weight_rows(place_now, wide_kinds[:1])[0]
    out_other = weight_rows(place_now, wide_kinds[1:], None, [in_other])[0]
    grad_norm, third_gain, third_bias = normalize_back(
        grad_third, third_unit, third_inv, gain_rows[2]
    )
    grad_cross = grad_out + grad_norm
    cross_branch = grad_cross.astype(jnp.bfloat16)
    grad_mixed = matmul_right_t(cross_branch, cross_full[3]).astype(jnp.bfloat16)
    grad_cq, grad_ck, grad_cv = attend_backward(
        cross_query, cross_keys, cross_values, enc_len, False, grad_mixed
    )
    wide_stage = first_sums(wide_kinds, [in_other, out_other], grad_cq)
    cross_kind = (
        [second_low, encoded, encoded, cross_mixed],
        [grad_cq, grad_ck, grad_cv, cross_branch],
        rows,
        True,
    )
    cross_other = weight_rows(place_now, [cross_kind], None, [wide_stage[0]])[0]
    grad_self, self_branch, grad_mixed, second_gain, second_bias = branch_back(
        grad_cq,
        cross_full[0],
        after_self,
        gain_rows[1:2],
        grad_cross,
        self_full[3],
        cross_other,
    )
    second_gain, second_bias = second_gain[0], second_bias[0]
    grad_sq, grad_sk, grad_sv = attend_backward(
        query_rows, incoming_keys, incoming_values, dec_len, True, grad_mixed
    )
    self_kind = (
        [first_low, first_low, first_low, attended_values],
        [grad_sq, grad_sk, grad_sv, self_branch],
        rows,
        True,
    )
    wide_stage, wide_token = second_sums(wide_stage, grad_sq)
    cross_stage = first_sums([cross_kind], [cross_other], wide_token)
    self_other = weight_rows(place_now, [self_kind], None, [cross_stage[0]])[0]
    wide_stage = third_sums(wide_stage, self_other)
    cross_stage, cross_token = second_sums(cross_stage, wide_stage[0])
    self_stage = first_sums([self_kind], [self_other], cross_token, *cross_stage[3:])
    wide_fresh = fresh_blocks(place_now, *wide_stage, wide_moments, self_stage[0])
    wide_grads = wide_fresh[0]
    cross_stage = third_sums(cross_stage, wide_grads)
    self_stage, self_token = second_sums(self_stage, cross_stage[0])

    def owned(grads_fresh, *waited):
        mine, *sent = grads_fresh[1:]
        arrived = [from_chip(sent[turn - 1], turn) for turn in range(1, chips)]
        if waited:
            mine = held_until(mine, *waited)
        mine = jnp.concatenate([mine, *arrived])
        return mine, swap(mine)

    def to_both(result):
        other = from_chip(result[1], chips // 2)
        return jnp.stack(
            [jnp.where(is_lower, result[0], other), jnp.where(is_lower, other, result[0])]
        )

    wide_own = owned(wide_fresh)
    to_x, to_y, kept, later = gram_parts(place_now, *wide_own, reps, self_token)
    self_stage = third_sums(self_stage, kept, *cross_stage[1])
    gram_stage, gram_token = second_sums((kept, later, from_rep(to_x, 1), from_rep(to_y, 2)))
    kept, by_x, by_y, last_x, last_y = gram_stage
    quarter = jnp.concatenate(
        [add_low(kept[0, 0], by_x[0, 0], last_y[0]), add_low(kept[0, 1], by_y[0, 0], last_x[0])]
    )
    quarter_x, quarter_y = from_rep(quarter, 1), from_rep(quarter, 2)
    part = quarter.shape[0] // 2
    quarters = [
        quarter,
        quarter_x,
        quarter_y,
        from_rep(quarter_y[:part], 1),
        from_rep(quarter_x[part:], 2),
    ]
    square_fresh = fresh_blocks(
        place_now,
        jnp.concatenate([self_stage[0], cross_stage[0]]),
        [jnp.concatenate(pair) for pair in zip(self_stage[1], cross_stage[1])],
        square_moments,
        gram_token,
    )
    square_grads = square_fresh[0]
    square_own = owned(square_fresh, *quarters[3:])
    grads = held_until(jnp.concatenate([wide_grads, square_grads]), *quarters[3:])
    grads_x, grads_y = from_rep(grads, 1), from_rep(grads, 2)
    wide_rows = gram_schulz(place_now, quarters, *wide_own, rows, square_grads)
    wide_orth = to_both(wide_rows)
    wide_orth_shared = share_pair(wide_orth)
    square_rows = square_schulz(*square_own, rows, wide_orth)
    grads_across = [from_rep(grads_y[:2], 1), from_rep(grads_x[2:], 2)]
    late_sq = held_until(grad_sq, square_rows)
    late_ck = held_until(grad_ck, square_rows)
    grad_states = matmul_right_t(late_ck, cross_full[1]) + matmul_right_t(grad_cv, cross_full[2])
    grad_first = (
        matmul_right_t(late_sq, self_full[0])
        + matmul_right_t(grad_sk, self_full[1])
        + matmul_right_t(grad_sv, self_full[2])
    )
    grad_norm, first_gain, first_bias = normalize_back(
        grad_first, first_unit, first_inv, gain_rows[0]
    )
    grad_tokens = grad_self + grad_norm
    norm_local = jnp.stack(
        [
            jnp.stack([first_gain, second_gain, third_gain]),
            jnp.stack([first_bias, second_bias, third_bias]),
        ]
    )
    norm_local = held_until(norm_local, square_rows)
    norm_total = norm_local + swap(norm_local)
    norm_total = norm_total + from_rep(norm_total, 1)
    norm_total = norm_total + from_rep(norm_total, 2)
    norm_total = sum([from_chip(norm_total, turn) for turn in range(1, chips)], norm_total)
    width_part = norm_moment.shape[2]
    norm_grad = lax.dynamic_slice_in_dim(norm_total, my_place * width_part, width_part, 2)

    late_grads = held_until(grads, square_rows)
    wide_grads_shared = [late_grads[:2], grads_x[:2], grads_y[:2], grads_across[0]]
    square_grads_shared = [late_grads[2:], grads_x[2:], grads_y[2:], grads_across[1]]
    in_shared, out_shared = to_replicas(wide_grads_shared)
    self_shared, cross_shared = to_replicas(square_grads_shared)

    def stacked(pieces):
        return jnp.stack(pieces).astype(jnp.float32)

    def lengthwise(pieces):
        return jnp.concatenate(pieces).astype(jnp.float32)

    self_grad = stacked(self_shared)
    cross_grad = stacked(cross_shared)
    fc_in_grad = in_shard(in_shared).astype(jnp.float32)
    fc_out_grad = lengthwise(out_shared)
    self_fresh = MOMENTUM_DECAY * self_moment + self_grad
    cross_fresh = MOMENTUM_DECAY * cross_moment + cross_grad
    in_fresh = MOMENTUM_DECAY * fc_in_moment + fc_in_grad
    out_fresh = MOMENTUM_DECAY * fc_out_moment + fc_out_grad

    square_orth = held_until(
        to_both(square_rows),
        wide_orth_shared[1],
        wide_orth_shared[2],
        self_fresh,
        cross_fresh,
        in_fresh,
        out_fresh,
    )
    square_orth_shared = share_pair(square_orth)
    wide_orth_shared[0] = held_until(wide_orth_shared[0], *square_orth_shared[1:3])
    in_orth_shared, out_orth_shared = to_replicas(wide_orth_shared)
    self_orth_shared, cross_orth_shared = to_replicas(square_orth_shared)
    self_orth = stacked(self_orth_shared)
    cross_orth = stacked(cross_orth_shared)
    in_orth = in_shard(in_orth_shared).astype(jnp.float32)
    out_orth = lengthwise(out_orth_shared)
    norm_fresh = MOMENTUM_DECAY * norm_moment + norm_grad
    self_new = self_weights - MATRIX_RATE * stretch((width, width)) * self_orth
    cross_new = cross_weights - MATRIX_RATE * stretch((width, width)) * cross_orth
    in_new = fc_in - MATRIX_RATE * stretch((width, hidden_width)) * in_orth
    out_new = fc_out - MATRIX_RATE * stretch((hidden_width, width)) * out_orth
    own_params = lax.dynamic_slice_in_dim(norm_params, my_place * width_part, width_part, 2)
    total_tokens = reps * shards * tokens.shape[0] * tokens.shape[1]
    norm_new = own_params - VECTOR_RATE * norm_fresh / math.sqrt(total_tokens)
    return (
        block_out[None].astype(jnp.bfloat16),
        grad_tokens[None].astype(jnp.bfloat16),
        grad_states[None].astype(jnp.bfloat16),
        self_grad,
        cross_grad,
        fc_in_grad,
        fc_out_grad,
        norm_grad,
        self_fresh,
        cross_fresh,
        in_fresh,
        out_fresh,
        norm_fresh,
        self_new,
        cross_new,
        in_new,
        out_new,
        norm_new,
        self_new.astype(jnp.bfloat16),
        cross_new.astype(jnp.bfloat16),
        in_new.astype(jnp.bfloat16),
        out_new.astype(jnp.bfloat16),
    )


def solution(mesh):
    placed = (
        P(("rep", "shard"), None, None),
        P(("rep", "shard"), None, None),
        P(("rep", "shard"), None, None),
        P(("rep", "shard")),
        P(("rep", "shard")),
        P(None, "shard", None),
        P(None, "shard", None),
        P("shard", None),
        P("shard", None),
        P(),
        P(None, "shard", None),
        P(None, "shard", None),
        P("shard", None),
        P("shard", None),
        P(None, None, "shard"),
    )
    return jax.shard_map(
        on_device,
        mesh=mesh,
        in_specs=placed,
        out_specs=(
            P(("rep", "shard"), None, None),
            P(("rep", "shard"), None, None),
            P(("rep", "shard"), None, None),
            P(None, "shard", None),
            P(None, "shard", None),
            P("shard", None),
            P("shard", None),
            P(None, None, "shard"),
            P(None, "shard", None),
            P(None, "shard", None),
            P("shard", None),
            P("shard", None),
            P(None, None, "shard"),
            P(None, "shard", None),
            P(None, "shard", None),
            P("shard", None),
            P("shard", None),
            P(None, None, "shard"),
            P(None, "shard", None),
            P(None, "shard", None),
            P("shard", None),
            P("shard", None),
        ),
        check_vma=False,
    )
```

```python
import math

import jax
import jax.numpy as jnp
from jax import lax
from jax.experimental import pallas as pl
from jax.experimental.pallas import tpu as pltpu
from jax.sharding import PartitionSpec as P

HEADS = 16
HEAD_DIM = 64
NS_STEPS = 3


NORM_EPSILON = 1e-05
MOMENTUM_DECAY = 0.9
MATRIX_RATE = 0.6
VECTOR_RATE = 0.05
SCHULZ_FIRST = 3.4445
SCHULZ_SECOND = -4.775
SCHULZ_THIRD = 2.0315


def matmul(left, right):
    return jnp.dot(left, right, preferred_element_type=jnp.float32)


def matmul_left_t(left, right):
    return lax.dot_general(
        left, right, (((0,), (0,)), ((), ())), preferred_element_type=jnp.float32
    )


def matmul_right_t(left, right):
    return lax.dot_general(
        left, right, (((1,), (1,)), ((), ())), preferred_element_type=jnp.float32
    )


def normalize_parts(values, gain, bias):
    centered = values - jnp.mean(values, axis=-1, keepdims=True)
    inverse = lax.rsqrt(jnp.mean(centered * centered, axis=-1, keepdims=True) + NORM_EPSILON)
    unit_part = centered * inverse
    return (unit_part * gain + bias, unit_part, inverse)


def normalize_back(grad_out, unit_part, inverse, gain):
    grad_unit = grad_out * gain
    grad_in = inverse * (
        grad_unit
        - jnp.mean(grad_unit, axis=-1, keepdims=True)
        - unit_part * jnp.mean(grad_unit * unit_part, axis=-1, keepdims=True)
    )
    return (grad_in, jnp.sum(grad_out * unit_part, axis=0), jnp.sum(grad_out, axis=0))


PAIR = 2 * HEAD_DIM
SMALL = pl.CostEstimate(flops=1024, bytes_accessed=1024, transcendentals=0)


def attention_parts(count_ref, causal, query_part, keys, is_first):
    lane = lax.broadcasted_iota(jnp.int32, (1, PAIR), 1)
    own = (lane < HEAD_DIM) == is_first
    scores = matmul_right_t(jnp.where(own, query_part, 0), keys) * HEAD_DIM ** (-0.5)
    key_place = lax.broadcasted_iota(jnp.int32, scores.shape, 1)
    valid = key_place < count_ref[0]
    if causal:
        valid = valid & (key_place <= lax.broadcasted_iota(jnp.int32, scores.shape, 0))
    scores = jnp.where(valid, scores, -jnp.inf)
    exponent = jnp.exp(scores - jnp.max(scores, axis=-1, keepdims=True))
    return exponent / jnp.sum(exponent, axis=-1, keepdims=True), own


def head_pairs(width, body):
    def step(index, carry):
        body(pl.ds(pl.multiple_of(index * PAIR, PAIR), PAIR))
        return carry

    lax.fori_loop(0, width // PAIR, step, 0)


def attention_call(kernel, out_shapes, count, arrays, waited):
    rows, width = arrays[0].shape
    keys = arrays[1].shape[0]
    vmem = pl.BlockSpec(memory_space=pltpu.VMEM)
    return pl.pallas_call(
        kernel,
        out_shape=tuple(out_shapes),
        in_specs=[pl.BlockSpec(memory_space=pltpu.SMEM)]
        + [vmem] * len(arrays)
        + [pl.BlockSpec(memory_space=pl.ANY)] * len(waited),
        out_specs=tuple([vmem] * len(out_shapes)),
        compiler_params=pltpu.CompilerParams(vmem_limit_bytes=56 * 2**20),
        cost_estimate=SMALL,
    )(count, *arrays, *waited)


def attend_forward(query_rows, incoming_keys, incoming_values, count, causal, *waited):
    def kernel(count_ref, query_ref, key_ref, value_ref, *refs):
        mixed_ref = refs[-1]

        def one_pair(columns):
            query_part, keys = query_ref[:, columns], key_ref[:, columns]
            values = value_ref[:, columns]
            mixed = None
            for is_first in (True, False):
                weights, own = attention_parts(count_ref, causal, query_part, keys, is_first)
                here = matmul(weights.astype(jnp.bfloat16), values)
                mixed = here if mixed is None else jnp.where(own, here, mixed)
            mixed_ref[:, columns] = mixed.astype(jnp.bfloat16)

        head_pairs(query_ref.shape[1], one_pair)

    return attention_call(
        kernel,
        [low(*query_rows.shape)],
        count,
        [query_rows, incoming_keys, incoming_values],
        waited,
    )[0]


def attend_backward(
    query_rows, incoming_keys, incoming_values, count, causal, grad_mixed, *waited
):
    def kernel(count_ref, query_ref, key_ref, value_ref, grad_ref, *refs):
        grad_query, grad_keys, grad_values = refs[-3:]
        scale = HEAD_DIM ** (-0.5)

        def one_pair(columns):
            query_part, keys = query_ref[:, columns], key_ref[:, columns]
            values, grads = value_ref[:, columns], grad_ref[:, columns]
            found = None
            for is_first in (True, False):
                weights, own = attention_parts(count_ref, causal, query_part, keys, is_first)
                grad_prob = matmul_right_t(jnp.where(own, grads, 0), values)
                shift = jnp.sum(grad_prob * weights, axis=-1, keepdims=True)
                score_grad = (weights * (grad_prob - shift)).astype(jnp.bfloat16)
                here = (
                    matmul(score_grad, keys) * scale,
                    matmul_left_t(score_grad, query_part) * scale,
                    matmul_left_t(weights.astype(jnp.bfloat16), grads),
                )
                if found is None:
                    found = here
                else:
                    found = [jnp.where(own, new, old) for new, old in zip(here, found)]
            for ref, value in zip((grad_query, grad_keys, grad_values), found):
                ref[:, columns] = value.astype(jnp.bfloat16)

        head_pairs(query_ref.shape[1], one_pair)

    return attention_call(
        kernel,
        [low(*query_rows.shape), low(*incoming_keys.shape), low(*incoming_keys.shape)],
        count,
        [query_rows, incoming_keys, incoming_values, grad_mixed],
        waited,
    )


TILE = 256


def in_tiles(size, body):
    def step(index, carry):
        body(pl.ds(pl.multiple_of(index * TILE, TILE), TILE))
        return carry

    lax.fori_loop(0, size // TILE, step, 0)


def wide_view(ref, rows):
    return ref[rows, :].astype(jnp.float32)


def first_and_opposite(rows, total):
    return slice(0, rows), slice(total // 2, total // 2 + rows)


def square_schulz(mine, sibling, rows, *waited):
    size = mine.shape[1]
    half = mine.shape[0]

    def kernel(mine_ref, sibling_ref, *refs):
        result, current, gram, poly, total = refs[len(waited) :]
        current[:half], current[half:] = mine_ref[...], sibling_ref[...]
        total[...] = jnp.zeros_like(total)

        def add_squares(rows):
            part = wide_view(current, rows)
            total[...] += jnp.sum(part * part, axis=0, keepdims=True)

        in_tiles(size, add_squares)
        scale = 1.0 / (jnp.sqrt(jnp.sum(total[...])) + 1e-07)

        def scaled(rows):
            current[rows, :] = (wide_view(current, rows) * scale).astype(jnp.bfloat16)

        in_tiles(size, scaled)
        for sweep_index in range(NS_STEPS):

            def gram_rows(rows):
                gram[rows, :] = matmul_right_t(current[rows, :], current[...]).astype(
                    jnp.bfloat16
                )

            def poly_rows(rows):
                poly[rows, :] = (
                    SCHULZ_SECOND * wide_view(gram, rows)
                    + SCHULZ_THIRD * matmul(gram[rows, :], gram[...])
                ).astype(jnp.bfloat16)

            def next_rows(rows):
                gram[rows, :] = (
                    SCHULZ_FIRST * wide_view(current, rows) + matmul(poly[rows, :], current[...])
                ).astype(jnp.bfloat16)

            in_tiles(size, gram_rows)
            if sweep_index == NS_STEPS - 1:
                for block, here in enumerate(first_and_opposite(rows, half)):
                    poly_rows(here)
                    result[block] = (
                        SCHULZ_FIRST * wide_view(current, here)
                        + matmul(poly[here, :], current[...])
                    ).astype(jnp.bfloat16)
            else:
                in_tiles(size, poly_rows)
                in_tiles(size, next_rows)
                current[...] = gram[...]

    vmem = pl.BlockSpec(memory_space=pltpu.VMEM)
    return pl.pallas_call(
        kernel,
        out_shape=low(2, rows, size),
        in_specs=[vmem] * 2 + [pl.BlockSpec(memory_space=pl.ANY)] * len(waited),
        out_specs=vmem,
        scratch_shapes=[pltpu.VMEM((size, size), jnp.bfloat16)] * 3
        + [pltpu.VMEM((1, size), jnp.float32)],
        compiler_params=pltpu.CompilerParams(vmem_limit_bytes=56 * 2**20),
        cost_estimate=SMALL,
    )(mine, sibling, *waited)


def gram_parts(place, mine, sibling, reps, *waited):
    size = mine.shape[1]
    half = mine.shape[0]
    part = size // (2 * reps)

    def kernel(place_ref, mine_ref, sibling_ref, *refs):
        to_x, to_y, kept, later, both, gram = refs[len(waited) :]
        both[:half], both[half:] = mine_ref[...], sibling_ref[...]
        is_lower = place_ref[3] == 1

        def row_products(rows):
            gram[rows, :] = matmul_right_t(both[rows, :], both[...]).astype(jnp.bfloat16)

        def column_products(columns):
            gram[columns, :] = matmul_left_t(both[:, columns], both[...]).astype(jnp.bfloat16)

        @pl.when(is_lower)
        def _():
            in_tiles(size, row_products)

        @pl.when(jnp.logical_not(is_lower))
        def _():
            in_tiles(size, column_products)

        def piece(step, index):
            first_row = (place_ref[0] ^ step) * (2 * part) + index * part
            return gram[pl.ds(pl.multiple_of(first_row, part), part), :]

        to_x[0, 0], to_x[0, 1] = piece(1, 0), piece(3, 0)
        to_y[0, 0], to_y[0, 1] = piece(2, 1), piece(3, 1)
        kept[0, 0], kept[0, 1] = piece(0, 0), piece(0, 1)
        later[0, 0], later[0, 1] = piece(2, 0), piece(1, 1)

    vmem = pl.BlockSpec(memory_space=pltpu.VMEM)
    return pl.pallas_call(
        kernel,
        out_shape=tuple([low(1, 2, part, size)] * 4),
        in_specs=[pl.BlockSpec(memory_space=pltpu.SMEM)]
        + [vmem] * 2
        + [pl.BlockSpec(memory_space=pl.ANY)] * len(waited),
        out_specs=tuple([vmem] * 4),
        scratch_shapes=[pltpu.VMEM((size, size), jnp.bfloat16)] * 2,
        compiler_params=pltpu.CompilerParams(vmem_limit_bytes=56 * 2**20),
        cost_estimate=SMALL,
    )(place, mine, sibling, *waited)


def gram_schulz(place, quarters, mine, sibling, rows, *waited):
    size = mine.shape[1]
    half_rows = mine.shape[0]
    part = quarters[0].shape[0]

    def kernel(place_ref, q_ref, x_ref, y_ref, a_ref, b_ref, mine_ref, sibling_ref, *refs):
        result, gram, product, current, poly, half, unit = refs[len(waited) :]
        my_rep = place_ref[0]

        def put(step, offset, ref):
            first_row = (my_rep ^ step) * part + offset
            size_here = ref.shape[0]
            gram[pl.ds(pl.multiple_of(first_row, size_here), size_here), :] = ref[...]

        put(0, 0, q_ref)
        put(1, 0, x_ref)
        put(2, 0, y_ref)
        put(3, 0, a_ref)
        put(3, part // 2, b_ref)

        def trace_of(index, total):
            rows = pl.ds(pl.multiple_of(index * TILE, TILE), TILE)
            here = wide_view(gram, rows)
            row_number = lax.broadcasted_iota(jnp.int32, here.shape, 0) + index * TILE
            column_number = lax.broadcasted_iota(jnp.int32, here.shape, 1)
            return total + jnp.sum(jnp.where(row_number == column_number, here, 0.0))

        trace = lax.fori_loop(0, size // TILE, trace_of, jnp.float32(0.0))
        scale = (1.0 / (jnp.sqrt(jnp.full((8, 128), trace)) + 1e-07))[0:1, 0:1]
        unit[:half_rows] = (mine_ref[...].astype(jnp.float32) * scale).astype(jnp.bfloat16)
        unit[half_rows:] = (sibling_ref[...].astype(jnp.float32) * scale).astype(jnp.bfloat16)

        def scaled(rows):
            current[rows, :] = (wide_view(gram, rows) * (scale * scale)).astype(jnp.bfloat16)

        in_tiles(size, scaled)
        factor = 1.0
        for sweep_index in range(NS_STEPS):

            def poly_rows(rows):
                poly[rows, :] = (
                    SCHULZ_SECOND * wide_view(current, rows)
                    + SCHULZ_THIRD * matmul(current[rows, :], current[...])
                ).astype(jnp.bfloat16)

            def product_rows(rows):
                half[rows, :] = (
                    SCHULZ_FIRST * wide_view(product, rows)
                    + factor * wide_view(poly, rows)
                    + matmul(poly[rows, :], product[...])
                ).astype(jnp.bfloat16)

            def half_rows_of(rows):
                half[rows, :] = (
                    SCHULZ_FIRST * wide_view(current, rows) + matmul(poly[rows, :], current[...])
                ).astype(jnp.bfloat16)

            def current_rows(rows):
                current[rows, :] = (
                    SCHULZ_FIRST * wide_view(half, rows) + matmul(half[rows, :], poly[...])
                ).astype(jnp.bfloat16)

            in_tiles(size, poly_rows)
            if sweep_index == 0:
                product[...] = poly[...]
            else:
                in_tiles(size, product_rows)
                product[...] = half[...]
            factor = factor * SCHULZ_FIRST
            if sweep_index < NS_STEPS - 1:
                in_tiles(size, half_rows_of)
                in_tiles(size, current_rows)

        is_lower = place_ref[3] == 1
        for block, here in enumerate(first_and_opposite(rows, half_rows)):
            plain = factor * wide_view(unit, here)

            @pl.when(is_lower)
            def _():
                turned = matmul(product[here, :], unit[...])
                result[block] = (plain + turned).astype(jnp.bfloat16)

            @pl.when(jnp.logical_not(is_lower))
            def _():
                turned = matmul(unit[here, :], product[...])
                result[block] = (plain + turned).astype(jnp.bfloat16)

    vmem = pl.BlockSpec(memory_space=pltpu.VMEM)
    return pl.pallas_call(
        kernel,
        out_shape=low(2, rows, size),
        in_specs=[pl.BlockSpec(memory_space=pltpu.SMEM)]
        + [vmem] * 7
        + [pl.BlockSpec(memory_space=pl.ANY)] * len(waited),
        out_specs=vmem,
        scratch_shapes=[pltpu.VMEM((size, size), jnp.bfloat16)] * 6,
        compiler_params=pltpu.CompilerParams(vmem_limit_bytes=56 * 2**20),
        cost_estimate=SMALL,
    )(place, *quarters, mine, sibling, *waited)


def low(*shape):
    return jax.ShapeDtypeStruct(shape, jnp.bfloat16)


def fresh_blocks(place, own, arrived, moments, *waited):
    kinds, rows, width = own.shape
    chips = len(arrived) + 1

    def kernel(place_ref, own_ref, *refs):
        arrived_refs = refs[: chips - 1]
        moment_ref = refs[chips - 1]
        grad_ref, *out = refs[chips + len(waited) : -1]
        fresh_ref = refs[-1]
        for kind in range(kinds):
            grad_ref[kind] = add_low(own_ref[kind], *[ref[kind] for ref in arrived_refs])
            fresh_ref[kind] = (
                MOMENTUM_DECAY * moment_ref[kind] + grad_ref[kind].astype(jnp.float32)
            ).astype(jnp.bfloat16)
        for turn in range(chips):
            chip = lax.rem(place_ref[1] + chips - turn, chips)
            out[turn][...] = fresh_ref[jnp.where(chip < chips // 2, 0, 1)]

    vmem = pl.BlockSpec(memory_space=pltpu.VMEM)
    return pl.pallas_call(
        kernel,
        out_shape=tuple([low(kinds, rows, width)] + [low(rows, width)] * chips),
        in_specs=[pl.BlockSpec(memory_space=pltpu.SMEM)]
        + [vmem] * (chips + 1)
        + [pl.BlockSpec(memory_space=pl.ANY)] * len(waited),
        out_specs=tuple([vmem] * (chips + 1)),
        scratch_shapes=[pltpu.VMEM((kinds, rows, width), jnp.bfloat16)],
        compiler_params=pltpu.CompilerParams(vmem_limit_bytes=56 * 2**20),
        cost_estimate=SMALL,
    )(place, own, *arrived, moments, *waited)


def first_seen(arrays):
    kept, index = [], []
    for array in arrays:
        found = [place for place, other in enumerate(kept) if other is array]
        if not found:
            kept.append(array)
        index.append(found[0] if found else len(kept) - 1)
    return kept, index


def weight_rows(place, kinds, received=None, waited=()):
    count = len(kinds)
    steps = len(kinds[0][0])
    rows, width = kinds[0][0][0].shape[1] // 2, kinds[0][1][0].shape[1]
    half = rows // 2
    is_own = received is not None
    aligned = all(kind[2] % 128 == 0 for kind in kinds)
    lefts, left_index = first_seen([left for kind in kinds for left in kind[0]])
    rights, right_index = first_seen([right for kind in kinds for right in kind[1]])
    core_rows = [
        kinds[left_index.index(index) // steps][2] for index in range(len(lefts))
    ]
    if not aligned:
        def chosen(left, size):
            cut = left.reshape(left.shape[0], -1, 2, size)
            first_core = (place[2] == 0) if is_own else (place[2] == 1)
            return jnp.where(first_core, cut[:, :, 0], cut[:, :, 1]).reshape(left.shape[0], rows)

        lefts = [chosen(left, size) for left, size in zip(lefts, core_rows)]
    arrays = lefts + rights + (list(received) if is_own else [])

    def kernel(place_ref, *refs):
        left_refs = refs[: len(lefts)]
        right_refs = refs[len(lefts) : len(lefts) + len(rights)]
        received_refs = refs[len(lefts) + len(rights) : len(arrays)]
        rest = refs[len(arrays) + len(waited) :]
        core = place_ref[2] if is_own else 1 - place_ref[2]

        def columns(index):
            ref, size = left_refs[index], core_rows[index]
            if not aligned:
                return ref[...]
            parts = [
                ref[:, pl.ds(pl.multiple_of((2 * chip + core) * size, 128), size)]
                for chip in range(rows // size)
            ]
            return jnp.concatenate(parts, axis=1)

        for kind in range(count):
            for block in range(steps):
                spot = kind * steps + block
                total = matmul_left_t(
                    columns(left_index[spot]), right_refs[right_index[spot]][...]
                )
                step = (place_ref[0] ^ block) if kinds[kind][3] else block
                if is_own:
                    total = total + received_refs[kind][step].astype(jnp.float32)
                    rest[4][kind, step] = total.astype(jnp.bfloat16)
                else:
                    rest[kind][step] = total.astype(jnp.bfloat16)
            if is_own:
                to_x, to_y, kept, later, sums = rest
                to_x[kind, 0], to_x[kind, 1] = sums[kind, 1, :half], sums[kind, 3, :half]
                to_y[kind, 0], to_y[kind, 1] = sums[kind, 2, half:], sums[kind, 3, half:]
                kept[kind, 0], kept[kind, 1] = sums[kind, 0, :half], sums[kind, 0, half:]
                later[kind, 0], later[kind, 1] = sums[kind, 2, :half], sums[kind, 1, half:]

    if is_own:
        out_shapes = [low(count, 2, half, width)] * 4
    else:
        out_shapes = [low(steps, rows, width)] * count
    vmem = pl.BlockSpec(memory_space=pltpu.VMEM)
    flops = sum(2 * rows * width * left.shape[0] for kind in kinds for left in kind[0])
    return pl.pallas_call(
        kernel,
        out_shape=tuple(out_shapes),
        in_specs=[pl.BlockSpec(memory_space=pltpu.SMEM)]
        + [vmem] * len(arrays)
        + [pl.BlockSpec(memory_space=pl.ANY)] * len(waited),
        out_specs=tuple([vmem] * len(out_shapes)),
        scratch_shapes=(
            [pltpu.VMEM((count, steps, rows, width), jnp.bfloat16)] if is_own else []
        ),
        compiler_params=pltpu.CompilerParams(vmem_limit_bytes=56 * 2**20),
        cost_estimate=SMALL,
    )(place, *arrays, *waited)


def later_sums(later, by_x, by_y, waited):
    def kernel(later_ref, x_ref, y_ref, *refs):
        to_y, to_x = refs[-2:]
        for kind in range(later_ref.shape[0]):
            to_y[kind] = add_low(later_ref[kind, 0], x_ref[kind, 1])
            to_x[kind] = add_low(later_ref[kind, 1], y_ref[kind, 1])

    vmem = pl.BlockSpec(memory_space=pltpu.VMEM)
    shape = low(later.shape[0], *later.shape[2:])
    return pl.pallas_call(
        kernel,
        out_shape=(shape, shape),
        in_specs=[vmem] * 3 + [pl.BlockSpec(memory_space=pl.ANY)] * len(waited),
        out_specs=(vmem, vmem),
        compiler_params=pltpu.CompilerParams(vmem_limit_bytes=56 * 2**20),
        cost_estimate=SMALL,
    )(later, by_x, by_y, *waited)


def held_until(value, *waited):
    def kernel(*refs):
        del refs

    anywhere = pl.BlockSpec(memory_space=pl.ANY)
    return pl.pallas_call(
        kernel,
        out_shape=jax.ShapeDtypeStruct(value.shape, value.dtype),
        in_specs=[anywhere] * (1 + len(waited)),
        out_specs=anywhere,
        input_output_aliases={0: 0},
        compiler_params=pltpu.CompilerParams(
            vmem_limit_bytes=56 * 2**20, has_side_effects=True
        ),
        cost_estimate=SMALL,
    )(value, *waited)


def sorted_blocks(place, kept, by_x, by_y, last_x, last_y, chips, waited):
    kinds, _, half, width = kept.shape
    rows = 2 * half // chips

    def kernel(place_ref, kept_ref, x_ref, y_ref, last_x_ref, last_y_ref, *refs):
        out, whole = refs[len(waited) : -1], refs[-1]
        for kind in range(kinds):
            whole[: chips // 2] = add_low(
                kept_ref[kind, 0], x_ref[kind, 0], last_y_ref[kind]
            ).reshape(chips // 2, rows, width)
            whole[chips // 2 :] = add_low(
                kept_ref[kind, 1], y_ref[kind, 0], last_x_ref[kind]
            ).reshape(chips // 2, rows, width)
            for turn in range(chips):
                out[turn][kind] = whole[lax.rem(place_ref[1] + turn, chips)]

    vmem = pl.BlockSpec(memory_space=pltpu.VMEM)
    return pl.pallas_call(
        kernel,
        out_shape=tuple([low(kinds, rows, width)] * chips),
        in_specs=[pl.BlockSpec(memory_space=pltpu.SMEM)]
        + [vmem] * 5
        + [pl.BlockSpec(memory_space=pl.ANY)] * len(waited),
        out_specs=tuple([vmem] * chips),
        scratch_shapes=[pltpu.VMEM((chips, rows, width), jnp.bfloat16)],
        compiler_params=pltpu.CompilerParams(vmem_limit_bytes=56 * 2**20),
        cost_estimate=SMALL,
    )(place, kept, by_x, by_y, last_x, last_y, *waited)


def held_until(value, *waited):
    def kernel(*refs):
        del refs

    anywhere = pl.BlockSpec(memory_space=pl.ANY)
    return pl.pallas_call(
        kernel,
        out_shape=jax.ShapeDtypeStruct(value.shape, value.dtype),
        in_specs=[anywhere] * (1 + len(waited)),
        out_specs=anywhere,
        input_output_aliases={0: 0},
        compiler_params=pltpu.CompilerParams(
            vmem_limit_bytes=56 * 2**20, has_side_effects=True
        ),
        cost_estimate=SMALL,
    )(value, *waited)


def stretch(shape):
    return math.sqrt(max(shape[0], shape[1]) / min(shape[0], shape[1]))


def add_low(*terms):
    total = terms[0].astype(jnp.float32)
    for term in terms[1:]:
        total = total + term.astype(jnp.float32)
    return total.astype(jnp.bfloat16)


def phase_blocks(arrived, by_x, by_y, waited):
    given = [*(arrived or []), *([by_x, by_y] if by_x is not None else [])]
    width = given[0].shape[-1]
    if arrived:
        rows, turns = arrived[0].shape[0], len(arrived)
        total = rows * turns
        half = total // 2
    else:
        total, half = 0, by_x.shape[0] // 3
    send = total + (half if by_x is not None else 0)
    came = by_x.shape[0] if by_x is not None else 0
    out_shapes = [low(send, width)] * 2 + [low(2 * came + total, width)]

    def kernel(*refs):
        inputs = list(refs[: len(given)])
        to_x, to_y, to_core = refs[len(given) + len(waited) :]
        if arrived:
            for turn in range(turns):
                here = slice(turn * rows, (turn + 1) * rows)
                block = inputs.pop(0)[...]
                to_x[here] = to_y[here] = block
                first_row = 2 * came + turn * rows
                to_core[first_row : first_row + rows] = block
        if by_x is not None:
            x_ref, y_ref = inputs.pop(0), inputs.pop(0)
            to_x[total:] = y_ref[:half]
            to_y[total:] = x_ref[half : 2 * half]
            to_core[:came], to_core[came : 2 * came] = x_ref[...], y_ref[...]

    vmem = pl.BlockSpec(memory_space=pltpu.VMEM)
    return pl.pallas_call(
        kernel,
        out_shape=tuple(out_shapes),
        in_specs=[vmem] * len(given) + [pl.BlockSpec(memory_space=pl.ANY)] * len(waited),
        out_specs=tuple([vmem] * len(out_shapes)),
        compiler_params=pltpu.CompilerParams(vmem_limit_bytes=56 * 2**20),
        cost_estimate=SMALL,
    )(*given, *waited)


def block_shares(shares):
    flat = [part[0] if isinstance(part, tuple) else part for share in shares for part in share]
    starts = [part[1] for share in shares for part in share[1:]]
    return flat, starts


def start_blocks(place_ref, flat_refs, starts, out, sem_of, kind, chips, by_rep):
    reps, rows = flat_refs[0].shape[1:3]
    turns = chips - 1
    half = turns * rows // 2
    my_rep, my_chip, my_core = place_ref[0], place_ref[1], place_ref[2]
    cuts = []
    for turn in range(turns):
        low_end, high_end = turn * rows, (turn + 1) * rows
        middle = min(max(half, low_end), high_end)
        if middle > low_end:
            cuts.append((0, low_end, turn, 0, middle - low_end))
        if high_end > middle:
            cuts.append((1, middle - half, turn, middle - low_end, high_end - middle))
    copies = [[] for step in range(reps)]

    def start(step, source, target):
        copy = pltpu.make_async_copy(source, target, sem_of(step, len(copies[step])))
        copy.start()
        copies[step].append(copy)

    for step in range(reps):
        from_rep = my_rep ^ step
        to_rep = from_rep if by_rep else step
        for side in range(2):
            core = my_core if side == 0 else 1 - my_core
            own, *moved = flat_refs[6 * side : 6 * side + 6]
            first_rows = starts[5 * side : 5 * side + 5]
            start(step, own.at[kind, from_rep], out.at[to_rep, my_chip, core])
            if step < reps - 1:
                for turn in range(turns):
                    start(
                        step,
                        moved[step].at[pl.ds(first_rows[step] + turn * rows, rows)],
                        out.at[to_rep, lax.rem(my_chip + 1 + turn, chips), core],
                    )
            else:
                for part, source_row, turn, target_row, count in cuts:
                    start(
                        step,
                        moved[3 + part].at[pl.ds(first_rows[3 + part] + source_row, count)],
                        out.at[
                            to_rep,
                            lax.rem(my_chip + 1 + turn, chips),
                            core,
                            pl.ds(target_row, count),
                        ],
                    )
    return copies


def placed_blocks(place, shares, kind, chips, waited):
    reps, rows, width = shares[0][0].shape[1:]
    flat, starts = block_shares(shares)

    def kernel(place_ref, *refs):
        results = refs[len(flat) + len(waited) : -3]
        out, sems, out_sems = refs[-3:]
        copies = start_blocks(
            place_ref,
            refs[: len(flat)],
            starts,
            out,
            lambda step, index: sems.at[step, index],
            kind,
            chips,
            True,
        )
        for step in range(reps):
            for copy in copies[step]:
                copy.wait()
        writes = [
            pltpu.make_async_copy(out.at[step], results[step], out_sems.at[step])
            for step in range(reps)
        ]
        for write in writes:
            write.start()
        for write in writes:
            write.wait()

    shape = (reps, chips, 2, rows, width)
    anywhere = pl.BlockSpec(memory_space=pl.ANY)
    full = pl.pallas_call(
        kernel,
        out_shape=tuple([low(*shape[1:])] * reps),
        in_specs=[pl.BlockSpec(memory_space=pltpu.SMEM)] + [anywhere] * (len(flat) + len(waited)),
        out_specs=tuple([anywhere] * reps),
        scratch_shapes=[
            pltpu.VMEM(shape, jnp.bfloat16),
            pltpu.SemaphoreType.DMA((reps, 2 * chips + 2)),
            pltpu.SemaphoreType.DMA((reps,)),
        ],
        compiler_params=pltpu.CompilerParams(vmem_limit_bytes=56 * 2**20),
        cost_estimate=SMALL,
    )(place, *flat, *waited)
    return [matrix.reshape(-1, width) for matrix in full]


GELU_SCALE = math.sqrt(2.0 / math.pi)
GELU_CUBE = 0.044715


def feed_forward(place, in_shares, out_shares, chips, third_low, residual, grad_branch):
    reps, rows, width = in_shares[0][0].shape[1:]
    in_flat, in_starts = block_shares(in_shares)
    out_flat, out_starts = block_shares(out_shares)
    tokens = third_low.shape[0]

    def kernel(place_ref, third_ref, residual_ref, branch_ref, *refs):
        in_refs = refs[: len(in_flat)]
        out_refs = refs[len(in_flat) : len(in_flat) + len(out_flat)]
        block_out, grad_third, *parts = refs[len(in_flat) + len(out_flat) : -3]
        hidden, grad_pre = parts[:reps], parts[reps:]
        in_full, out_full, sems = refs[-3:]
        in_copies = start_blocks(
            place_ref, in_refs, in_starts, in_full,
            lambda step, index: sems.at[0, step, index], 2, chips, False,
        )
        out_copies = start_blocks(
            place_ref, out_refs, out_starts, out_full,
            lambda step, index: sems.at[1, step, index], 3, chips, False,
        )
        for step in range(reps):
            for copy in in_copies[step]:
                copy.wait()
            in_weights = in_full[step].reshape(-1, width)
            pre = matmul(third_ref[...], in_weights)
            for copy in out_copies[step]:
                copy.wait()
            out_weights = out_full[step].reshape(-1, width)
            grad_hidden = matmul_right_t(branch_ref[...], out_weights)
            square = pre * pre
            bent = jnp.tanh(GELU_SCALE * pre * (1.0 + GELU_CUBE * square))
            units = (0.5 * pre * (1.0 + bent)).astype(jnp.bfloat16)
            slope = 0.5 * (1.0 + bent) + 0.5 * pre * (1.0 - bent * bent) * GELU_SCALE * (
                1.0 + 3.0 * GELU_CUBE * square
            )
            grads = (grad_hidden * slope).astype(jnp.bfloat16)
            hidden[step][...] = units
            grad_pre[step][...] = grads
            to_third = matmul_right_t(grads, in_weights)
            to_out = matmul(units, out_weights)
            if step == 0:
                grad_third[...] = to_third
                block_out[...] = residual_ref[...] + to_out
            else:
                grad_third[...] += to_third
                block_out[...] += to_out

    vmem = pl.BlockSpec(memory_space=pltpu.VMEM)
    whole = jax.ShapeDtypeStruct((tokens, width), jnp.float32)
    shape = (reps, chips, 2, rows, width)
    results = pl.pallas_call(
        kernel,
        out_shape=(whole, whole, *[low(tokens, width)] * (2 * reps)),
        in_specs=[pl.BlockSpec(memory_space=pltpu.SMEM)]
        + [vmem] * 3
        + [pl.BlockSpec(memory_space=pl.ANY)] * (len(in_flat) + len(out_flat)),
        out_specs=(vmem,) * (2 + 2 * reps),
        scratch_shapes=[
            pltpu.VMEM(shape, jnp.bfloat16),
            pltpu.VMEM(shape, jnp.bfloat16),
            pltpu.SemaphoreType.DMA((2, reps, 2 * chips + 2)),
        ],
        compiler_params=pltpu.CompilerParams(vmem_limit_bytes=56 * 2**20),
        cost_estimate=SMALL,
    )(place, third_low, residual, grad_branch, *in_flat, *out_flat)
    block_out, grad_third, *parts = results
    return block_out, grad_third, parts[:reps], parts[reps:]


def prepared(place, matrices, moments, shards, sub, waited):
    reps, rows, width = matrices[0].shape

    def kernel(place_ref, *refs):
        stacks, hidden_in, hidden_out = refs[0:2], refs[2], refs[3]
        old_stacks, old_in, old_out = refs[4:6], refs[6], refs[7]
        whole, *outs = refs[8 + len(waited) :]
        quarters, wide_old, square_old, sems = outs[:3], outs[3], outs[4], outs[5]
        my_rep = place_ref[0]
        copies = []

        def start(source, target):
            copy = pltpu.make_async_copy(source, target, sems.at[len(copies)])
            copy.start()
            copies.append(copy)

        for kind in range(2):
            start(old_stacks[kind].at[my_rep], square_old.at[kind])
        start(old_out.at[pl.ds(pl.multiple_of(my_rep * sub, sub), sub)], wide_old.at[1])
        for shard in range(shards):
            first = pl.multiple_of((shard * reps + my_rep) * sub, sub)
            start(
                old_in.at[:, pl.ds(first, sub)],
                wide_old.at[0, :, pl.ds(shard * sub, sub)],
            )
        for kind in range(2):
            whole[kind] = stacks[kind][...].astype(jnp.bfloat16)
        for step in range(reps):
            for shard in range(shards):
                first = (shard * reps + step) * sub
                whole[2, step, :, shard * sub : (shard + 1) * sub] = hidden_in[
                    :, first : first + sub
                ].astype(jnp.bfloat16)
            whole[3, step] = hidden_out[step * sub : (step + 1) * sub].astype(jnp.bfloat16)
        for kind in range(1, 4):
            quarters[kind - 1][...] = whole[kind, my_rep]
        for copy in copies:
            copy.wait()

    vmem = pl.BlockSpec(memory_space=pltpu.VMEM)
    anywhere = pl.BlockSpec(memory_space=pl.ANY)
    old = jax.ShapeDtypeStruct((2, rows, width), jnp.float32)
    whole, *parts, wide_old, square_old = pl.pallas_call(
        kernel,
        out_shape=(low(4, reps, rows, width), *[low(rows, width)] * 3, old, old),
        in_specs=[pl.BlockSpec(memory_space=pltpu.SMEM)]
        + [vmem] * 4
        + [anywhere] * (4 + len(waited)),
        out_specs=(vmem,) * 6,
        scratch_shapes=[pltpu.SemaphoreType.DMA((shards + 3,))],
        compiler_params=pltpu.CompilerParams(vmem_limit_bytes=56 * 2**20),
        cost_estimate=SMALL,
    )(place, *matrices, *moments, *waited)
    return whole, parts, wide_old, square_old


def branch_back(grad_query, weights, stream, gain, grad_stream, next_weights, *waited):
    rows, width = stream.shape

    def kernel(query_ref, weights_ref, stream_ref, gain_ref, grad_ref, next_ref, *refs):
        total_ref, branch_ref, mixed_ref, gain_grad, bias_grad = refs[len(waited) :]
        grad_out = matmul_right_t(query_ref[...], weights_ref[...])
        values = stream_ref[...]
        centered = values - jnp.mean(values, axis=-1, keepdims=True)
        inverse = lax.rsqrt(jnp.mean(centered * centered, axis=-1, keepdims=True) + NORM_EPSILON)
        unit_part = centered * inverse
        grad_unit = grad_out * gain_ref[...]
        grad_in = inverse * (
            grad_unit
            - jnp.mean(grad_unit, axis=-1, keepdims=True)
            - unit_part * jnp.mean(grad_unit * unit_part, axis=-1, keepdims=True)
        )
        total = grad_ref[...] + grad_in
        branch = total.astype(jnp.bfloat16)
        total_ref[...] = total
        branch_ref[...] = branch
        mixed_ref[...] = matmul_right_t(branch, next_ref[...]).astype(jnp.bfloat16)
        gain_grad[...] = jnp.sum(grad_out * unit_part, axis=0, keepdims=True)
        bias_grad[...] = jnp.sum(grad_out, axis=0, keepdims=True)

    vmem = pl.BlockSpec(memory_space=pltpu.VMEM)
    line = jax.ShapeDtypeStruct((1, width), jnp.float32)
    return pl.pallas_call(
        kernel,
        out_shape=(
            jax.ShapeDtypeStruct((rows, width), jnp.float32),
            low(rows, width),
            low(rows, width),
            line,
            line,
        ),
        in_specs=[vmem] * 6 + [pl.BlockSpec(memory_space=pl.ANY)] * len(waited),
        out_specs=(vmem,) * 5,
        compiler_params=pltpu.CompilerParams(vmem_limit_bytes=56 * 2**20),
        cost_estimate=SMALL,
    )(grad_query, weights, stream, gain, grad_stream, next_weights, *waited)


def on_device(
    tokens,
    states,
    cotangent,
    dec_len,
    enc_len,
    self_weights,
    cross_weights,
    fc_in,
    fc_out,
    norm_params,
    self_moment,
    cross_moment,
    fc_in_moment,
    fc_out_moment,
    norm_moment,
):
    reps = lax.axis_size("rep")
    shards = lax.axis_size("shard")
    chips = shards // 2
    my_rep = lax.axis_index("rep")
    my_place = lax.axis_index("shard")
    my_chip = my_place // 2
    my_core = lax.rem(my_place, 2)
    even = my_core == 0
    width = self_weights.shape[2]
    rows = self_weights.shape[1]
    hidden_width = fc_in.shape[1]
    sub = hidden_width // (shards * reps)

    def swap(values):
        return lax.ppermute(values, "shard", [(index, index ^ 1) for index in range(shards)])

    def from_chip(values, turn):
        pairs = [
            (2 * ((chip + turn) % chips) + core, 2 * chip + core)
            for chip in range(chips)
            for core in range(2)
        ]
        return lax.ppermute(values, "shard", pairs)

    def from_rep(values, step):
        return lax.ppermute(values, "rep", [(index ^ step, index) for index in range(reps)])

    low_bit = (my_rep & 1) == 1
    high_bit = (my_rep & 2) == 2

    def by_rep(steps):
        turned = [jnp.where(low_bit, steps[step ^ 1], steps[step]) for step in range(reps)]
        return [jnp.where(high_bit, turned[step ^ 2], turned[step]) for step in range(reps)]

    is_lower = my_chip < chips // 2
    place_now = jnp.stack([my_rep, my_chip, my_core, is_lower]).astype(jnp.int32)

    def first_blocks(quarter):
        return [from_chip(quarter, turn) for turn in range(1, chips)]

    total_rows = (chips - 1) * rows

    def run_phase(state, phase, waited):
        to_x, to_y, to_core = phase_blocks(
            state["arrived"] if phase < 4 else None,
            state["by_x"][-1] if phase > 0 else None,
            state["by_y"][-1] if phase > 0 else None,
            [*waited, *state["came"][-1:]],
        )
        if phase < 3:
            quarter = held_until(state["quarters"][phase], to_core)
            state["arrived"] = first_blocks(quarter)
        state["sent"].append(to_x)
        state["by_x"].append(from_rep(to_x, 1))
        state["by_y"].append(from_rep(to_y, 2))
        state["came"].append(swap(to_core))

    def shares_of(state, kind, last_pair=None):
        by_x, by_y, came = state["by_x"], state["by_y"], state["came"]
        size = total_rows if kind == 0 else total_rows + total_rows // 2
        next_size = total_rows // 2 if kind == 3 else total_rows + total_rows // 2
        behind = next_size - total_rows // 2
        before = [0, 2 * total_rows, 3 * total_rows, 3 * total_rows][kind]
        mine = [
            state["shards"],
            (state["sent"][kind], 0),
            (by_x[kind], 0),
            (by_y[kind], 0),
            (by_x[kind + 1], behind),
            (by_y[kind + 1], behind),
        ]
        last = last_pair or (came[kind + 2], came[kind + 2])
        siblings = [
            state["other_shards"],
            (came[kind], before),
            (came[kind + 1], 0),
            (came[kind + 1], size),
            (last[0], behind),
            (last[1], behind if last_pair else next_size + behind),
        ]
        return mine, siblings

    def of_rep(values):
        return lax.dynamic_index_in_dim(values, my_rep, 0, keepdims=False)

    def in_quarters(matrix):
        return matrix.reshape(rows, shards, reps, sub).transpose(2, 0, 1, 3).reshape(
            reps, rows, shards * sub
        )

    def in_shard(pieces):
        cut = jnp.stack(pieces).reshape(reps, rows, shards, sub)
        return cut.transpose(1, 2, 0, 3).reshape(rows, hidden_width)

    def prepare(first):
        matrices = [self_weights, cross_weights, fc_in, fc_out]
        moments = [self_moment, cross_moment, fc_in_moment, fc_out_moment]
        if sub % 128 == 0:
            return prepared(place_now, matrices, moments, shards, sub, first)
        whole = jnp.stack(
            [
                self_weights.astype(jnp.bfloat16),
                cross_weights.astype(jnp.bfloat16),
                in_quarters(fc_in.astype(jnp.bfloat16)),
                fc_out.reshape(reps, sub, width).astype(jnp.bfloat16),
            ]
        )
        wide_old = [of_rep(in_quarters(fc_in_moment)), of_rep(moments[3].reshape(reps, sub, width))]
        square_old = [of_rep(self_moment), of_rep(cross_moment)]
        quarters = [of_rep(whole[kind]) for kind in range(1, 4)]
        return whole, quarters, jnp.stack(wide_old), jnp.stack(square_old)

    state = {"by_x": [], "by_y": [], "came": [], "sent": []}
    state["arrived"] = first_blocks(of_rep(self_weights).astype(jnp.bfloat16))
    state["shards"], state["quarters"], wide_moments, square_moments = prepare(
        state["arrived"]
    )
    state["other_shards"] = swap(state["shards"])
    run_phase(state, 0, [])
    run_phase(state, 1, [state["other_shards"]])
    run_phase(state, 2, [])
    self_full = placed_blocks(place_now, shares_of(state, 0), 0, chips, [])

    def first_sums(kinds, others, *waited):
        received = [swap(other) for other in others]
        to_x, to_y, kept, later = weight_rows(place_now, kinds, received, waited)
        return kept, later, from_rep(to_x, 1), from_rep(to_y, 2)

    def second_sums(stage, *waited):
        kept, later, by_x, by_y = stage
        to_y, to_x = later_sums(later, by_x, by_y, waited)
        return (kept, by_x, by_y, from_rep(to_x, 1), from_rep(to_y, 2)), to_x

    def third_sums(stage, *waited):
        blocks = sorted_blocks(place_now, *stage, chips, waited)
        arrived = [from_chip(blocks[chips - turn], turn) for turn in range(1, chips)]
        return blocks[0], arrived

    def share_pair(pair, *waited):
        by_x, by_y = from_rep(pair, 1), from_rep(pair, 2)
        across = jnp.stack([from_rep(by_y[0], 1), from_rep(by_x[1], 2)])
        return [pair, by_x, by_y, across]

    def to_replicas(steps):
        return by_rep([step[0] for step in steps]), by_rep([step[1] for step in steps])

    source = tokens[0].astype(jnp.float32)
    encoded = states[0]
    gain_rows = norm_params[0]
    bias_rows = norm_params[1]
    first, first_unit, first_inv = normalize_parts(source, gain_rows[0], bias_rows[0])
    first_low = first.astype(jnp.bfloat16)
    query_rows = matmul(first_low, self_full[0]).astype(jnp.bfloat16)
    incoming_keys = matmul(first_low, self_full[1]).astype(jnp.bfloat16)
    incoming_values = matmul(first_low, self_full[2]).astype(jnp.bfloat16)
    run_phase(state, 3, [query_rows, incoming_keys, incoming_values])
    cross_full = placed_blocks(place_now, shares_of(state, 1), 1, chips, [])
    attended_values = attend_forward(query_rows, incoming_keys, incoming_values, dec_len, True)
    after_self = source + matmul(attended_values, self_full[3])
    second, second_unit, second_inv = normalize_parts(after_self, gain_rows[1], bias_rows[1])
    second_low = second.astype(jnp.bfloat16)
    cross_keys = matmul(encoded, cross_full[1]).astype(jnp.bfloat16)
    cross_values = matmul(encoded, cross_full[2]).astype(jnp.bfloat16)
    run_phase(state, 4, [cross_keys, cross_values, after_self])
    hidden_shares = [
        shares_of(state, 2),
        shares_of(state, 3, (swap(state["by_x"][-1]), swap(state["by_y"][-1]))),
    ]
    cross_query = matmul(second_low, cross_full[0]).astype(jnp.bfloat16)
    cross_mixed = attend_forward(cross_query, cross_keys, cross_values, enc_len, False)
    after_cross = after_self + matmul(cross_mixed, cross_full[3])
    third, third_unit, third_inv = normalize_parts(after_cross, gain_rows[2], bias_rows[2])
    third_low = third.astype(jnp.bfloat16)
    grad_out = cotangent[0].astype(jnp.float32)
    grad_branch = cotangent[0]
    block_out, grad_third, hidden, grad_pre = feed_forward(
        place_now, *hidden_shares, chips, third_low, after_cross, grad_branch
    )
    wide_kinds = [
        ([third_low] * reps, grad_pre, rows, False),
        (hidden, [grad_branch] * reps, sub, False),
    ]
    in_other = weight_rows(place_now, wide_kinds[:1])[0]
    out_other = weight_rows(place_now, wide_kinds[1:], None, [in_other])[0]
    grad_norm, third_gain, third_bias = normalize_back(
        grad_third, third_unit, third_inv, gain_rows[2]
    )
    grad_cross = grad_out + grad_norm
    cross_branch = grad_cross.astype(jnp.bfloat16)
    grad_mixed = matmul_right_t(cross_branch, cross_full[3]).astype(jnp.bfloat16)
    grad_cq, grad_ck, grad_cv = attend_backward(
        cross_query, cross_keys, cross_values, enc_len, False, grad_mixed
    )
    wide_stage = first_sums(wide_kinds, [in_other, out_other], grad_cq)
    cross_kind = (
        [second_low, encoded, encoded, cross_mixed],
        [grad_cq, grad_ck, grad_cv, cross_branch],
        rows,
        True,
    )
    cross_other = weight_rows(place_now, [cross_kind], None, [wide_stage[0]])[0]
    grad_self, self_branch, grad_mixed, second_gain, second_bias = branch_back(
        grad_cq,
        cross_full[0],
        after_self,
        gain_rows[1:2],
        grad_cross,
        self_full[3],
        cross_other,
    )
    second_gain, second_bias = second_gain[0], second_bias[0]
    grad_sq, grad_sk, grad_sv = attend_backward(
        query_rows, incoming_keys, incoming_values, dec_len, True, grad_mixed
    )
    self_kind = (
        [first_low, first_low, first_low, attended_values],
        [grad_sq, grad_sk, grad_sv, self_branch],
        rows,
        True,
    )
    wide_stage, wide_token = second_sums(wide_stage, grad_sq)
    cross_stage = first_sums([cross_kind], [cross_other], wide_token)
    self_other = weight_rows(place_now, [self_kind], None, [cross_stage[0]])[0]
    wide_stage = third_sums(wide_stage, self_other)
    cross_stage, cross_token = second_sums(cross_stage, wide_stage[0])
    self_stage = first_sums([self_kind], [self_other], cross_token, *cross_stage[3:])
    wide_fresh = fresh_blocks(place_now, *wide_stage, wide_moments, self_stage[0])
    wide_grads = wide_fresh[0]
    cross_stage = third_sums(cross_stage, wide_grads)
    self_stage, self_token = second_sums(self_stage, cross_stage[0])

    def owned(grads_fresh):
        mine, *sent = grads_fresh[1:]
        arrived = [from_chip(sent[turn - 1], turn) for turn in range(1, chips)]
        mine = jnp.concatenate([mine, *arrived])
        return mine, swap(mine)

    def to_both(result):
        other = from_chip(result[1], chips // 2)
        return jnp.stack(
            [jnp.where(is_lower, result[0], other), jnp.where(is_lower, other, result[0])]
        )

    wide_own = owned(wide_fresh)
    to_x, to_y, kept, later = gram_parts(place_now, *wide_own, reps, self_token)
    self_stage = third_sums(self_stage, kept, *cross_stage[1])
    gram_stage, gram_token = second_sums((kept, later, from_rep(to_x, 1), from_rep(to_y, 2)))
    kept, by_x, by_y, last_x, last_y = gram_stage
    quarter = jnp.concatenate(
        [add_low(kept[0, 0], by_x[0, 0], last_y[0]), add_low(kept[0, 1], by_y[0, 0], last_x[0])]
    )
    quarter_x, quarter_y = from_rep(quarter, 1), from_rep(quarter, 2)
    part = quarter.shape[0] // 2
    quarters = [
        quarter,
        quarter_x,
        quarter_y,
        from_rep(quarter_y[:part], 1),
        from_rep(quarter_x[part:], 2),
    ]
    square_fresh = fresh_blocks(
        place_now,
        jnp.concatenate([self_stage[0], cross_stage[0]]),
        [jnp.concatenate(pair) for pair in zip(self_stage[1], cross_stage[1])],
        square_moments,
        gram_token,
    )
    square_grads = square_fresh[0]
    square_own = owned(square_fresh)
    grads = jnp.concatenate([wide_grads, square_grads])
    grads_x, grads_y = from_rep(grads, 1), from_rep(grads, 2)
    wide_rows = gram_schulz(place_now, quarters, *wide_own, rows, square_grads)
    wide_orth = to_both(wide_rows)
    wide_orth_shared = share_pair(wide_orth)
    square_rows = square_schulz(*square_own, rows, wide_orth, grads_x, grads_y)
    grads_across = [from_rep(grads_y[:2], 1), from_rep(grads_x[2:], 2)]
    late_sq = held_until(grad_sq, square_rows)
    late_ck = held_until(grad_ck, square_rows)
    grad_states = matmul_right_t(late_ck, cross_full[1]) + matmul_right_t(grad_cv, cross_full[2])
    grad_first = (
        matmul_right_t(late_sq, self_full[0])
        + matmul_right_t(grad_sk, self_full[1])
        + matmul_right_t(grad_sv, self_full[2])
    )
    grad_norm, first_gain, first_bias = normalize_back(
        grad_first, first_unit, first_inv, gain_rows[0]
    )
    grad_tokens = grad_self + grad_norm
    norm_local = jnp.stack(
        [
            jnp.stack([first_gain, second_gain, third_gain]),
            jnp.stack([first_bias, second_bias, third_bias]),
        ]
    )
    norm_local = held_until(norm_local, square_rows)
    norm_total = norm_local + swap(norm_local)
    norm_total = norm_total + from_rep(norm_total, 1)
    norm_total = norm_total + from_rep(norm_total, 2)
    norm_total = sum([from_chip(norm_total, turn) for turn in range(1, chips)], norm_total)
    width_part = norm_moment.shape[2]
    norm_grad = lax.dynamic_slice_in_dim(norm_total, my_place * width_part, width_part, 2)

    late_grads = held_until(grads, square_rows)
    wide_grads_shared = [late_grads[:2], grads_x[:2], grads_y[:2], grads_across[0]]
    square_grads_shared = [late_grads[2:], grads_x[2:], grads_y[2:], grads_across[1]]
    in_shared, out_shared = to_replicas(wide_grads_shared)
    self_shared, cross_shared = to_replicas(square_grads_shared)

    def stacked(pieces):
        return jnp.stack(pieces).astype(jnp.float32)

    def lengthwise(pieces):
        return jnp.concatenate(pieces).astype(jnp.float32)

    self_grad = stacked(self_shared)
    cross_grad = stacked(cross_shared)
    fc_in_grad = in_shard(in_shared).astype(jnp.float32)
    fc_out_grad = lengthwise(out_shared)
    self_fresh = MOMENTUM_DECAY * self_moment + self_grad
    cross_fresh = MOMENTUM_DECAY * cross_moment + cross_grad
    in_fresh = MOMENTUM_DECAY * fc_in_moment + fc_in_grad
    out_fresh = MOMENTUM_DECAY * fc_out_moment + fc_out_grad

    square_orth = held_until(
        to_both(square_rows),
        wide_orth_shared[1],
        wide_orth_shared[2],
        self_fresh,
        cross_fresh,
        in_fresh,
        out_fresh,
    )
    square_orth_shared = share_pair(square_orth)
    wide_orth_shared[0] = held_until(wide_orth_shared[0], *square_orth_shared[1:3])
    in_orth_shared, out_orth_shared = to_replicas(wide_orth_shared)
    self_orth_shared, cross_orth_shared = to_replicas(square_orth_shared)
    self_orth = stacked(self_orth_shared)
    cross_orth = stacked(cross_orth_shared)
    in_orth = in_shard(in_orth_shared).astype(jnp.float32)
    out_orth = lengthwise(out_orth_shared)
    norm_fresh = MOMENTUM_DECAY * norm_moment + norm_grad
    self_new = self_weights - MATRIX_RATE * stretch((width, width)) * self_orth
    cross_new = cross_weights - MATRIX_RATE * stretch((width, width)) * cross_orth
    in_new = fc_in - MATRIX_RATE * stretch((width, hidden_width)) * in_orth
    out_new = fc_out - MATRIX_RATE * stretch((hidden_width, width)) * out_orth
    own_params = lax.dynamic_slice_in_dim(norm_params, my_place * width_part, width_part, 2)
    total_tokens = reps * shards * tokens.shape[0] * tokens.shape[1]
    norm_new = own_params - VECTOR_RATE * norm_fresh / math.sqrt(total_tokens)
    return (
        block_out[None].astype(jnp.bfloat16),
        grad_tokens[None].astype(jnp.bfloat16),
        grad_states[None].astype(jnp.bfloat16),
        self_grad,
        cross_grad,
        fc_in_grad,
        fc_out_grad,
        norm_grad,
        self_fresh,
        cross_fresh,
        in_fresh,
        out_fresh,
        norm_fresh,
        self_new,
        cross_new,
        in_new,
        out_new,
        norm_new,
        self_new.astype(jnp.bfloat16),
        cross_new.astype(jnp.bfloat16),
        in_new.astype(jnp.bfloat16),
        out_new.astype(jnp.bfloat16),
    )


def solution(mesh):
    placed = (
        P(("rep", "shard"), None, None),
        P(("rep", "shard"), None, None),
        P(("rep", "shard"), None, None),
        P(("rep", "shard")),
        P(("rep", "shard")),
        P(None, "shard", None),
        P(None, "shard", None),
        P("shard", None),
        P("shard", None),
        P(),
        P(None, "shard", None),
        P(None, "shard", None),
        P("shard", None),
        P("shard", None),
        P(None, None, "shard"),
    )
    return jax.shard_map(
        on_device,
        mesh=mesh,
        in_specs=placed,
        out_specs=(
            P(("rep", "shard"), None, None),
            P(("rep", "shard"), None, None),
            P(("rep", "shard"), None, None),
            P(None, "shard", None),
            P(None, "shard", None),
            P("shard", None),
            P("shard", None),
            P(None, None, "shard"),
            P(None, "shard", None),
            P(None, "shard", None),
            P("shard", None),
            P("shard", None),
            P(None, None, "shard"),
            P(None, "shard", None),
            P(None, "shard", None),
            P("shard", None),
            P("shard", None),
            P(None, None, "shard"),
            P(None, "shard", None),
            P(None, "shard", None),
            P("shard", None),
            P("shard", None),
        ),
        check_vma=False,
    )
```
